32 devices in a mesh: seq: 8 (over y, x, core), batch: 4 (over z).
Axes of the slice: x: 2, y: 2, z: 4, core: 2. Of those that a mesh axis runs over, the one named last changes fastest.
Arguments:
- inputs: bfloat16 [4, 3072, 512], P('batch', 'seq'), may hold values from -6 to 6
- memory: bfloat16 [4, 1536, 512], P('batch', 'seq'), may hold values from -6 to 6
- target_lengths: int32 [4, 33], P('batch'), may hold values from 32 to 1024, as said below
- source_lengths: int32 [4, 33], P('batch'), may hold values from 16 to 512, as said below
- target_order: int32 [4, 16], P('batch'), may hold values from 0 to 15, as said below
- source_order: int32 [4, 16], P('batch'), may hold values from 0 to 15, as said below
- self_gain: bfloat16 [512], replicated, may hold values from 0.099609375 to 1.8984375
- self_shift: bfloat16 [512], replicated, may hold values from -1.75 to 1.75
- self_query: bfloat16 [512, 512], replicated, may hold values from -0.25 to 0.25
- query_bias: bfloat16 [512], replicated, may hold values from -1.75 to 1.75
- self_key: bfloat16 [512, 512], replicated, may hold values from -0.25 to 0.25
- self_value: bfloat16 [512, 512], replicated, may hold values from -0.25 to 0.25
- value_bias: bfloat16 [512], replicated, may hold values from -1.75 to 1.75
- self_output: bfloat16 [512, 512], replicated, may hold values from -1 to 1
- output_bias: bfloat16 [512], replicated, may hold values from -1.75 to 1.75
- cross_gain: bfloat16 [512], replicated, may hold values from 0.099609375 to 1.8984375
- cross_shift: bfloat16 [512], replicated, may hold values from -1.75 to 1.75
- cross_query: bfloat16 [512, 512], replicated, may hold values from -0.25 to 0.25
- cquery_bias: bfloat16 [512], replicated, may hold values from -1.75 to 1.75
- cross_key: bfloat16 [512, 512], replicated, may hold values from -0.25 to 0.25
- cross_value: bfloat16 [512, 512], replicated, may hold values from -0.25 to 0.25
- cvalue_bias: bfloat16 [512], replicated, may hold values from -1.75 to 1.75
- cross_output: bfloat16 [512, 512], replicated, may hold values from -1 to 1
- coutput_bias: bfloat16 [512], replicated, may hold values from -1.75 to 1.75
- final_gain: bfloat16 [512], replicated, may hold values from 0.099609375 to 1.8984375
- final_shift: bfloat16 [512], replicated, may hold values from -1.75 to 1.75
- inner_weight: bfloat16 [512, 2048], replicated, may hold values from -0.25 to 0.25
- inner_bias: bfloat16 [2048], replicated, may hold values from -1.75 to 1.75
- outer_weight: bfloat16 [2048, 512], replicated, may hold values from -0.125 to 0.125
- outer_bias: bfloat16 [512], replicated, may hold values from -1.75 to 1.75
- cotangent: bfloat16 [4, 3072, 512], P('batch', 'seq'), may hold values from -6 to 6
Outputs:
- block_output: bfloat16 [4, 3072, 512], P('batch', 'seq')
- inputs_grad: float32 [4, 3072, 512], P('batch', 'seq')
- memory_grad: float32 [4, 1536, 512], P('batch', 'seq')
- self_gain_grad: float32 [512], replicated
- self_shift_grad: float32 [512], replicated
- self_query_grad: float32 [512, 512], replicated
- query_bias_grad: float32 [512], replicated
- self_key_grad: float32 [512, 512], replicated
- self_value_grad: float32 [512, 512], replicated
- value_bias_grad: float32 [512], replicated
- self_output_grad: float32 [512, 512], replicated
- output_bias_grad: float32 [512], replicated
- cross_gain_grad: float32 [512], replicated
- cross_shift_grad: float32 [512], replicated
- cross_query_grad: float32 [512, 512], replicated
- cquery_bias_grad: float32 [512], replicated
- cross_key_grad: float32 [512, 512], replicated
- cross_value_grad: float32 [512, 512], replicated
- cvalue_bias_grad: float32 [512], replicated
- cross_output_grad: float32 [512, 512], replicated
- coutput_bias_grad: float32 [512], replicated
- final_gain_grad: float32 [512], replicated
- final_shift_grad: float32 [512], replicated
- inner_weight_grad: float32 [512, 2048], replicated
- inner_bias_grad: float32 [2048], replicated
- outer_weight_grad: float32 [2048, 512], replicated
- outer_bias_grad: float32 [512], replicated
The draws below stay inside these ranges and needn't reach their ends.
Inputs may be any that keep to these rules, and one draw needn't show every extreme that they name: `target_lengths`: in each stream exactly one document, at an index drawn from the seed, has 1024 target tokens; the others have 64//2 to 64; the lengths sum to at most 3072, and stream positions past the sum are padding. `source_lengths`: document d's source pairs with target document d; the document that has 1024 target tokens has exactly 512 source tokens, the others 32//2 to 31; the lengths sum to less than 1536, so the last source position is always padding. Each row is a permutation of 0 to 15: stored block s holds stream block target_order[s]. Each row is a permutation of 0 to 15: stored block s holds source stream block source_order[s].
All inputs are finite; a program needn't handle non-finite values.
Results may differ from the reference program's by a relative error of at most 0.025.
Values may be sent and summed in bfloat16 or wider, within the bound.
A program may use at most 448 MiB of HBM per device.

```python
import math
import jax
import jax.numpy as jnp
import numpy as np
from jax import lax

D = 512
HEADS = 8
FF = 2048
HDIM = 64
TOK_DEV = 384
SHORT = 64
GROUPS = 4
TGT = 3072
SRC_DEV = 192
SRC = 1536
LONG = 1024
SLONG = 512
SSHORT = 32
NDOC = 33
BLOCKS = 16


def slot_table(count):
    half = count // 2
    chosen = [0, half, count - 2]
    remaining = [slot for slot in range(count) if slot not in chosen]
    return np.array(chosen + remaining, dtype=np.int32)


def arrange(key, first, count):
    scores = jax.random.permutation(key, count).astype(jnp.int32)
    index = jnp.arange(count, dtype=jnp.int32)
    scores = jnp.where(index == first, -3, jnp.where(index == first + 1, -2, jnp.where(index == first + 2, -1, scores)))
    ranked = jnp.argsort(scores, stable=True).astype(jnp.int32)
    return jnp.zeros((count,), jnp.int32).at[jnp.asarray(slot_table(count))].set(ranked)


def stream_layout(key):
    pick_key, target_key, source_key, target_place, source_place = jax.random.split(key, 5)
    longest = jax.random.randint(pick_key, (), 0, NDOC)
    index = jnp.arange(NDOC, dtype=jnp.int32)
    target = jnp.where(index == longest, LONG, jax.random.randint(target_key, (NDOC,), SHORT // 2, SHORT + 1)).astype(jnp.int32)
    source = jnp.where(index == longest, SLONG, jax.random.randint(source_key, (NDOC,), SSHORT // 2, SSHORT)).astype(jnp.int32)
    target_start = jnp.sum(jnp.where(index < longest, target, 0))
    source_start = jnp.sum(jnp.where(index < longest, source, 0))
    target_blocks = arrange(target_place, target_start // (TOK_DEV // 2), BLOCKS)
    source_blocks = arrange(source_place, source_start // (SRC_DEV // 2), BLOCKS)
    return (target, source, target_blocks, source_blocks)


def layouts(key):
    return jax.vmap(stream_layout)(jax.random.split(key, GROUPS))


def draw_target_lengths(key, part):
    return layouts(key)[0]


def draw_source_lengths(key, part):
    return layouts(key)[1]


def draw_target_order(key, part):
    return layouts(key)[2]


def draw_source_order(key, part):
    return layouts(key)[3]


def levels(stream_key, dims, cuts, low, largest):
    def one(dim, parts):
        draws = jax.random.uniform(jax.random.fold_in(jax.random.fold_in(stream_key, 6), dim), (parts,), jnp.float32, low / len(cuts), largest / len(cuts))
        return jnp.repeat(jnp.exp(draws), dims[dim] // parts).reshape((-1,) + (1,) * (len(dims) - dim - 1))

    level = one(*cuts[0])
    for cut in cuts[1:]:
        level = level * one(*cut)
    return level


def scatter_about(own_key, extent, scale, bound, cuts=(), held_as=jnp.bfloat16):
    values = scale * jax.random.normal(own_key, extent, jnp.float32)
    if cuts:
        values = values * levels(own_key, extent, cuts, -0.22, 0.18)
    return jnp.clip(values, -bound, bound).astype(held_as)


def setup_inputs(seed: int = 0) -> dict:
    arg_keys = jax.random.split(jax.random.key(seed), 32)
    inputs = scatter_about(arg_keys[0], (GROUPS, TGT, D), 1.0, 6.0, ((0, 4), (1, 8)))
    memory = scatter_about(arg_keys[1], (GROUPS, SRC, D), 1.0, 6.0, ((0, 4), (1, 8)))
    target_lengths = draw_target_lengths(jax.random.fold_in(arg_keys[31], 71), 0)
    source_lengths = draw_source_lengths(jax.random.fold_in(arg_keys[31], 71), 0)
    target_order = draw_target_order(jax.random.fold_in(arg_keys[31], 71), 0)
    source_order = draw_source_order(jax.random.fold_in(arg_keys[31], 71), 0)
    self_gain = jnp.clip(1.0 + 0.18 * jax.random.normal(arg_keys[6], (D,), jnp.float32), 0.099609375, 1.8984375).astype(jnp.bfloat16)
    self_shift = scatter_about(arg_keys[7], (D,), 0.3, 1.75)
    self_query = scatter_about(arg_keys[8], (D, D), D ** -0.5, 0.25)
    query_bias = scatter_about(arg_keys[9], (D,), 0.3, 1.75)
    self_key = scatter_about(arg_keys[10], (D, D), D ** -0.5, 0.25)
    self_value = scatter_about(arg_keys[11], (D, D), D ** -0.5, 0.25)
    value_bias = scatter_about(arg_keys[12], (D,), 0.3, 1.75)
    self_output = scatter_about(arg_keys[13], (D, D), (D // 16) ** -0.5, 1.0)
    output_bias = scatter_about(arg_keys[14], (D,), 0.3, 1.75)
    cross_gain = jnp.clip(1.0 + 0.18 * jax.random.normal(arg_keys[15], (D,), jnp.float32), 0.099609375, 1.8984375).astype(jnp.bfloat16)
    cross_shift = scatter_about(arg_keys[16], (D,), 0.3, 1.75)
    cross_query = scatter_about(arg_keys[17], (D, D), D ** -0.5, 0.25)
    cquery_bias = scatter_about(arg_keys[18], (D,), 0.3, 1.75)
    cross_key = scatter_about(arg_keys[19], (D, D), D ** -0.5, 0.25)
    cross_value = scatter_about(arg_keys[20], (D, D), D ** -0.5, 0.25)
    cvalue_bias = scatter_about(arg_keys[21], (D,), 0.3, 1.75)
    cross_output = scatter_about(arg_keys[22], (D, D), (D // 16) ** -0.5, 1.0)
    coutput_bias = scatter_about(arg_keys[23], (D,), 0.3, 1.75)
    final_gain = jnp.clip(1.0 + 0.18 * jax.random.normal(arg_keys[24], (D,), jnp.float32), 0.099609375, 1.8984375).astype(jnp.bfloat16)
    final_shift = scatter_about(arg_keys[25], (D,), 0.3, 1.75)
    inner_weight = scatter_about(arg_keys[26], (D, FF), D ** -0.5, 0.25)
    inner_bias = scatter_about(arg_keys[27], (FF,), 0.3, 1.75)
    outer_weight = scatter_about(arg_keys[28], (FF, D), FF ** -0.5, 0.125)
    outer_bias = scatter_about(arg_keys[29], (D,), 0.3, 1.75)
    cotangent = scatter_about(arg_keys[30], (GROUPS, TGT, D), 1.0, 6.0, ((0, 4), (1, 8)))
    return {"inputs": inputs, "memory": memory, "target_lengths": target_lengths, "source_lengths": source_lengths, "target_order": target_order, "source_order": source_order, "self_gain": self_gain, "self_shift": self_shift, "self_query": self_query, "query_bias": query_bias, "self_key": self_key, "self_value": self_value, "value_bias": value_bias, "self_output": self_output, "output_bias": output_bias, "cross_gain": cross_gain, "cross_shift": cross_shift, "cross_query": cross_query, "cquery_bias": cquery_bias, "cross_key": cross_key, "cross_value": cross_value, "cvalue_bias": cvalue_bias, "cross_output": cross_output, "coutput_bias": coutput_bias, "final_gain": final_gain, "final_shift": final_shift, "inner_weight": inner_weight, "inner_bias": inner_bias, "outer_weight": outer_weight, "outer_bias": outer_bias, "cotangent": cotangent}


@jax.custom_vjp
def low(v):
    return lax.optimization_barrier(v.astype(jnp.bfloat16)).astype(jnp.float32)

@jax.custom_vjp
def low_back(v):
    return v

def low_keep(v):
    return (low(v), None)

def low_pass(kept, grad):
    return (grad,)

def back_keep(v):
    return (v, None)

def back_low(kept, grad):
    return (low(grad),)
low.defvjp(low_keep, low_pass)
low_back.defvjp(back_keep, back_low)
EPSILON = 1e-05
HIGH = lax.Precision.HIGHEST

def both(values):
    return low(low_back(values))

def norm(values, gain, shift):
    center = values - lax.optimization_barrier(jnp.mean(values, axis=-1, keepdims=True))
    spread = lax.optimization_barrier(jnp.mean(center * center, axis=-1, keepdims=True))
    return center * lax.rsqrt(spread + EPSILON) * gain + shift

def matmul(left, right):
    return jnp.dot(left, right, precision=HIGH)

def placement(order, lengths, blocksize, total):
    index = jnp.arange(total, dtype=jnp.int32)
    slot = index // blocksize
    picked = lax.optimization_barrier(jnp.sum(jnp.where(slot[:, None] == jnp.arange(order.shape[0], dtype=jnp.int32)[None, :], order[None, :], 0), axis=1))
    position = (picked * blocksize + index % blocksize).astype(jnp.int32)
    ends = jnp.cumsum(lengths)
    document = lax.optimization_barrier(jnp.sum((position[:, None] >= ends[None, :]).astype(jnp.int32), axis=1)).astype(jnp.int32)
    return (document, position)

def visible(query_doc, query_pos, key_doc, key_pos, causal, padded):
    same = query_doc[:, None] == key_doc[None, :]
    if causal:
        return same & (key_pos[None, :] <= query_pos[:, None])
    return same

def attend(queries, keys, values, query_info, key_info, causal, padded):
    total = queries.shape[0]
    width = math.gcd(total, 512)
    count = total // width
    key_heads = keys.reshape(keys.shape[0], HEADS, HDIM)
    value_heads = values.reshape(values.shape[0], HEADS, HDIM)

    def block(item):
        block_rows, block_doc, block_pos = item
        scores = low_back(jnp.einsum('qhd,khd->qhk', block_rows.reshape(width, HEADS, HDIM), key_heads, precision=HIGH))
        allowed = visible(block_doc, block_pos, key_info[0], key_info[1], causal, padded)[:, None, :]
        highest = lax.optimization_barrier(jnp.max(jnp.where(allowed, scores, -jnp.inf), axis=-1, keepdims=True))
        powers = jnp.exp(jnp.where(allowed, scores - highest, -jnp.inf))
        weights = low(powers / lax.optimization_barrier(jnp.sum(powers, axis=-1, keepdims=True)))
        return jnp.einsum('qhk,khd->qhd', weights, value_heads, precision=HIGH).reshape(width, D)
    output = lax.map(jax.checkpoint(block), (queries.reshape(count, width, D), query_info[0].reshape(count, width), query_info[1].reshape(count, width)))
    return output.reshape(total, D)

def layer(weights, inputs, memory, target_info, source_info, padded):
    self_gain, self_shift, self_query, query_bias, self_key, self_value, value_bias, self_output, output_bias, cross_gain, cross_shift, cross_query, cquery_bias, cross_key, cross_value, cvalue_bias, cross_output, coutput_bias, final_gain, final_shift, inner_weight, inner_bias, outer_weight, outer_bias = weights
    scale = HDIM ** (-0.5)
    normed = low(norm(inputs, self_gain, self_shift))
    queries = both((matmul(normed, self_query) + query_bias) * scale)
    keys = both(matmul(normed, self_key))
    values = both(matmul(normed, self_value) + value_bias)
    mixed = both(attend(queries, keys, values, target_info, target_info, True, padded))
    middle = inputs + low_back(matmul(mixed, self_output) + output_bias)
    crossed = low(norm(middle, cross_gain, cross_shift))
    cqueries = both((matmul(crossed, cross_query) + cquery_bias) * scale)
    ckeys = both(matmul(memory, cross_key))
    cvalues = both(matmul(memory, cross_value) + cvalue_bias)
    heard = both(attend(cqueries, ckeys, cvalues, target_info, source_info, False, padded))
    later = middle + low_back(matmul(heard, cross_output) + coutput_bias)
    fed = low(norm(later, final_gain, final_shift))
    before = low_back(matmul(fed, inner_weight) + inner_bias)
    after = low(jax.nn.gelu(before, approximate=False))
    return later + low_back(matmul(after, outer_weight) + outer_bias)

def reference(inputs, memory, target_lengths, source_lengths, target_order, source_order, self_gain, self_shift, self_query, query_bias, self_key, self_value, value_bias, self_output, output_bias, cross_gain, cross_shift, cross_query, cquery_bias, cross_key, cross_value, cvalue_bias, cross_output, coutput_bias, final_gain, final_shift, inner_weight, inner_bias, outer_weight, outer_bias, cotangent):
    weights = tuple((weight.astype(jnp.float32) for weight in (self_gain, self_shift, self_query, query_bias, self_key, self_value, value_bias, self_output, output_bias, cross_gain, cross_shift, cross_query, cquery_bias, cross_key, cross_value, cvalue_bias, cross_output, coutput_bias, final_gain, final_shift, inner_weight, inner_bias, outer_weight, outer_bias)))
    padded = target_lengths.shape[1]
    target_info = jax.vmap(lambda order, lengths: placement(order, lengths, TOK_DEV // 2, TGT))(target_order, target_lengths)
    source_info = jax.vmap(lambda order, lengths: placement(order, lengths, SRC_DEV // 2, SRC))(source_order, source_lengths)

    def whole(weights, states, encoded):

        def single(item):
            return layer(weights, item[0], item[1], (item[2], item[3]), (item[4], item[5]), padded)
        return lax.map(single, (states, encoded, target_info[0], target_info[1], source_info[0], source_info[1]))
    result, pullback = jax.vjp(whole, weights, inputs.astype(jnp.float32), memory.astype(jnp.float32))
    grad_weights, grad_inputs, grad_memory = pullback(cotangent.astype(jnp.float32))
    return (result.astype(jnp.bfloat16), grad_inputs, grad_memory, grad_weights[0], grad_weights[1], grad_weights[2], grad_weights[3], grad_weights[4], grad_weights[5], grad_weights[6], grad_weights[7], grad_weights[8], grad_weights[9], grad_weights[10], grad_weights[11], grad_weights[12], grad_weights[13], grad_weights[14], grad_weights[15], grad_weights[16], grad_weights[17], grad_weights[18], grad_weights[19], grad_weights[20], grad_weights[21], grad_weights[22], grad_weights[23])
```

```python
import math

import jax
import jax.numpy as jnp
from jax import lax
from jax.experimental import pallas as pl
from jax.experimental.pallas import tpu as pltpu
from jax.sharding import PartitionSpec as P

D = 512
HEADS = 8


EPSILON = 1e-05
NEGATIVE = -1e30


def norm(values, gain, shift):
    center = values - jnp.mean(values, axis=-1, keepdims=True)
    spread = jnp.mean(center * center, axis=-1, keepdims=True)
    return center * lax.rsqrt(spread + EPSILON) * gain + shift


def product(left, right):
    return jnp.dot(left, right, preferred_element_type=jnp.float32)


def weight_grad(left, right):
    return jnp.einsum("ti,to->io", left, right, preferred_element_type=jnp.float32)


def input_grad(grad, weight):
    return jnp.einsum("to,io->ti", grad, weight, preferred_element_type=jnp.float32)


def split_heads(values):
    return values.reshape(values.shape[0], HEADS, -1)


def locate(order, lengths, blocksize, start, count):
    index = start + jnp.arange(count, dtype=jnp.int32)
    slot = index // blocksize
    picked = jnp.sum(
        jnp.where(
            slot[:, None] == jnp.arange(order.shape[0], dtype=jnp.int32)[None, :], order[None, :], 0
        ),
        axis=1,
    )
    position = picked * blocksize + index % blocksize
    ends = jnp.cumsum(lengths)
    document = jnp.sum((position[:, None] >= ends[None, :]).astype(jnp.int32), axis=1)
    return (document, position)


def visible(query_doc, query_pos, key_doc, key_pos, causal):
    same = query_doc[:, None] == key_doc[None, :]
    if causal:
        return same & (key_pos[None, :] <= query_pos[:, None])
    return same


def opening(rows):
    return (
        jnp.zeros((rows, HEADS, D // HEADS), jnp.float32),
        jnp.full((rows, HEADS), NEGATIVE, jnp.float32),
        jnp.zeros((rows, HEADS), jnp.float32),
    )


def online(carry, query_heads, piece_keys, piece_values, allowed):
    weighted, highest, total = carry
    scores = jnp.einsum(
        "qhd,khd->qhk", query_heads, split_heads(piece_keys), preferred_element_type=jnp.float32
    )
    allowed = allowed[:, None, :]
    raised = jnp.maximum(highest, jnp.max(jnp.where(allowed, scores, NEGATIVE), axis=-1))
    powers = jnp.exp(jnp.where(allowed, scores - raised[..., None], NEGATIVE))
    total = jnp.sum(powers, axis=-1)
    weighted = jnp.einsum(
        "qhk,khd->qhd",
        powers.astype(jnp.bfloat16),
        split_heads(piece_values),
        preferred_element_type=jnp.float32,
    )
    return (weighted, raised, total)


def finish(carry):
    weighted, highest, total = carry
    return (highest + jnp.log(total), (weighted / total[..., None]).reshape(weighted.shape[0], D))


def block_back(query_heads, grad_heads, log_total, delta, piece_keys, piece_values, allowed):
    key_heads = split_heads(piece_keys)
    value_heads = split_heads(piece_values)
    scores = jnp.einsum("qhd,khd->qhk", query_heads, key_heads, preferred_element_type=jnp.float32)
    weights = jnp.exp(jnp.where(allowed[:, None, :], scores - log_total[..., None], NEGATIVE))
    grad_weights = jnp.einsum(
        "qhd,khd->qhk", grad_heads, value_heads, preferred_element_type=jnp.float32
    )
    grad_scores = (weights * (grad_weights - delta[..., None])).astype(jnp.bfloat16)
    grad_values = jnp.einsum(
        "qhk,qhd->khd", weights.astype(jnp.bfloat16), grad_heads, preferred_element_type=jnp.float32
    )
    grad_keys = jnp.einsum(
        "qhk,qhd->khd", grad_scores, query_heads, preferred_element_type=jnp.float32
    )
    grad_query = jnp.einsum(
        "qhk,khd->qhd", grad_scores, key_heads, preferred_element_type=jnp.float32
    )
    return (grad_query, grad_keys, grad_values)


def scan_back(
    query_heads,
    grad_heads,
    log_total,
    delta,
    all_keys,
    all_values,
    row_doc,
    row_pos,
    order,
    lengths,
    blocksize,
    causal,
):
    total_keys = all_keys.shape[0]
    width = math.gcd(total_keys, 512)
    count = total_keys // width

    def step(grad_query, item):
        block_keys, block_values, number = item
        key_doc, key_pos = locate(order, lengths, blocksize, number * width, width)
        allowed = visible(row_doc, row_pos, key_doc, key_pos, causal)
        query_term, key_term, value_term = block_back(
            query_heads, grad_heads, log_total, delta, block_keys, block_values, allowed
        )
        return (grad_query + query_term, (key_term, value_term))

    grad_query, (grad_keys, grad_values) = lax.scan(
        step,
        jnp.zeros(query_heads.shape, jnp.float32),
        (
            all_keys.reshape(count, width, D),
            all_values.reshape(count, width, D),
            jnp.arange(count, dtype=jnp.int32),
        ),
    )
    return (grad_query, grad_keys.reshape(total_keys, D), grad_values.reshape(total_keys, D))


def on_device(
    inputs,
    memory,
    target_lengths,
    source_lengths,
    target_order,
    source_order,
    self_gain,
    self_shift,
    self_query,
    query_bias,
    self_key,
    self_value,
    value_bias,
    self_output,
    output_bias,
    cross_gain,
    cross_shift,
    cross_query,
    cquery_bias,
    cross_key,
    cross_value,
    cvalue_bias,
    cross_output,
    coutput_bias,
    final_gain,
    final_shift,
    inner_weight,
    inner_bias,
    outer_weight,
    outer_bias,
    cotangent,
):
    rows = inputs.shape[1]
    sources = memory.shape[1]
    target_half = rows // 2
    source_half = sources // 2
    own_lengths = target_lengths[0]
    memory_lengths = source_lengths[0]
    own_order = target_order[0]
    memory_order = source_order[0]
    scale = float(D // HEADS) ** (-0.5)
    place = lax.axis_index("seq")
    row_doc, row_pos = locate(own_order, own_lengths, target_half, place * rows, rows)
    inputs_f = inputs[0].astype(jnp.float32)
    encoded = memory[0]
    normed, norm_back = jax.vjp(
        norm, inputs_f, self_gain.astype(jnp.float32), self_shift.astype(jnp.float32)
    )
    normed_low = normed.astype(jnp.bfloat16)
    queries = ((product(normed_low, self_query) + query_bias) * scale).astype(jnp.bfloat16)
    keys = product(normed_low, self_key).astype(jnp.bfloat16)
    values = (product(normed_low, self_value) + value_bias).astype(jnp.bfloat16)
    query_heads = split_heads(queries)
    piece = (
        lax.all_gather(keys, "seq", axis=0, tiled=True),
        lax.all_gather(values, "seq", axis=0, tiled=True),
    )
    key_doc, key_pos = locate(own_order, own_lengths, target_half, jnp.int32(0), piece[0].shape[0])
    self_carry = online(
        opening(rows),
        query_heads,
        piece[0],
        piece[1],
        visible(row_doc, row_pos, key_doc, key_pos, True),
    )
    self_total, mixed = finish(self_carry)
    mixed_low = mixed.astype(jnp.bfloat16)
    middle = inputs_f + product(mixed_low, self_output) + output_bias
    crossed, cross_back = jax.vjp(
        norm, middle, cross_gain.astype(jnp.float32), cross_shift.astype(jnp.float32)
    )
    crossed_low = crossed.astype(jnp.bfloat16)
    cqueries = ((product(crossed_low, cross_query) + cquery_bias) * scale).astype(jnp.bfloat16)
    ckeys = product(encoded, cross_key).astype(jnp.bfloat16)
    cvalues = (product(encoded, cross_value) + cvalue_bias).astype(jnp.bfloat16)
    cquery_heads = split_heads(cqueries)
    piece = (
        lax.all_gather(ckeys, "seq", axis=0, tiled=True),
        lax.all_gather(cvalues, "seq", axis=0, tiled=True),
    )
    key_doc, key_pos = locate(
        memory_order, memory_lengths, source_half, jnp.int32(0), piece[0].shape[0]
    )
    cross_carry = online(
        opening(rows),
        cquery_heads,
        piece[0],
        piece[1],
        visible(row_doc, row_pos, key_doc, key_pos, False),
    )
    cross_total, heard = finish(cross_carry)
    heard_low = heard.astype(jnp.bfloat16)
    later = middle + product(heard_low, cross_output) + coutput_bias
    fed, final_back = jax.vjp(
        norm, later, final_gain.astype(jnp.float32), final_shift.astype(jnp.float32)
    )
    fed_low = fed.astype(jnp.bfloat16)
    before = product(fed_low, inner_weight) + inner_bias
    after, gelu_back = jax.vjp(lambda entry: jax.nn.gelu(entry, approximate=False), before)
    after_low = after.astype(jnp.bfloat16)
    result = later + product(after_low, outer_weight) + outer_bias
    grad_out = cotangent[0]
    outer_weight_grad = weight_grad(after_low, grad_out)
    outer_bias_grad = jnp.sum(grad_out.astype(jnp.float32), axis=0)
    grad_after = input_grad(grad_out, outer_weight)
    grad_before = gelu_back(grad_after)[0].astype(jnp.bfloat16)
    inner_weight_grad = weight_grad(fed_low, grad_before)
    inner_bias_grad = jnp.sum(grad_before.astype(jnp.float32), axis=0)
    grad_fed = input_grad(grad_before, inner_weight)
    grad_later_norm, final_gain_grad, final_shift_grad = final_back(grad_fed)
    grad_later = cotangent[0].astype(jnp.float32) + grad_later_norm
    grad_cbranch = grad_later.astype(jnp.bfloat16)
    cross_output_grad = weight_grad(heard_low, grad_cbranch)
    coutput_bias_grad = jnp.sum(grad_cbranch.astype(jnp.float32), axis=0)
    grad_heard = input_grad(grad_cbranch, cross_output).astype(jnp.bfloat16)
    grad_heard_heads = split_heads(grad_heard)
    cross_delta = jnp.sum(grad_heard_heads.astype(jnp.float32) * split_heads(heard), axis=-1)
    all_ckeys, all_cvalues = (
        lax.all_gather(ckeys, "seq", axis=0, tiled=True),
        lax.all_gather(cvalues, "seq", axis=0, tiled=True),
    )
    grad_cq, part_ckeys, part_cvalues = scan_back(
        cquery_heads,
        grad_heard_heads,
        cross_total,
        cross_delta,
        all_ckeys,
        all_cvalues,
        row_doc,
        row_pos,
        memory_order,
        memory_lengths,
        source_half,
        False,
    )
    own_ckeys, own_cvalues = (
        lax.psum_scatter(
            part_ckeys.astype(jnp.bfloat16), "seq", scatter_dimension=0, tiled=True
        ).astype(jnp.float32),
        lax.psum_scatter(
            part_cvalues.astype(jnp.bfloat16), "seq", scatter_dimension=0, tiled=True
        ).astype(jnp.float32),
    )
    own_ckeys_low = own_ckeys.astype(jnp.bfloat16)
    own_cvalues_low = own_cvalues.astype(jnp.bfloat16)
    cross_key_grad = weight_grad(encoded, own_ckeys_low)
    cross_value_grad = weight_grad(encoded, own_cvalues_low)
    cvalue_bias_grad = jnp.sum(own_cvalues_low.astype(jnp.float32), axis=0)
    memory_grad = input_grad(own_ckeys_low, cross_key) + input_grad(own_cvalues_low, cross_value)
    grad_cq_low = grad_cq.reshape(rows, D).astype(jnp.bfloat16)
    cross_query_grad = weight_grad(crossed_low, grad_cq_low) * scale
    cquery_bias_grad = jnp.sum(grad_cq_low.astype(jnp.float32), axis=0) * scale
    grad_crossed = input_grad(grad_cq_low, cross_query) * scale
    grad_middle_norm, cross_gain_grad, cross_shift_grad = cross_back(grad_crossed)
    grad_middle = grad_later + grad_middle_norm
    grad_sbranch = grad_middle.astype(jnp.bfloat16)
    self_output_grad = weight_grad(mixed_low, grad_sbranch)
    output_bias_grad = jnp.sum(grad_sbranch.astype(jnp.float32), axis=0)
    grad_mixed = input_grad(grad_sbranch, self_output).astype(jnp.bfloat16)
    grad_mixed_heads = split_heads(grad_mixed)
    self_delta = jnp.sum(grad_mixed_heads.astype(jnp.float32) * split_heads(mixed), axis=-1)
    all_keys, all_values = (
        lax.all_gather(keys, "seq", axis=0, tiled=True),
        lax.all_gather(values, "seq", axis=0, tiled=True),
    )
    grad_q, part_keys, part_values = scan_back(
        query_heads,
        grad_mixed_heads,
        self_total,
        self_delta,
        all_keys,
        all_values,
        row_doc,
        row_pos,
        own_order,
        own_lengths,
        target_half,
        True,
    )
    own_keys, own_values = (
        lax.psum_scatter(
            part_keys.astype(jnp.bfloat16), "seq", scatter_dimension=0, tiled=True
        ).astype(jnp.float32),
        lax.psum_scatter(
            part_values.astype(jnp.bfloat16), "seq", scatter_dimension=0, tiled=True
        ).astype(jnp.float32),
    )
    own_keys_low = own_keys.astype(jnp.bfloat16)
    own_values_low = own_values.astype(jnp.bfloat16)
    self_key_grad = weight_grad(normed_low, own_keys_low)
    self_value_grad = weight_grad(normed_low, own_values_low)
    value_bias_grad = jnp.sum(own_values_low.astype(jnp.float32), axis=0)
    grad_q_low = grad_q.reshape(rows, D).astype(jnp.bfloat16)
    self_query_grad = weight_grad(normed_low, grad_q_low) * scale
    query_bias_grad = jnp.sum(grad_q_low.astype(jnp.float32), axis=0) * scale
    grad_normed = (
        input_grad(grad_q_low, self_query) * scale
        + input_grad(own_keys_low, self_key)
        + input_grad(own_values_low, self_value)
    )
    grad_in_norm, self_gain_grad, self_shift_grad = norm_back(grad_normed)
    inputs_grad = grad_middle + grad_in_norm
    summed = lax.psum(
        (
            self_gain_grad,
            self_shift_grad,
            self_query_grad,
            query_bias_grad,
            self_key_grad,
            self_value_grad,
            value_bias_grad,
            self_output_grad,
            output_bias_grad,
            cross_gain_grad,
            cross_shift_grad,
            cross_query_grad,
            cquery_bias_grad,
            cross_key_grad,
            cross_value_grad,
            cvalue_bias_grad,
            cross_output_grad,
            coutput_bias_grad,
            final_gain_grad,
            final_shift_grad,
            inner_weight_grad,
            inner_bias_grad,
            outer_weight_grad,
            outer_bias_grad,
        ),
        ("seq", "batch"),
    )
    return (result.astype(jnp.bfloat16)[None], inputs_grad[None], memory_grad[None]) + tuple(summed)


HDIM = D // HEADS
SHORTEST = 32
LONGEST = 1024
CHUNK = 256
PIECE = 64
MESH = pl.DeviceIdType.MESH
PARTS = 2
BF = jnp.bfloat16
F32 = jnp.float32
VECTORS = 24


def nn(left, right):
    return lax.dot_general(left, right, (((1,), (0,)), ((), ())), preferred_element_type=F32)


def nt(left, right):
    return lax.dot_general(left, right, (((1,), (1,)), ((), ())), preferred_element_type=F32)


def tn(left, right):
    return lax.dot_general(left, right, (((0,), (0,)), ((), ())), preferred_element_type=F32)


def centred(values):
    center = values - jnp.mean(values, axis=-1, keepdims=True)
    spread = lax.rsqrt(jnp.mean(center * center, axis=-1, keepdims=True) + EPSILON)
    return center * spread, spread


def norm_back(grad, unit, spread, gain):
    scaled = grad * gain
    return spread * (
        scaled
        - jnp.mean(scaled, axis=-1, keepdims=True)
        - unit * jnp.mean(scaled * unit, axis=-1, keepdims=True)
    )


def column_sum(values):
    return jnp.sum(values, axis=0, keepdims=True)


def spread_heads(block, heads):
    lane = lax.broadcasted_iota(jnp.int32, block.shape, 1)
    return jnp.concatenate(
        [
            jnp.where((lane >= h * HDIM) & (lane < (h + 1) * HDIM), block, 0.0)
            for h in range(heads)
        ],
        axis=0,
    )


def join_heads(stacked, heads):
    rows = stacked.shape[0] // heads
    lane = lax.broadcasted_iota(jnp.int32, (rows, stacked.shape[1]), 1)
    total = stacked[:rows]
    for h in range(1, heads):
        total = jnp.where(lane >= h * HDIM, stacked[h * rows : (h + 1) * rows], total)
    return total


def part_of(array, index, size):
    if len(array.shape) == 3:
        count = size // PIECE
        return array[pl.ds(index * count, count)].reshape(size, array.shape[2])
    return array[pl.ds(pl.multiple_of(index * size, size), size), :]


def whole_of(array):
    return array[...].reshape(-1, array.shape[-1])


def attend(queries, keys, values, low, high, scores, powers):
    total = math.prod(keys.shape[:-1])
    width = queries.shape[0]
    chunk = total // PARTS
    pieces = chunk // PIECE

    def first(c, highest):
        rows = pl.ds(pl.multiple_of(c * chunk, chunk), chunk)
        place = lax.broadcasted_iota(jnp.int32, (chunk, width), 0) + c * chunk
        found = jnp.where((place >= low) & (place < high), nt(part_of(keys, c, chunk), queries), NEGATIVE)
        scores[rows, :] = found
        return jnp.maximum(highest, jnp.max(found, axis=0, keepdims=True))

    highest = lax.fori_loop(0, total // chunk, first, jnp.full((1, width), NEGATIVE, F32))

    def second(c, summed):
        rows = pl.ds(pl.multiple_of(c * chunk, chunk), chunk)
        power = jnp.exp(scores[rows, :] - highest)
        powers[pl.ds(c * pieces, pieces)] = power.astype(BF).reshape(pieces, PIECE, width)
        return summed + column_sum(power)

    summed = lax.fori_loop(0, total // chunk, second, jnp.zeros((1, width), F32))
    inverse = 1.0 / summed
    mixed = tn(whole_of(values), powers[0 : total // PIECE].reshape(total, width)) * inverse
    return mixed.T, inverse


def attend_back(queries, grads, product_of, keys, values, inverse, powers, store):
    total = math.prod(keys.shape[:-1])
    width = queries.shape[0]
    chunk = total // PARTS
    pieces = chunk // PIECE
    ones = jnp.ones((8, queries.shape[1]), BF)
    coarse = product_of.astype(BF)
    fine = (product_of - coarse.astype(F32)).astype(BF)
    delta = (nt(ones, coarse) + nt(ones, fine))[0:1]

    def step(c, carry):
        part = pl.ds(c * pieces, pieces)
        weights = powers[part].reshape(chunk, width).astype(F32) * inverse
        weights_low = weights.astype(BF)
        change = (weights * (nt(part_of(values, c, chunk), grads) - delta)).astype(BF)
        powers[part] = change.reshape(pieces, PIECE, width)
        store(c, nn(change, queries), nn(weights_low, grads))
        return carry

    lax.fori_loop(0, total // chunk, step, 0)
    return tn(whole_of(keys), powers[0 : total // PIECE].reshape(total, width)).T


class Cube:
    def __init__(self, me, level, levels):
        self.me, self.level, self.levels = me, level, levels
        self.bits = (lax.rem(me, 2), lax.rem(lax.div(me, 2), 2), lax.div(me, 4))

    def other(self, code):
        place = self.me
        for axis in range(3):
            if code >> axis & 1:
                place = place + (1 << axis) * (1 - 2 * self.bits[axis])
        return place

    def plane(self, step):
        return lax.rem(self.level + step, self.levels)

    def greet(self):
        barrier = pltpu.get_barrier_semaphore()
        for code in (1, 2, 4):
            pl.semaphore_signal(
                barrier, inc=1, device_id={"seq": self.other(code)}, device_id_type=MESH
            )
        for step in range(1, self.levels):
            pl.semaphore_signal(
                barrier, inc=1, device_id={"batch": self.plane(step)}, device_id_type=MESH
            )
        pl.semaphore_wait(barrier, 2 + self.levels)

    def send(self, code, source, target, send_sem, recv_sem):
        copy = pltpu.make_async_remote_copy(
            src_ref=source,
            dst_ref=target,
            send_sem=send_sem,
            recv_sem=recv_sem,
            device_id={"seq": self.other(code)},
            device_id_type=MESH,
        )
        copy.start()
        return copy


class Steps:
    def copies(self, step):
        return [
            pltpu.make_async_remote_copy(
                src_ref=source,
                dst_ref=target,
                send_sem=self.send_sem.at[index],
                recv_sem=self.recv_sem.at[index],
                device_id=device,
                device_id_type=MESH,
            )
            for device, source, target, index in self.moves(step)
        ]

    def begin(self, step):
        for copy in self.copies(step):
            copy.start()

    def end(self, step):
        for copy in self.copies(step):
            copy.wait()

    def advance(self, step):
        self.end(step)
        self.take(step)
        self.begin(step + 1)


class Reduce(Steps):
    def __init__(self, cube, panels, first, pair, flat, edge, deep, leave, send_sem, recv_sem, sent):
        self.cube, self.panels, self.first = cube, panels, first
        self.pair, self.flat, self.edge, self.deep, self.leave = pair, flat, edge, deep, leave
        self.send_sem, self.recv_sem, self.sent = send_sem, recv_sem, sent

    def begin(self, step):
        for index in {6: (1, 2), 8: (0,)}.get(step, ()):
            pl.semaphore_wait(self.sent.at[index], 1)
        if step == 4:
            for k in range(1, self.cube.levels):
                there = self.first + self.cube.plane(k)
                for axis in (1, 2):
                    self.leave[k - 1, axis - 1] = self.panels[there, self.rows(axis=axis, further=0), :]
        super().begin(step)

    def end(self, step):
        super().end(step)
        for index in {1: (0,), 3: (1, 2)}.get(step, ()):
            pl.semaphore_signal(
                self.sent.at[index],
                inc=1,
                device_id={"seq": self.cube.other(1 << index)},
                device_id_type=MESH,
            )

    def rows(self, core=0, axis=None, far=0, further=None):
        bits = self.cube.bits
        flip = lambda bit, other: 1 - bit if other else bit
        start, size = flip(bits[0], core) * (D // 2), D // 2
        if axis is not None:
            size = D // 8
            start = start + (axis - 1) * (D // 4) + flip(bits[axis], far) * size
            if further is not None:
                size = D // 16
                start = start + flip(bits[3 - axis], further) * size
        return pl.ds(pl.multiple_of(start, D // 16), size)

    def all(self, rows):
        return self.panels.at[pl.ds(self.first, 4), rows, :]

    def moves(self, step):
        cube = self.cube
        near = lambda code: {"seq": cube.other(code)}
        if step == 1:
            return [(near(1), self.all(self.rows(core=1)), self.pair, 0)]
        if step == 2:
            return [
                (near(2 * axis), self.all(self.rows(axis=axis, far=1)), self.flat.at[axis - 1], axis)
                for axis in (1, 2)
            ]
        if step == 3:
            return [
                (
                    near(6 - 2 * axis),
                    self.all(self.rows(axis=axis, further=1)),
                    self.edge.at[axis - 1],
                    2 + axis,
                )
                for axis in (1, 2)
            ]
        if step == 4:
            return [
                (
                    {"batch": cube.plane(k)},
                    self.leave.at[k - 1, axis - 1],
                    self.deep.at[k - 1, axis - 1],
                    3 + 2 * k + axis - 1,
                )
                for k in range(1, cube.levels)
                for axis in (1, 2)
            ]
        if step == 5:
            there = self.first + cube.level
            return [
                (
                    {"batch": cube.plane(k)},
                    self.panels.at[there, self.rows(axis=axis, further=0), :],
                    self.panels.at[there, self.rows(axis=axis, further=0), :],
                    9 + 2 * k + axis - 1,
                )
                for k in range(1, cube.levels)
                for axis in (1, 2)
            ]
        if step == 6:
            parts = [(6 - 2 * axis, self.all(self.rows(axis=axis, further=0)), 16 + axis) for axis in (1, 2)]
        elif step == 7:
            parts = [(2 * axis, self.all(self.rows(axis=axis)), 18 + axis) for axis in (1, 2)]
        else:
            parts = [(1, self.all(self.rows()), 21)]
        return [(near(code), part, part, index) for code, part, index in parts]

    def add(self, rows, found):
        def one(i, carry):
            there = self.first + i
            total = self.panels[there, rows, :].astype(F32) + found[i].astype(F32)
            self.panels[there, rows, :] = total.astype(BF)
            return carry

        lax.fori_loop(0, 4, one, 0)

    def take(self, step):
        if step == 1:
            self.add(self.rows(), self.pair)
        elif step == 2:
            for axis in (1, 2):
                self.add(self.rows(axis=axis), self.flat.at[axis - 1])
        elif step == 3:
            for axis in (1, 2):
                self.add(self.rows(axis=axis, further=0), self.edge.at[axis - 1])
        elif step == 4:
            there = self.first + self.cube.level
            for axis in (1, 2):
                rows = self.rows(axis=axis, further=0)
                total = self.panels[there, rows, :].astype(F32)
                for k in range(self.cube.levels - 1):
                    total = total + self.deep[k, axis - 1].astype(F32)
                self.panels[there, rows, :] = total.astype(BF)


class Scatter(Steps):
    def __init__(self, cube, block, spare, send_sem, recv_sem):
        self.cube, self.block, self.spare = cube, block, spare
        self.send_sem, self.recv_sem = send_sem, recv_sem

    def at(self, code, part):
        return self.block(2 * self.cube.other(code) + part)

    def moves(self, step):
        near = lambda code: {"seq": self.cube.other(code)}
        if step == 1:
            parts = [(1, 2 * i + 1, part, 2 * i + part) for i in range(4) for part in range(2)]
        elif step == 2:
            parts = [(2, 2, 0, 8), (2, 6, 0, 9), (4, 4, 1, 10), (4, 6, 1, 11)]
        else:
            parts = [(4, 4, 0, 12), (2, 2, 1, 13)]
        return [(near(to), self.at(code, part), self.spare(k), k) for to, code, part, k in parts]

    def take(self, step):
        if step == 1:
            parts = [(2 * i, part, 2 * i + part) for i in range(4) for part in range(2)]
        else:
            parts = [(0, 0, 8), (4, 0, 9), (0, 1, 10), (2, 1, 11)]
        for code, part, k in parts:
            here = self.at(code, part)
            here[...] = (here[...].astype(F32) + self.spare(k)[...].astype(F32)).astype(BF)

    def result(self, part):
        return self.at(0, part)[...].astype(F32) + self.spare(12 + part)[...].astype(F32)


class Small(Steps):
    def __init__(self, cube, array, spare, planes, send_sem, recv_sem):
        self.cube, self.array, self.spare, self.planes = cube, array, spare, planes
        self.send_sem, self.recv_sem = send_sem, recv_sem

    def moves(self, step):
        cube = self.cube
        if step < 4:
            return [({"seq": cube.other(1 << (step - 1))}, self.array, self.spare.at[step - 1], step - 1)]
        here = self.planes.at[cube.level]
        return [
            ({"batch": cube.plane(k)}, here, here, 2 + k) for k in range(1, cube.levels)
        ]

    def take(self, step):
        if step < 4:
            self.array[...] += self.spare[step - 1]
        if step == 3:
            self.planes[self.cube.level] = self.array[...]
        if step == 4:
            total = self.planes[0]
            for k in range(1, self.cube.levels):
                total = total + self.planes[k]
            self.array[...] = total


class Gather:
    def __init__(self, cube, own, slot_ref, send_sem, recv_sem):
        self.cube, self.own, self.slot_ref = cube, own, slot_ref
        self.send_sem, self.recv_sem = send_sem, recv_sem
        self.sent = []

    def push(self, step, code, part):
        slot = 2 * self.cube.other(code) + part
        target = self.slot_ref(slot)
        source = self.own.at[part] if code == 0 else target
        self.sent.append(
            self.cube.send(
                step,
                source,
                target,
                self.send_sem.at[len(self.sent)],
                self.recv_sem.at[2 * (code ^ step) + part],
            )
        )

    def take(self, code, part):
        slot = self.slot_ref(2 * self.cube.other(code) + part)
        pltpu.make_async_remote_copy(
            src_ref=slot,
            dst_ref=slot,
            send_sem=self.send_sem.at[0],
            recv_sem=self.recv_sem.at[2 * code + part],
            device_id={"seq": self.cube.other(1)},
            device_id_type=MESH,
        ).wait_recv()

    def arrived(self, code):
        for part in range(2):
            self.take(code, part)

    def open(self):
        for step, part in ((2, 0), (4, 1), (2, 1), (4, 0), (1, 0), (1, 1)):
            self.push(step, 0, part)

    def pass_on(self):
        self.take(2, 0)
        self.push(4, 2, 0)
        self.take(4, 1)
        self.push(2, 4, 1)
        self.push(1, 2, 0)
        self.push(1, 4, 1)
        self.take(2, 1)
        self.push(1, 2, 1)
        self.take(4, 0)
        self.push(1, 4, 0)

    def finish(self):
        for part in range(2):
            self.take(6, part)
            self.push(1, 6, part)

    def close(self):
        for copy in self.sent:
            copy.wait_send()


def publish_kernel(grads, dvec, *refs):
    kept, outs, (narrow, broad, load_sem, store_sem, keep_sem) = refs[:3], refs[3:-5], refs[-5:]
    keeps = [pltpu.make_async_copy(kept[i], outs[24 + i], keep_sem.at[i]) for i in range(3)]
    order = list(range(8, 16)) + list(range(4, 8)) + list(range(4))
    loads = [pltpu.make_async_copy(grads.at[i], narrow.at[i], load_sem.at[i]) for i in order]
    for load in loads + keeps:
        load.start()
    for i in range(13):
        outs[10 + i][...] = dvec[i, :]
    for i in range(4):
        outs[23][i * D : (i + 1) * D] = dvec[13 + i, :]
    stores = []
    for load, i in zip(loads, order):
        load.wait()
        broad[i] = narrow[i].astype(F32)
        if i < 8:
            target = outs[i]
        elif i % 2 == 0:
            target = outs[8].at[:, pl.ds((i - 8) // 2 * D, D)]
        else:
            target = outs[9].at[pl.ds((i - 8) // 2 * D, D), :]
        store = pltpu.make_async_copy(broad.at[i], target, store_sem.at[i])
        store.start()
        stores.append(store)
    for store in stores + keeps:
        store.wait()


def publish(grads, dvec, kept):
    vmem = pl.BlockSpec(memory_space=pltpu.VMEM)
    hbm = pl.BlockSpec(memory_space=pl.ANY)
    shapes = [(D, D)] * 8 + [(D, 4 * D), (4 * D, D)] + [(D,)] * 13 + [(4 * D,)]
    return pl.pallas_call(
        publish_kernel,
        out_shape=tuple(
            [jax.ShapeDtypeStruct(shape, F32) for shape in shapes]
            + [jax.ShapeDtypeStruct(array.shape, array.dtype) for array in kept]
        ),
        in_specs=[hbm, vmem] + [hbm] * 3,
        out_specs=tuple([hbm] * 10 + [vmem] * 14 + [hbm] * 3),
        scratch_shapes=[
            pltpu.VMEM((16, D, D), BF),
            pltpu.VMEM((16, D, D), F32),
            pltpu.SemaphoreType.DMA((16,)),
            pltpu.SemaphoreType.DMA((16,)),
            pltpu.SemaphoreType.DMA((3,)),
        ],
        compiler_params=pltpu.CompilerParams(vmem_limit_bytes=48 << 20),
    )(grads, dvec, *kept)


def layer_kernel(
    sizes,
    tlen,
    slen,
    tord,
    sord,
    own,
    cot,
    own_memory,
    vectors,
    w_small,
    w_in,
    w_out,
    result,
    dinputs,
    dmemory,
    dvec,
    grads,
    vec,
    nrm,
    memory,
    stream,
    weight,
    kv,
    queries,
    ckeys,
    cvalues,
    scores,
    powers,
    cpowers,
    inverses,
    cinverses,
    mixed,
    heard,
    unit,
    low,
    tinv,
    sinv,
    pairs,
    flats,
    edges,
    deeps,
    leaves,
    spares,
    planes,
    sem,
    send_sem,
    recv_sem,
    group_send,
    group_recv,
    group_sent,
    scatter_send,
    scatter_recv,
    small_send,
    small_recv,
    ready,
):
    rows, blocks, half, sblocks, shalf, ndoc, window = (
        sizes["rows"],
        sizes["blocks"],
        sizes["half"],
        sizes["sblocks"],
        sizes["shalf"],
        sizes["ndoc"],
        sizes["window"],
    )
    around = -(-window // half)
    pad = around * half - window
    sources = sblocks * shalf
    later = dinputs
    me = lax.axis_index("seq")
    scale = float(HDIM) ** -0.5
    thirds = half // PIECE
    cube = Cube(me, lax.axis_index("batch"), sizes["levels"])
    cube.greet()

    def raw(slot):
        return powers.at[lax.rem(slot, 4), pl.ds(lax.div(slot, 4) * thirds, thirds), :, 0:D]

    def raw_memory(slot):
        return memory.at[slot]

    gather_rows = Gather(cube, own, raw, send_sem.at[0], recv_sem.at[0])
    gather_sources = Gather(cube, own_memory, raw_memory, send_sem.at[1], recv_sem.at[1])
    gather_rows.open()
    groups = [
        Reduce(
            cube, weight, first, pairs.at[turn % 2], flats.at[turn % 2], edges.at[turn % 2],
            deeps.at[turn % 2], leaves.at[turn % 2], group_send.at[turn], group_recv.at[turn],
            group_sent.at[turn],
        )
        for turn, first in enumerate((8, 12, 4, 0))
    ]

    def spare_block(k):
        return powers.at[k % 4, pl.ds(k // 4 * thirds, thirds), :, 0:D]

    rows_back = Scatter(
        cube, lambda slot: nrm.at[slot], spare_block, scatter_send.at[0], scatter_recv.at[0]
    )
    memory_back = Scatter(
        cube,
        lambda slot: cvalues.at[pl.ds(pl.multiple_of(slot * shalf, shalf), shalf), :],
        lambda k: memory.at[k],
        scatter_send.at[1],
        scatter_recv.at[1],
    )
    small = Small(cube, dvec, spares, planes, small_send, small_recv)

    row = 0
    for vector_ref in vectors:
        for start in range(0, vector_ref.shape[0], D):
            vec[row : row + 1, :] = vector_ref[start : start + D].astype(F32).reshape(1, D)
            row += 1

    copies = []
    for index, (source, target) in enumerate(
        [(w_small[i], weight.at[i]) for i in range(8)]
        + [(w_in.at[:, pl.ds(D * i, D)], weight.at[8 + 2 * i]) for i in range(4)]
        + [(w_out.at[pl.ds(D * i, D), :], weight.at[9 + 2 * i]) for i in range(4)]
    ):
        copy = pltpu.make_async_copy(source, target, sem.at[index])
        copy.start()
        copies.append(copy)

    for order, inverse_of, count in ((tord, tinv, blocks), (sord, sinv, sblocks)):
        for t in range(count):
            found = jnp.int32(0)
            for s in range(count):
                found = jnp.where(order[0, s] == t, s, found)
            inverse_of[t] = found
    tends, sends = [], []
    tend, send = jnp.int32(0), jnp.int32(0)
    for d in range(ndoc):
        tend, send = tend + tlen[0, d], send + slen[0, d]
        tends.append(tend)
        sends.append(send)
    base = [tord[0, 2 * me + b] for b in range(2)]

    def vector(index):
        return vec[index : index + 1, :]

    for copy in copies:
        copy.wait()

    states = own[...].reshape(rows, D)
    own_normed = (centred(states.astype(F32))[0] * vector(0) + vector(1)).astype(BF)
    queries[...] = ((nn(own_normed, weight[0]) + vector(2)) * scale).astype(BF)

    def project_block(s, block):
        found, _ = centred(block.astype(F32))
        normed = (found * vector(0) + vector(1)).astype(BF)
        nrm[s] = normed.reshape(thirds, PIECE, D)
        keys = nn(normed, weight[1]).astype(BF)
        values = (nn(normed, weight[2]) + vector(3)).astype(BF)
        for quad in range(2):
            kv[0, quad, s] = keys[:, quad * 256 : (quad + 1) * 256]
            kv[1, quad, s] = values[:, quad * 256 : (quad + 1) * 256]

    def project(code):
        def one(part, carry):
            s = 2 * cube.other(code) + part
            project_block(s, raw(s)[...].reshape(half, D))
            return carry

        lax.fori_loop(0, 2, one, 0)

    for part in range(2):
        project_block(2 * me + part, own[part].reshape(half, D))
    gather_rows.arrived(1)
    project(1)
    gather_rows.pass_on()
    gather_sources.open()
    project(2)
    project(4)
    gather_rows.arrived(3)
    project(3)
    gather_rows.arrived(5)
    project(5)
    gather_rows.finish()
    project(6)
    gather_rows.arrived(7)
    project(7)
    gather_rows.close()
    gather_sources.pass_on()

    def limits(b):
        index = lax.broadcasted_iota(jnp.int32, (1, 4 * half), 1)
        row = index
        for h in range(1, 4):
            row = jnp.where(index >= h * half, index - h * half, row)
        position = base[b] * half + row
        start = jnp.zeros_like(position)
        for end in tends:
            start = jnp.where(position >= end, end, start)
        shift = (base[b] + 1) * half - window
        return start - shift, position - shift + 1

    kwin, vwin = [
        cpowers.at[kind, pl.ds(0, window // PIECE), :, pl.ds(D, 4 * HDIM)] for kind in range(2)
    ]

    def fill(b, quad):
        skip = pad // PIECE
        for j in range(around):
            slot = tinv[jnp.maximum(base[b] - (around - 1) + j, 0)]
            for kind, target in ((0, kwin), (1, vwin)):
                block = kv[kind, quad, slot].reshape(thirds, PIECE, 4 * HDIM)
                if j == 0:
                    target[0 : thirds - skip] = block[skip:]
                else:
                    target[j * thirds - skip : (j + 1) * thirds - skip] = block

    for b in range(2):
        begin, stop = limits(b)

        def forward(quad, carry, b=b, begin=begin, stop=stop):
            fill(b, quad)
            lanes = pl.ds(pl.multiple_of(quad * 256, 256), 256)
            block = queries[b * half : (b + 1) * half, lanes].astype(F32)
            out, inverse = attend(
                spread_heads(block, 4).astype(BF),
                kwin,
                vwin,
                begin,
                stop,
                scores.at[pl.ds(0, window), :],
                powers.at[b * 2 + quad],
            )
            inverses[b * 2 + quad] = jnp.broadcast_to(inverse, (8, 4 * half))
            mixed[b * half : (b + 1) * half, lanes] = join_heads(out, 4)
            return carry

        lax.fori_loop(0, 2, forward, 0)

    middle = own[...].reshape(rows, D).astype(F32) + nn(mixed[...].astype(BF), weight[3]) + vector(4)
    found, spread = centred(middle)
    later[...] = middle
    unit[0] = found
    low[0] = (found * vector(5) + vector(6)).astype(BF)
    cross_spread = spread
    low[1] = ((nn(low[0], weight[4]) + vector(7)) * scale).astype(BF)

    gather_sources.finish()
    for code in (1, 3, 5, 7):
        gather_sources.arrived(code)
    for part in range(2):
        memory[2 * me + part] = own_memory[part]
    gather_sources.close()

    def place(t, carry):
        stream[t] = memory[sinv[t]]
        return carry

    lax.fori_loop(0, sblocks, place, 0)
    step = sources // 2
    some = sblocks // 2

    def sources_of(c, carry):
        part = pl.ds(pl.multiple_of(c * step, step), step)
        block = stream[pl.ds(c * some, some)].reshape(step, D)
        ckeys[part, :] = nn(block, weight[5]).astype(BF)
        cvalues[part, :] = (nn(block, weight[6]) + vector(8)).astype(BF)
        return carry

    lax.fori_loop(0, sources // step, sources_of, 0)
    index = lax.broadcasted_iota(jnp.int32, (1, 2 * rows), 1)
    row = jnp.where(index >= rows, index - rows, index)
    position = jnp.where(row >= half, base[1] * half + row - half, base[0] * half + row)
    begin = jnp.zeros_like(position)
    stop = jnp.full_like(position, sources)
    for end, send in zip(tends, sends):
        begin = jnp.where(position >= end, send, begin)
    for end, send in reversed(list(zip(tends, sends))):
        stop = jnp.where(position < end, send, stop)

    def cross_forward(pair, carry):
        lanes = pl.ds(pl.multiple_of(pair * 128, 128), 128)
        out, inverse = attend(
            spread_heads(low[1, :, lanes].astype(F32), 2).astype(BF),
            ckeys.at[:, lanes],
            cvalues.at[:, lanes],
            begin,
            stop,
            scores,
            cpowers.at[pair],
        )
        cinverses[pair] = jnp.broadcast_to(inverse, (8, 2 * rows))
        heard[:, lanes] = join_heads(out, 2)
        return carry

    lax.fori_loop(0, 4, cross_forward, 0)
    after_cross = later[...] + nn(heard[...].astype(BF), weight[7]) + vector(9)
    found, spread = centred(after_cross)
    unit[1] = found
    final_spread = spread
    low[2] = (found * vector(10) + vector(11)).astype(BF)
    later[...] = after_cross + vector(12)

    cotangent = cot[...]
    unit[2] = jnp.zeros((rows, D), F32)

    def feed(c, carry):
        fed = low[2]
        first, second = weight[8 + 2 * c], weight[9 + 2 * c]
        before = nn(fed, first) + vec[pl.ds(13 + c, 1), :]
        cumulative = 0.5 * (1.0 + lax.erf(before * (2.0**-0.5)))
        after = (before * cumulative).astype(BF)
        slope = cumulative + before * jnp.exp(-0.5 * before * before) * ((2.0 * math.pi) ** -0.5)
        later[...] += nn(after, second)
        change = nt(cotangent, second) * slope
        change_low = change.astype(BF)
        dvec[pl.ds(13 + c, 1), :] = column_sum(change_low.astype(F32))
        unit[2] += nt(change_low, first)
        weight[8 + 2 * c] = tn(fed, change_low).astype(BF)
        weight[9 + 2 * c] = tn(after, cotangent).astype(BF)

        @pl.when(c == 1)
        def _():
            groups[0].begin(1)

        return carry

    lax.fori_loop(0, 4, feed, 0)
    groups[0].advance(1)
    groups[1].begin(1)
    result[...] = later[...].astype(BF)
    cot_f = cotangent.astype(F32)
    dvec[12:13, :] = column_sum(cot_f)
    dfed = unit[2]
    dvec[10:11, :] = column_sum(dfed * unit[1])
    dvec[11:12, :] = column_sum(dfed)
    dlater = cot_f + norm_back(dfed, unit[1], final_spread, vector(10))
    later[...] = dlater
    branch = dlater.astype(BF)
    dvec[9:10, :] = column_sum(branch.astype(F32))
    dheard = nt(branch, weight[7]).astype(BF)
    weight[7] = tn(heard[...].astype(BF), branch).astype(BF)
    low[2] = dheard
    heard[...] = heard[...] * dheard.astype(F32)

    def cross_backward(pair, carry):
        lanes = pl.ds(pl.multiple_of(pair * 128, 128), 128)

        def store(c, dkeys, dvalues):
            part = pl.ds(pl.multiple_of(c * dkeys.shape[0], dkeys.shape[0]), dkeys.shape[0])
            scores[part, 0:128] = dkeys
            cvalues[part, lanes] = dvalues.astype(BF)

        out = attend_back(
            spread_heads(low[1, :, lanes].astype(F32), 2).astype(BF),
            spread_heads(low[2, :, lanes].astype(F32), 2).astype(BF),
            spread_heads(heard[:, lanes], 2),
            ckeys.at[:, lanes],
            cvalues.at[:, lanes],
            cinverses[pair, 0:1, :],
            cpowers.at[pair],
            store,
        )
        ckeys[:, lanes] = scores[:, 0:128].astype(BF)
        unit[1, :, lanes] = join_heads(out, 2)

        @pl.when(pair == 0)
        def _():
            groups[1].advance(1)

        @pl.when(pair == 1)
        def _():
            groups[0].advance(2)

        @pl.when(pair == 2)
        def _():
            groups[0].advance(3)
            groups[1].advance(2)

        return carry

    lax.fori_loop(0, 4, cross_backward, 0)

    dvec[8:9, :] = column_sum(cvalues[...].astype(F32))
    block = stream[...].reshape(sources, D)
    fresh = [tn(block, ckeys[...]).astype(BF), tn(block, cvalues[...]).astype(BF)]

    def sources_back(c, carry):
        part = pl.ds(pl.multiple_of(c * step, step), step)
        back = nt(ckeys[part, :], weight[5]) + nt(cvalues[part, :], weight[6])
        stream[pl.ds(c * some, some)] = back.astype(BF).reshape(some, shalf, D)
        return carry

    lax.fori_loop(0, sources // step, sources_back, 0)
    weight[5] = fresh[0]
    weight[6] = fresh[1]

    def place_back(s, carry):
        there = pl.ds(pl.multiple_of(s * shalf, shalf), shalf)
        cvalues[there, :] = stream[sord[0, s]]
        return carry

    lax.fori_loop(0, sblocks, place_back, 0)
    memory_back.begin(1)
    groups[0].advance(4)
    groups[1].advance(3)
    ckeys[0:D, :] = weight[1]
    ckeys[D : 2 * D, :] = weight[2]

    dcq = unit[1].astype(BF)
    dvec[7:8, :] = column_sum(dcq.astype(F32)) * scale
    dcrossed = nt(dcq, weight[4]) * scale
    weight[4] = (tn(low[0], dcq) * scale).astype(BF)
    dvec[5:6, :] = column_sum(dcrossed * unit[0])
    dvec[6:7, :] = column_sum(dcrossed)
    groups[2].begin(1)
    dmid = later[...] + norm_back(dcrossed, unit[0], cross_spread, vector(5))
    later[...] = dmid
    branch = dmid.astype(BF)
    dvec[4:5, :] = column_sum(branch.astype(F32))
    dmixed = nt(branch, weight[3]).astype(BF)
    weight[3] = tn(mixed[...].astype(BF), branch).astype(BF)
    low[2] = dmixed
    mixed[...] = mixed[...] * dmixed.astype(F32)

    for b in range(2):
        for kind in range(2):
            if pad:
                cpowers[2 * kind + b, 0 : pad // PIECE, :, 0:D] = jnp.zeros((pad // PIECE, PIECE, D), BF)

        def backward(quad, carry, b=b):
            fill(b, quad)
            lanes = pl.ds(pl.multiple_of(quad * 256, 256), 256)

            def store(c, dkeys, dvalues):
                pieces = dkeys.shape[0] // PIECE
                part = pl.ds(c * pieces + pad // PIECE, pieces)
                cpowers[b, part, :, lanes] = dkeys.astype(BF).reshape(pieces, PIECE, 256)
                cpowers[2 + b, part, :, lanes] = dvalues.astype(BF).reshape(pieces, PIECE, 256)

            out = attend_back(
                spread_heads(queries[b * half : (b + 1) * half, lanes].astype(F32), 4).astype(BF),
                spread_heads(low[2, b * half : (b + 1) * half, lanes].astype(F32), 4).astype(BF),
                spread_heads(mixed[b * half : (b + 1) * half, lanes], 4),
                kwin,
                vwin,
                inverses[b * 2 + quad, 0:1, :],
                powers.at[b * 2 + quad],
                store,
            )
            unit[1, b * half : (b + 1) * half, lanes] = join_heads(out, 4)

            @pl.when(quad == 0)
            def _():
                if b == 0:
                    groups[0].advance(5)
                    groups[1].advance(4)
                    groups[2].advance(1)
                    memory_back.advance(1)
                else:
                    groups[1].advance(6)
                    memory_back.advance(2)
                    groups[2].advance(2)

            return carry

        lax.fori_loop(0, 2, backward, 0)
        if b == 0:
            groups[0].advance(6)
            groups[1].advance(5)
    for axis in (1, 2):
        pl.semaphore_signal(
            ready.at[axis - 1],
            inc=1,
            device_id={"seq": cube.other(2 * axis)},
            device_id_type=MESH,
        )
    groups[0].advance(7)
    groups[2].advance(3)

    dq = unit[1].astype(BF)
    dvec[2:3, :] = column_sum(dq.astype(F32)) * scale
    heard[...] = nt(dq, weight[0]) * scale
    own_normed = nrm[pl.ds(2 * me, 2)].reshape(rows, D)
    weight[0] = (tn(own_normed, dq) * scale).astype(BF)

    def assemble(s, carry):
        for kind in range(2):
            for third in range(thirds):
                total = jnp.zeros((PIECE, D), F32)
                for b in range(2):
                    back = base[b] - tord[0, s]
                    inside = (back >= 0) & (back < around)
                    first = jnp.clip(around - 1 - back, 0, around - 1) * thirds
                    part = cpowers[2 * kind + b, first + third][:, 0:D]
                    total = total + jnp.where(inside, part.astype(F32), 0.0)
                total_low = total.astype(BF)
                if kind == 1:
                    dvec[3:4, :] += column_sum(total_low.astype(F32))
                for quad in range(2):
                    kv[kind, quad, s, third * PIECE : (third + 1) * PIECE, :] = total_low[
                        :, quad * 256 : (quad + 1) * 256
                    ]
        return carry

    dvec[3:4, :] = jnp.zeros((1, D), F32)
    lax.fori_loop(0, blocks, assemble, 0)
    whole = nrm[...].reshape(blocks * half, D)
    for kind in range(2):
        for quad in range(2):
            weight[1 + kind, :, quad * 256 : (quad + 1) * 256] = tn(
                whole, kv[kind, quad].reshape(blocks * half, 256)
            ).astype(BF)
    groups[3].begin(1)
    memory_back.end(3)
    for part in range(2):
        dmemory[part * shalf : (part + 1) * shalf, :] = memory_back.result(part)
    groups[1].advance(7)
    groups[2].advance(4)

    def spread_back(code):
        def one(part, carry):
            s = 2 * cube.other(code) + part
            total = jnp.zeros((half, D), F32)
            for kind in range(2):
                for quad in range(2):
                    total = total + nt(
                        kv[kind, quad, s],
                        ckeys[kind * D : (kind + 1) * D, quad * 256 : (quad + 1) * 256],
                    )
            if code == 0:
                total = total + heard[pl.ds(pl.multiple_of(part * half, half), half), :]
            nrm[s] = total.astype(BF).reshape(thirds, PIECE, D)
            return carry

        lax.fori_loop(0, 2, one, 0)

    for code in (1, 3, 5, 7):
        spread_back(code)
    groups[3].advance(1)
    rows_back.begin(1)
    for code in (6, 2, 4, 0):
        spread_back(code)
    groups[2].advance(5)
    for axis in (1, 2):
        pl.semaphore_wait(ready.at[axis - 1], 1)
    rows_back.advance(1)
    groups[3].advance(2)
    rows_back.advance(2)
    groups[2].advance(6)
    groups[3].advance(3)
    rows_back.end(3)
    dvec[0:2, :] = jnp.zeros((2, D), F32)
    dvec[17:VECTORS, :] = jnp.zeros((VECTORS - 17, D), F32)
    for part in range(2):
        own_unit, own_spread = centred(own[part].reshape(half, D).astype(F32))
        dnormed = rows_back.result(part).reshape(half, D)
        here = pl.ds(part * half, half)
        dinputs[here, :] = later[here, :] + norm_back(dnormed, own_unit, own_spread, vector(0))
        dvec[0:1, :] += column_sum(dnormed * own_unit)
        dvec[1:2, :] += column_sum(dnormed)
    small.begin(1)
    groups[3].advance(4)
    groups[2].advance(7)
    small.advance(1)
    groups[3].advance(5)
    small.advance(2)
    groups[3].advance(6)
    small.advance(3)
    groups[0].end(8)
    groups[1].end(8)
    groups[2].end(8)
    copies = [
        pltpu.make_async_copy(
            weight.at[pl.ds(first, size)], grads.at[pl.ds(first, size)], sem.at[first]
        )
        for first, size in ((4, 12), (0, 4))
    ]
    copies[0].start()
    small.end(4)
    small.take(4)
    groups[3].advance(7)
    groups[3].end(8)
    copies[1].start()
    for copy in copies:
        copy.wait()


def layer_call(sizes, small_ints, own, cot, own_memory, vectors, w_small, w_in, w_out):
    rows, blocks, half, sblocks, shalf, window = (
        sizes["rows"],
        sizes["blocks"],
        sizes["half"],
        sizes["sblocks"],
        sizes["shalf"],
        sizes["window"],
    )
    sources = sblocks * shalf
    levels = sizes["levels"]
    vmem = pl.BlockSpec(memory_space=pltpu.VMEM)
    smem = pl.BlockSpec(memory_space=pltpu.SMEM)
    hbm = pl.BlockSpec(memory_space=pl.ANY)

    count = len(vectors)

    def body(*refs):
        head, rest = refs[:7], refs[7:]
        vector_refs, rest = rest[:count], rest[count:]
        layer_kernel(sizes, *head, vector_refs, rest[:8], *rest[8:])

    return pl.pallas_call(
        body,
        out_shape=(
            jax.ShapeDtypeStruct((rows, D), BF),
            jax.ShapeDtypeStruct((rows, D), F32),
            jax.ShapeDtypeStruct((2 * shalf, D), F32),
            jax.ShapeDtypeStruct((VECTORS, D), F32),
            jax.ShapeDtypeStruct((16, D, D), BF),
        ),
        in_specs=[smem] * 4 + [vmem] * (3 + count) + [hbm] * 10,
        out_specs=(vmem, vmem, vmem, vmem, hbm),
        scratch_shapes=[
            pltpu.VMEM((VECTORS, D), F32),
            pltpu.VMEM((blocks, half // PIECE, PIECE, D), BF),
            pltpu.VMEM((sblocks, shalf, D), BF),
            pltpu.VMEM((sblocks, shalf, D), BF),
            pltpu.VMEM((16, D, D), BF),
            pltpu.VMEM((2, 2, blocks, half, 256), BF),
            pltpu.VMEM((rows, D), BF),
            pltpu.VMEM((sources, D), BF),
            pltpu.VMEM((sources, D), BF),
            pltpu.VMEM((sources, 2 * rows), F32),
            pltpu.VMEM((4, window // PIECE, PIECE, 4 * half), BF),
            pltpu.VMEM((4, sources // PIECE, PIECE, 2 * rows), BF),
            pltpu.VMEM((4, 8, 4 * half), F32),
            pltpu.VMEM((4, 8, 2 * rows), F32),
            pltpu.VMEM((rows, D), F32),
            pltpu.VMEM((rows, D), F32),
            pltpu.VMEM((3, rows, D), F32),
            pltpu.VMEM((3, rows, D), BF),
            pltpu.SMEM((blocks,), jnp.int32),
            pltpu.SMEM((sblocks,), jnp.int32),
            pltpu.VMEM((2, 4, D // 2, D), BF),
            pltpu.VMEM((2, 2, 4, D // 8, D), BF),
            pltpu.VMEM((2, 2, 4, D // 16, D), BF),
            pltpu.VMEM((2, levels - 1, 2, D // 16, D), BF),
            pltpu.VMEM((2, levels - 1, 2, D // 16, D), BF),
            pltpu.VMEM((3, VECTORS, D), F32),
            pltpu.VMEM((levels, VECTORS, D), F32),
            pltpu.SemaphoreType.DMA((16,)),
            pltpu.SemaphoreType.DMA((2, 16)),
            pltpu.SemaphoreType.DMA((2, 16)),
            pltpu.SemaphoreType.DMA((4, 22)),
            pltpu.SemaphoreType.DMA((4, 22)),
            pltpu.SemaphoreType.REGULAR((4, 3)),
            pltpu.SemaphoreType.DMA((2, 14)),
            pltpu.SemaphoreType.DMA((2, 14)),
            pltpu.SemaphoreType.DMA((6,)),
            pltpu.SemaphoreType.DMA((6,)),
            pltpu.SemaphoreType.REGULAR((2,)),
        ],
        compiler_params=pltpu.CompilerParams(
            vmem_limit_bytes=64 << 20, collective_id=0, has_side_effects=True
        ),
    )(*small_ints, own, cot, own_memory, *vectors, *w_small, w_in, w_out)


def fused_on_device(
    inputs, memory, target_lengths, source_lengths, target_order, source_order,
    self_gain, self_shift, self_query, query_bias, self_key, self_value, value_bias,
    self_output, output_bias, cross_gain, cross_shift, cross_query, cquery_bias, cross_key,
    cross_value, cvalue_bias, cross_output, coutput_bias, final_gain, final_shift,
    inner_weight, inner_bias, outer_weight, outer_bias, cotangent,
):
    rows = inputs.shape[1]
    blocks = target_order.shape[1]
    sblocks = source_order.shape[1]
    ranks = lax.axis_size("seq")
    half = ranks * rows // blocks
    shalf = ranks * memory.shape[1] // sblocks
    ndoc = target_lengths.shape[1]
    reach = max(LONGEST, blocks * half - LONGEST - SHORTEST * (ndoc - 1))
    window = -(-(reach - 1 + half) // CHUNK) * CHUNK
    sizes = dict(
        rows=rows, blocks=blocks, half=half, sblocks=sblocks, shalf=shalf, ndoc=ndoc, window=window,
        levels=lax.axis_size("batch"),
    )
    result, dinputs, dmemory, dvec, grads = layer_call(
        sizes, (target_lengths, source_lengths, target_order, source_order),
        inputs.reshape(2, half // PIECE, PIECE, D), cotangent[0], memory.reshape(2, shalf, D),
        (
            self_gain, self_shift, query_bias, value_bias, output_bias, cross_gain, cross_shift,
            cquery_bias, cvalue_bias, coutput_bias, final_gain, final_shift, outer_bias, inner_bias,
        ),
        (self_query, self_key, self_value, self_output, cross_query, cross_key, cross_value, cross_output),
        inner_weight, outer_weight,
    )
    made = publish(grads, dvec, (result, dinputs, dmemory))
    result, dinputs, dmemory = made[24:]
    squares, wide, tall, rows_of, units = made[:8], made[8], made[9], made[10:23], made[23]
    return (
        result[None], dinputs[None], dmemory[None],
        rows_of[0], rows_of[1], squares[0], rows_of[2], squares[1], squares[2], rows_of[3],
        squares[3], rows_of[4], rows_of[5], rows_of[6], squares[4], rows_of[7], squares[5],
        squares[6], rows_of[8], squares[7], rows_of[9], rows_of[10], rows_of[11],
        wide, units, tall, rows_of[12],
    )


def solution(mesh):
    in_specs = (
        P("batch", "seq", None),
        P("batch", "seq", None),
        P("batch", None),
        P("batch", None),
        P("batch", None),
        P("batch", None),
        P(),
        P(),
        P(),
        P(),
        P(),
        P(),
        P(),
        P(),
        P(),
        P(),
        P(),
        P(),
        P(),
        P(),
        P(),
        P(),
        P(),
        P(),
        P(),
        P(),
        P(),
        P(),
        P(),
        P(),
        P("batch", "seq", None),
    )
    out_specs = (
        P("batch", "seq", None),
        P("batch", "seq", None),
        P("batch", "seq", None),
        P(),
        P(),
        P(),
        P(),
        P(),
        P(),
        P(),
        P(),
        P(),
        P(),
        P(),
        P(),
        P(),
        P(),
        P(),
        P(),
        P(),
        P(),
        P(),
        P(),
        P(),
        P(),
        P(),
        P(),
    )
    return jax.shard_map(
        fused_on_device if (mesh.shape["seq"], mesh.shape["batch"]) == (8, 4) else on_device,
        mesh=mesh, in_specs=in_specs, out_specs=out_specs, check_vma=False,
    )
```

```python
import math

import jax
import jax.numpy as jnp
from jax import lax
from jax.experimental import pallas as pl
from jax.experimental.pallas import tpu as pltpu
from jax.sharding import PartitionSpec as P

D = 512
HEADS = 8


EPSILON = 1e-05
NEGATIVE = -1e30


def norm(values, gain, shift):
    center = values - jnp.mean(values, axis=-1, keepdims=True)
    spread = jnp.mean(center * center, axis=-1, keepdims=True)
    return center * lax.rsqrt(spread + EPSILON) * gain + shift


def product(left, right):
    return jnp.dot(left, right, preferred_element_type=jnp.float32)


def weight_grad(left, right):
    return jnp.einsum("ti,to->io", left, right, preferred_element_type=jnp.float32)


def input_grad(grad, weight):
    return jnp.einsum("to,io->ti", grad, weight, preferred_element_type=jnp.float32)


def split_heads(values):
    return values.reshape(values.shape[0], HEADS, -1)


def locate(order, lengths, blocksize, start, count):
    index = start + jnp.arange(count, dtype=jnp.int32)
    slot = index // blocksize
    picked = jnp.sum(
        jnp.where(
            slot[:, None] == jnp.arange(order.shape[0], dtype=jnp.int32)[None, :], order[None, :], 0
        ),
        axis=1,
    )
    position = picked * blocksize + index % blocksize
    ends = jnp.cumsum(lengths)
    document = jnp.sum((position[:, None] >= ends[None, :]).astype(jnp.int32), axis=1)
    return (document, position)


def visible(query_doc, query_pos, key_doc, key_pos, causal):
    same = query_doc[:, None] == key_doc[None, :]
    if causal:
        return same & (key_pos[None, :] <= query_pos[:, None])
    return same


def opening(rows):
    return (
        jnp.zeros((rows, HEADS, D // HEADS), jnp.float32),
        jnp.full((rows, HEADS), NEGATIVE, jnp.float32),
        jnp.zeros((rows, HEADS), jnp.float32),
    )


def online(carry, query_heads, piece_keys, piece_values, allowed):
    weighted, highest, total = carry
    scores = jnp.einsum(
        "qhd,khd->qhk", query_heads, split_heads(piece_keys), preferred_element_type=jnp.float32
    )
    allowed = allowed[:, None, :]
    raised = jnp.maximum(highest, jnp.max(jnp.where(allowed, scores, NEGATIVE), axis=-1))
    powers = jnp.exp(jnp.where(allowed, scores - raised[..., None], NEGATIVE))
    total = jnp.sum(powers, axis=-1)
    weighted = jnp.einsum(
        "qhk,khd->qhd",
        powers.astype(jnp.bfloat16),
        split_heads(piece_values),
        preferred_element_type=jnp.float32,
    )
    return (weighted, raised, total)


def finish(carry):
    weighted, highest, total = carry
    return (highest + jnp.log(total), (weighted / total[..., None]).reshape(weighted.shape[0], D))


def block_back(query_heads, grad_heads, log_total, delta, piece_keys, piece_values, allowed):
    key_heads = split_heads(piece_keys)
    value_heads = split_heads(piece_values)
    scores = jnp.einsum("qhd,khd->qhk", query_heads, key_heads, preferred_element_type=jnp.float32)
    weights = jnp.exp(jnp.where(allowed[:, None, :], scores - log_total[..., None], NEGATIVE))
    grad_weights = jnp.einsum(
        "qhd,khd->qhk", grad_heads, value_heads, preferred_element_type=jnp.float32
    )
    grad_scores = (weights * (grad_weights - delta[..., None])).astype(jnp.bfloat16)
    grad_values = jnp.einsum(
        "qhk,qhd->khd", weights.astype(jnp.bfloat16), grad_heads, preferred_element_type=jnp.float32
    )
    grad_keys = jnp.einsum(
        "qhk,qhd->khd", grad_scores, query_heads, preferred_element_type=jnp.float32
    )
    grad_query = jnp.einsum(
        "qhk,khd->qhd", grad_scores, key_heads, preferred_element_type=jnp.float32
    )
    return (grad_query, grad_keys, grad_values)


def scan_back(
    query_heads,
    grad_heads,
    log_total,
    delta,
    all_keys,
    all_values,
    row_doc,
    row_pos,
    order,
    lengths,
    blocksize,
    causal,
):
    total_keys = all_keys.shape[0]
    width = math.gcd(total_keys, 512)
    count = total_keys // width

    def step(grad_query, item):
        block_keys, block_values, number = item
        key_doc, key_pos = locate(order, lengths, blocksize, number * width, width)
        allowed = visible(row_doc, row_pos, key_doc, key_pos, causal)
        query_term, key_term, value_term = block_back(
            query_heads, grad_heads, log_total, delta, block_keys, block_values, allowed
        )
        return (grad_query + query_term, (key_term, value_term))

    grad_query, (grad_keys, grad_values) = lax.scan(
        step,
        jnp.zeros(query_heads.shape, jnp.float32),
        (
            all_keys.reshape(count, width, D),
            all_values.reshape(count, width, D),
            jnp.arange(count, dtype=jnp.int32),
        ),
    )
    return (grad_query, grad_keys.reshape(total_keys, D), grad_values.reshape(total_keys, D))


def on_device(
    inputs,
    memory,
    target_lengths,
    source_lengths,
    target_order,
    source_order,
    self_gain,
    self_shift,
    self_query,
    query_bias,
    self_key,
    self_value,
    value_bias,
    self_output,
    output_bias,
    cross_gain,
    cross_shift,
    cross_query,
    cquery_bias,
    cross_key,
    cross_value,
    cvalue_bias,
    cross_output,
    coutput_bias,
    final_gain,
    final_shift,
    inner_weight,
    inner_bias,
    outer_weight,
    outer_bias,
    cotangent,
):
    rows = inputs.shape[1]
    sources = memory.shape[1]
    target_half = rows // 2
    source_half = sources // 2
    own_lengths = target_lengths[0]
    memory_lengths = source_lengths[0]
    own_order = target_order[0]
    memory_order = source_order[0]
    scale = float(D // HEADS) ** (-0.5)
    place = lax.axis_index("seq")
    row_doc, row_pos = locate(own_order, own_lengths, target_half, place * rows, rows)
    inputs_f = inputs[0].astype(jnp.float32)
    encoded = memory[0]
    normed, norm_back = jax.vjp(
        norm, inputs_f, self_gain.astype(jnp.float32), self_shift.astype(jnp.float32)
    )
    normed_low = normed.astype(jnp.bfloat16)
    queries = ((product(normed_low, self_query) + query_bias) * scale).astype(jnp.bfloat16)
    keys = product(normed_low, self_key).astype(jnp.bfloat16)
    values = (product(normed_low, self_value) + value_bias).astype(jnp.bfloat16)
    query_heads = split_heads(queries)
    piece = (
        lax.all_gather(keys, "seq", axis=0, tiled=True),
        lax.all_gather(values, "seq", axis=0, tiled=True),
    )
    key_doc, key_pos = locate(own_order, own_lengths, target_half, jnp.int32(0), piece[0].shape[0])
    self_carry = online(
        opening(rows),
        query_heads,
        piece[0],
        piece[1],
        visible(row_doc, row_pos, key_doc, key_pos, True),
    )
    self_total, mixed = finish(self_carry)
    mixed_low = mixed.astype(jnp.bfloat16)
    middle = inputs_f + product(mixed_low, self_output) + output_bias
    crossed, cross_back = jax.vjp(
        norm, middle, cross_gain.astype(jnp.float32), cross_shift.astype(jnp.float32)
    )
    crossed_low = crossed.astype(jnp.bfloat16)
    cqueries = ((product(crossed_low, cross_query) + cquery_bias) * scale).astype(jnp.bfloat16)
    ckeys = product(encoded, cross_key).astype(jnp.bfloat16)
    cvalues = (product(encoded, cross_value) + cvalue_bias).astype(jnp.bfloat16)
    cquery_heads = split_heads(cqueries)
    piece = (
        lax.all_gather(ckeys, "seq", axis=0, tiled=True),
        lax.all_gather(cvalues, "seq", axis=0, tiled=True),
    )
    key_doc, key_pos = locate(
        memory_order, memory_lengths, source_half, jnp.int32(0), piece[0].shape[0]
    )
    cross_carry = online(
        opening(rows),
        cquery_heads,
        piece[0],
        piece[1],
        visible(row_doc, row_pos, key_doc, key_pos, False),
    )
    cross_total, heard = finish(cross_carry)
    heard_low = heard.astype(jnp.bfloat16)
    later = middle + product(heard_low, cross_output) + coutput_bias
    fed, final_back = jax.vjp(
        norm, later, final_gain.astype(jnp.float32), final_shift.astype(jnp.float32)
    )
    fed_low = fed.astype(jnp.bfloat16)
    before = product(fed_low, inner_weight) + inner_bias
    after, gelu_back = jax.vjp(lambda entry: jax.nn.gelu(entry, approximate=False), before)
    after_low = after.astype(jnp.bfloat16)
    result = later + product(after_low, outer_weight) + outer_bias
    grad_out = cotangent[0]
    outer_weight_grad = weight_grad(after_low, grad_out)
    outer_bias_grad = jnp.sum(grad_out.astype(jnp.float32), axis=0)
    grad_after = input_grad(grad_out, outer_weight)
    grad_before = gelu_back(grad_after)[0].astype(jnp.bfloat16)
    inner_weight_grad = weight_grad(fed_low, grad_before)
    inner_bias_grad = jnp.sum(grad_before.astype(jnp.float32), axis=0)
    grad_fed = input_grad(grad_before, inner_weight)
    grad_later_norm, final_gain_grad, final_shift_grad = final_back(grad_fed)
    grad_later = cotangent[0].astype(jnp.float32) + grad_later_norm
    grad_cbranch = grad_later.astype(jnp.bfloat16)
    cross_output_grad = weight_grad(heard_low, grad_cbranch)
    coutput_bias_grad = jnp.sum(grad_cbranch.astype(jnp.float32), axis=0)
    grad_heard = input_grad(grad_cbranch, cross_output).astype(jnp.bfloat16)
    grad_heard_heads = split_heads(grad_heard)
    cross_delta = jnp.sum(grad_heard_heads.astype(jnp.float32) * split_heads(heard), axis=-1)
    all_ckeys, all_cvalues = (
        lax.all_gather(ckeys, "seq", axis=0, tiled=True),
        lax.all_gather(cvalues, "seq", axis=0, tiled=True),
    )
    grad_cq, part_ckeys, part_cvalues = scan_back(
        cquery_heads,
        grad_heard_heads,
        cross_total,
        cross_delta,
        all_ckeys,
        all_cvalues,
        row_doc,
        row_pos,
        memory_order,
        memory_lengths,
        source_half,
        False,
    )
    own_ckeys, own_cvalues = (
        lax.psum_scatter(
            part_ckeys.astype(jnp.bfloat16), "seq", scatter_dimension=0, tiled=True
        ).astype(jnp.float32),
        lax.psum_scatter(
            part_cvalues.astype(jnp.bfloat16), "seq", scatter_dimension=0, tiled=True
        ).astype(jnp.float32),
    )
    own_ckeys_low = own_ckeys.astype(jnp.bfloat16)
    own_cvalues_low = own_cvalues.astype(jnp.bfloat16)
    cross_key_grad = weight_grad(encoded, own_ckeys_low)
    cross_value_grad = weight_grad(encoded, own_cvalues_low)
    cvalue_bias_grad = jnp.sum(own_cvalues_low.astype(jnp.float32), axis=0)
    memory_grad = input_grad(own_ckeys_low, cross_key) + input_grad(own_cvalues_low, cross_value)
    grad_cq_low = grad_cq.reshape(rows, D).astype(jnp.bfloat16)
    cross_query_grad = weight_grad(crossed_low, grad_cq_low) * scale
    cquery_bias_grad = jnp.sum(grad_cq_low.astype(jnp.float32), axis=0) * scale
    grad_crossed = input_grad(grad_cq_low, cross_query) * scale
    grad_middle_norm, cross_gain_grad, cross_shift_grad = cross_back(grad_crossed)
    grad_middle = grad_later + grad_middle_norm
    grad_sbranch = grad_middle.astype(jnp.bfloat16)
    self_output_grad = weight_grad(mixed_low, grad_sbranch)
    output_bias_grad = jnp.sum(grad_sbranch.astype(jnp.float32), axis=0)
    grad_mixed = input_grad(grad_sbranch, self_output).astype(jnp.bfloat16)
    grad_mixed_heads = split_heads(grad_mixed)
    self_delta = jnp.sum(grad_mixed_heads.astype(jnp.float32) * split_heads(mixed), axis=-1)
    all_keys, all_values = (
        lax.all_gather(keys, "seq", axis=0, tiled=True),
        lax.all_gather(values, "seq", axis=0, tiled=True),
    )
    grad_q, part_keys, part_values = scan_back(
        query_heads,
        grad_mixed_heads,
        self_total,
        self_delta,
        all_keys,
        all_values,
        row_doc,
        row_pos,
        own_order,
        own_lengths,
        target_half,
        True,
    )
    own_keys, own_values = (
        lax.psum_scatter(
            part_keys.astype(jnp.bfloat16), "seq", scatter_dimension=0, tiled=True
        ).astype(jnp.float32),
        lax.psum_scatter(
            part_values.astype(jnp.bfloat16), "seq", scatter_dimension=0, tiled=True
        ).astype(jnp.float32),
    )
    own_keys_low = own_keys.astype(jnp.bfloat16)
    own_values_low = own_values.astype(jnp.bfloat16)
    self_key_grad = weight_grad(normed_low, own_keys_low)
    self_value_grad = weight_grad(normed_low, own_values_low)
    value_bias_grad = jnp.sum(own_values_low.astype(jnp.float32), axis=0)
    grad_q_low = grad_q.reshape(rows, D).astype(jnp.bfloat16)
    self_query_grad = weight_grad(normed_low, grad_q_low) * scale
    query_bias_grad = jnp.sum(grad_q_low.astype(jnp.float32), axis=0) * scale
    grad_normed = (
        input_grad(grad_q_low, self_query) * scale
        + input_grad(own_keys_low, self_key)
        + input_grad(own_values_low, self_value)
    )
    grad_in_norm, self_gain_grad, self_shift_grad = norm_back(grad_normed)
    inputs_grad = grad_middle + grad_in_norm
    summed = lax.psum(
        (
            self_gain_grad,
            self_shift_grad,
            self_query_grad,
            query_bias_grad,
            self_key_grad,
            self_value_grad,
            value_bias_grad,
            self_output_grad,
            output_bias_grad,
            cross_gain_grad,
            cross_shift_grad,
            cross_query_grad,
            cquery_bias_grad,
            cross_key_grad,
            cross_value_grad,
            cvalue_bias_grad,
            cross_output_grad,
            coutput_bias_grad,
            final_gain_grad,
            final_shift_grad,
            inner_weight_grad,
            inner_bias_grad,
            outer_weight_grad,
            outer_bias_grad,
        ),
        ("seq", "batch"),
    )
    return (result.astype(jnp.bfloat16)[None], inputs_grad[None], memory_grad[None]) + tuple(summed)


HDIM = D // HEADS
SHORTEST = 32
LONGEST = 1024
CHUNK = 256
PIECE = 64

SCHEDULE = dict(
    half="A",
    heard="BA",
    pair0="B",
    pair1="A",
    pair3="AB",
    sources="BV",
    middle="CA",
    self0="CM",
    self1="BMV",
    window="AC",
    self2="B",
    self3="A",
    weights="ECME",
    through0="BC",
    theirs="R",
    end="ECMREACAERBECRSESVECSBE",
)
MESH = pl.DeviceIdType.MESH
PARTS = 2
BF = jnp.bfloat16
F32 = jnp.float32
VECTORS = 24


def nn(left, right):
    return lax.dot_general(left, right, (((1,), (0,)), ((), ())), preferred_element_type=F32)


def nt(left, right):
    return lax.dot_general(left, right, (((1,), (1,)), ((), ())), preferred_element_type=F32)


def tn(left, right):
    return lax.dot_general(left, right, (((0,), (0,)), ((), ())), preferred_element_type=F32)


def centred(values):
    center = values - jnp.mean(values, axis=-1, keepdims=True)
    spread = lax.rsqrt(jnp.mean(center * center, axis=-1, keepdims=True) + EPSILON)
    return center * spread, spread


def norm_back(grad, unit, spread, gain):
    scaled = grad * gain
    return spread * (
        scaled
        - jnp.mean(scaled, axis=-1, keepdims=True)
        - unit * jnp.mean(scaled * unit, axis=-1, keepdims=True)
    )


def column_sum(values):
    return jnp.sum(values, axis=0, keepdims=True)


def spread_heads(block, heads):
    lane = lax.broadcasted_iota(jnp.int32, block.shape, 1)
    return jnp.concatenate(
        [
            jnp.where((lane >= h * HDIM) & (lane < (h + 1) * HDIM), block, 0.0)
            for h in range(heads)
        ],
        axis=0,
    )


def join_heads(stacked, heads):
    rows = stacked.shape[0] // heads
    lane = lax.broadcasted_iota(jnp.int32, (rows, stacked.shape[1]), 1)
    total = stacked[:rows]
    for h in range(1, heads):
        total = jnp.where(lane >= h * HDIM, stacked[h * rows : (h + 1) * rows], total)
    return total


def part_of(array, index, size):
    if len(array.shape) == 3:
        count = size // PIECE
        return array[pl.ds(index * count, count)].reshape(size, array.shape[2])
    return array[pl.ds(pl.multiple_of(index * size, size), size), :]


def whole_of(array):
    return array[...].reshape(-1, array.shape[-1])


def attend(queries, keys, values, low, high, scores, powers):
    total = math.prod(keys.shape[:-1])
    width = queries.shape[0]
    chunk = total // PARTS
    pieces = chunk // PIECE

    def first(c, highest):
        rows = pl.ds(pl.multiple_of(c * chunk, chunk), chunk)
        place = lax.broadcasted_iota(jnp.int32, (chunk, width), 0) + c * chunk
        found = jnp.where((place >= low) & (place < high), nt(part_of(keys, c, chunk), queries), NEGATIVE)
        scores[rows, :] = found
        return jnp.maximum(highest, jnp.max(found, axis=0, keepdims=True))

    highest = lax.fori_loop(0, total // chunk, first, jnp.full((1, width), NEGATIVE, F32))

    def second(c, summed):
        rows = pl.ds(pl.multiple_of(c * chunk, chunk), chunk)
        power = jnp.exp(scores[rows, :] - highest)
        powers[pl.ds(c * pieces, pieces)] = power.astype(BF).reshape(pieces, PIECE, width)
        return summed + column_sum(power)

    summed = lax.fori_loop(0, total // chunk, second, jnp.zeros((1, width), F32))
    inverse = 1.0 / summed
    mixed = tn(whole_of(values), powers[0 : total // PIECE].reshape(total, width)) * inverse
    return mixed.T, inverse


def attend_back(queries, grads, product_of, keys, values, inverse, powers, store):
    total = math.prod(keys.shape[:-1])
    width = queries.shape[0]
    chunk = total // PARTS
    pieces = chunk // PIECE
    ones = jnp.ones((8, queries.shape[1]), BF)
    coarse = product_of.astype(BF)
    fine = (product_of - coarse.astype(F32)).astype(BF)
    delta = (nt(ones, coarse) + nt(ones, fine))[0:1]

    def step(c, carry):
        part = pl.ds(c * pieces, pieces)
        weights = powers[part].reshape(chunk, width).astype(F32) * inverse
        weights_low = weights.astype(BF)
        change = (weights * (nt(part_of(values, c, chunk), grads) - delta)).astype(BF)
        powers[part] = change.reshape(pieces, PIECE, width)
        store(c, nn(change, queries), nn(weights_low, grads))
        return carry

    lax.fori_loop(0, total // chunk, step, 0)
    return tn(whole_of(keys), powers[0 : total // PIECE].reshape(total, width)).T


class Cube:
    def __init__(self, me, level, levels):
        self.me, self.level, self.levels = me, level, levels
        self.bits = (lax.rem(me, 2), lax.rem(lax.div(me, 2), 2), lax.div(me, 4))

    def other(self, code):
        place = self.me
        for axis in range(3):
            if code >> axis & 1:
                place = place + (1 << axis) * (1 - 2 * self.bits[axis])
        return place

    def plane(self, step):
        return lax.rem(self.level + step, self.levels)

    def greet(self):
        barrier = pltpu.get_barrier_semaphore()
        for code in range(1, 8):
            pl.semaphore_signal(
                barrier, inc=1, device_id={"seq": self.other(code)}, device_id_type=MESH
            )
        for step in range(1, self.levels):
            pl.semaphore_signal(
                barrier, inc=1, device_id={"batch": self.plane(step)}, device_id_type=MESH
            )
        pl.semaphore_wait(barrier, 6 + self.levels)

    def send(self, code, source, target, send_sem, recv_sem):
        copy = pltpu.make_async_remote_copy(
            src_ref=source,
            dst_ref=target,
            send_sem=send_sem,
            recv_sem=recv_sem,
            device_id={"seq": self.other(code)},
            device_id_type=MESH,
        )
        copy.start()
        return copy


class Steps:
    def copies(self, step):
        return [
            pltpu.make_async_remote_copy(
                src_ref=source,
                dst_ref=target,
                send_sem=self.send_sem.at[index],
                recv_sem=self.recv_sem.at[index],
                device_id=device,
                device_id_type=MESH,
            )
            for device, source, target, index in self.moves(step)
        ]

    def begin(self, step):
        for copy in self.copies(step):
            copy.start()

    def end(self, step):
        for copy in self.copies(step):
            copy.wait()

    step, last = 0, 0

    def advance(self):
        if self.step:
            self.end(self.step)
            self.take(self.step)
        self.step += 1
        if self.step <= self.last:
            self.begin(self.step)

    def take(self, step):
        pass


class Reduce(Steps):
    last = 8

    def __init__(self, cube, panels, first, pair, flat, edge, deep, leave, send_sem, recv_sem, sent, before, finish):
        self.before, self.finish, self.freed = before, finish, set()
        self.cube, self.panels, self.first = cube, panels, first
        self.pair, self.flat, self.edge, self.deep, self.leave = pair, flat, edge, deep, leave
        self.send_sem, self.recv_sem, self.sent = send_sem, recv_sem, sent

    def await_free(self, index):
        if index not in self.freed:
            self.freed.add(index)
            pl.semaphore_wait(self.sent.at[index], 1)

    def begin(self, step):
        for index in {6: (1, 2), 8: (0,)}.get(step, ()):
            self.await_free(index)
        if self.before is not None:
            for index in {1: (0,), 2: (1, 2)}.get(step, ()):
                self.before.await_free(index)
        if step == 4:
            for k in range(1, self.cube.levels):
                there = self.first + self.cube.plane(k)
                for axis in (1, 2):
                    self.leave[k - 1, axis - 1] = self.panels[there, self.rows(axis=axis, further=0), :]
        super().begin(step)

    def rows(self, core=0, axis=None, far=0, further=None):
        bits = self.cube.bits
        flip = lambda bit, other: 1 - bit if other else bit
        start, size = flip(bits[0], core) * (D // 2), D // 2
        if axis is not None:
            size = D // 8
            start = start + (axis - 1) * (D // 4) + flip(bits[axis], far) * size
            if further is not None:
                size = D // 16
                start = start + flip(bits[3 - axis], further) * size
        return pl.ds(pl.multiple_of(start, D // 16), size)

    def all(self, rows):
        return self.panels.at[pl.ds(self.first, 4), rows, :]

    def moves(self, step):
        cube = self.cube
        near = lambda code: {"seq": cube.other(code)}
        if step == 1:
            return [(near(1), self.all(self.rows(core=1)), self.pair, 0)]
        if step == 2:
            return [
                (near(2 * axis), self.all(self.rows(axis=axis, far=1)), self.flat.at[axis - 1], axis)
                for axis in (1, 2)
            ]
        if step == 3:
            return [
                (
                    near(6 - 2 * axis),
                    self.all(self.rows(axis=axis, further=1)),
                    self.edge.at[axis - 1],
                    2 + axis,
                )
                for axis in (1, 2)
            ]
        if step == 4:
            return [
                (
                    {"batch": cube.plane(k)},
                    self.leave.at[k - 1, axis - 1],
                    self.deep.at[k - 1, axis - 1],
                    3 + 2 * k + axis - 1,
                )
                for k in range(1, cube.levels)
                for axis in (1, 2)
            ]
        if step == 5:
            there = self.first + cube.level
            return [
                (
                    {"batch": cube.plane(k)},
                    self.panels.at[there, self.rows(axis=axis, further=0), :],
                    self.panels.at[there, self.rows(axis=axis, further=0), :],
                    9 + 2 * k + axis - 1,
                )
                for k in range(1, cube.levels)
                for axis in (1, 2)
            ]
        if step == 6:
            parts = [(6 - 2 * axis, self.all(self.rows(axis=axis, further=0)), 16 + axis) for axis in (1, 2)]
        elif step == 7:
            parts = [(2 * axis, self.all(self.rows(axis=axis)), 18 + axis) for axis in (1, 2)]
        else:
            parts = [(1, self.all(self.rows()), 21)]
        return [(near(code), part, part, index) for code, part, index in parts]

    def add(self, rows, found):
        def one(i, carry):
            there = self.first + i
            total = self.panels[there, rows, :].astype(F32) + found[i].astype(F32)
            self.panels[there, rows, :] = total.astype(BF)
            return carry

        lax.fori_loop(0, 4, one, 0)

    def take(self, step):
        if step == 1:
            self.add(self.rows(), self.pair)
        elif step == 2:
            for axis in (1, 2):
                self.add(self.rows(axis=axis), self.flat.at[axis - 1])
        elif step == 3:
            for axis in (1, 2):
                self.add(self.rows(axis=axis, further=0), self.edge.at[axis - 1])
        elif step == 4:
            there = self.first + self.cube.level
            for axis in (1, 2):
                rows = self.rows(axis=axis, further=0)
                total = self.panels[there, rows, :].astype(F32)
                for k in range(self.cube.levels - 1):
                    total = total + self.deep[k, axis - 1].astype(F32)
                self.panels[there, rows, :] = total.astype(BF)
        elif step == 8:
            self.finish()
        for index in {1: (0,), 3: (1, 2)}.get(step, ()):
            pl.semaphore_signal(
                self.sent.at[index],
                inc=1,
                device_id={"seq": self.cube.other(1 << index)},
                device_id_type=MESH,
            )


class Scatter(Steps):
    last = 3

    def __init__(self, cube, block, spare, send_sem, recv_sem, ready, finish):
        self.cube, self.block, self.spare = cube, block, spare
        self.ready, self.finish = ready, finish
        self.send_sem, self.recv_sem = send_sem, recv_sem

    def begin(self, step):
        if self.ready is not None:
            for index in {1: (0,), 2: (1, 2)}.get(step, ()):
                pl.semaphore_wait(self.ready.at[index], 1)
        super().begin(step)

    def at(self, code, part):
        return self.block(2 * self.cube.other(code) + part)

    def moves(self, step):
        near = lambda code: {"seq": self.cube.other(code)}
        if step == 1:
            parts = [(1, 2 * i + 1, part, 2 * i + part) for i in range(4) for part in range(2)]
        elif step == 2:
            parts = [(2, 2, 0, 8), (2, 6, 0, 9), (4, 4, 1, 10), (4, 6, 1, 11)]
        else:
            parts = [(4, 4, 0, 12), (2, 2, 1, 13)]
        return [(near(to), self.at(code, part), self.spare(k), k) for to, code, part, k in parts]

    def take(self, step):
        if step == 3:
            self.finish()
            return
        if step == 1:
            parts = [(2 * i, part, 2 * i + part) for i in range(4) for part in range(2)]
        else:
            parts = [(0, 0, 8), (4, 0, 9), (0, 1, 10), (2, 1, 11)]
        for code, part, k in parts:
            here = self.at(code, part)
            here[...] = (here[...].astype(F32) + self.spare(k)[...].astype(F32)).astype(BF)

    def result(self, part):
        return self.at(0, part)[...].astype(F32) + self.spare(12 + part)[...].astype(F32)


class Small(Steps):
    last = 2

    def __init__(self, cube, array, near, planes, send_sem, recv_sem):
        self.cube, self.array, self.near, self.planes = cube, array, near, planes
        self.send_sem, self.recv_sem = send_sem, recv_sem

    def moves(self, step):
        cube = self.cube
        if step == 1:
            here = self.near.at[cube.me]
            return [({"seq": cube.other(code)}, here, here, code - 1) for code in range(1, 8)]
        here = self.planes.at[cube.level]
        return [({"batch": cube.plane(k)}, here, here, 6 + k) for k in range(1, cube.levels)]

    def begin(self, step):
        if step == 1:
            self.near[self.cube.me] = self.array[...]
        super().begin(step)

    def take(self, step):
        found = self.near if step == 1 else self.planes
        total = found[0]
        for k in range(1, found.shape[0]):
            total = total + found[k]
        if step == 1:
            self.planes[self.cube.level] = total
        else:
            self.array[...] = total


class Gather:
    def __init__(self, cube, own, slot_ref, send_sem, recv_sem):
        self.cube, self.own, self.slot_ref = cube, own, slot_ref
        self.send_sem, self.recv_sem = send_sem, recv_sem
        self.sent = []

    def push(self, step, code, part):
        slot = 2 * self.cube.other(code) + part
        target = self.slot_ref(slot)
        source = self.own.at[part] if code == 0 else target
        self.sent.append(
            self.cube.send(
                step,
                source,
                target,
                self.send_sem.at[len(self.sent)],
                self.recv_sem.at[2 * (code ^ step) + part],
            )
        )

    def take(self, code, part):
        slot = self.slot_ref(2 * self.cube.other(code) + part)
        pltpu.make_async_remote_copy(
            src_ref=slot,
            dst_ref=slot,
            send_sem=self.send_sem.at[0],
            recv_sem=self.recv_sem.at[2 * code + part],
            device_id={"seq": self.cube.other(1)},
            device_id_type=MESH,
        ).wait_recv()

    def arrived(self, code):
        for part in range(2):
            self.take(code, part)

    def open(self):
        for step, part in ((2, 0), (4, 1), (2, 1), (4, 0), (1, 0), (1, 1)):
            self.push(step, 0, part)

    def pass_on(self):
        self.take(2, 0)
        self.push(4, 2, 0)
        self.take(4, 1)
        self.push(2, 4, 1)
        self.push(1, 2, 0)
        self.push(1, 4, 1)
        self.take(2, 1)
        self.push(1, 2, 1)
        self.take(4, 0)
        self.push(1, 4, 0)

    def finish(self):
        for part in range(2):
            self.take(6, part)
            self.push(1, 6, part)

    def close(self):
        for copy in self.sent:
            copy.wait_send()


def publish_kernel(grads, dvec, *refs):
    kept, outs, (narrow, broad, load_sem, store_sem, keep_sem) = refs[:3], refs[3:-5], refs[-5:]
    keeps = [pltpu.make_async_copy(kept[i], outs[24 + i], keep_sem.at[i]) for i in range(3)]
    order = list(range(8, 16)) + list(range(4, 8)) + list(range(4))
    loads = [pltpu.make_async_copy(grads.at[i], narrow.at[i], load_sem.at[i]) for i in order]
    for load in loads + keeps:
        load.start()
    for i in range(13):
        outs[10 + i][...] = dvec[i, :]
    for i in range(4):
        outs[23][i * D : (i + 1) * D] = dvec[13 + i, :]
    stores = []
    for load, i in zip(loads, order):
        load.wait()
        broad[i] = narrow[i].astype(F32)
        if i < 8:
            target = outs[i]
        elif i % 2 == 0:
            target = outs[8].at[:, pl.ds((i - 8) // 2 * D, D)]
        else:
            target = outs[9].at[pl.ds((i - 8) // 2 * D, D), :]
        store = pltpu.make_async_copy(broad.at[i], target, store_sem.at[i])
        store.start()
        stores.append(store)
    for store in stores + keeps:
        store.wait()


def publish(grads, dvec, kept):
    vmem = pl.BlockSpec(memory_space=pltpu.VMEM)
    hbm = pl.BlockSpec(memory_space=pl.ANY)
    shapes = [(D, D)] * 8 + [(D, 4 * D), (4 * D, D)] + [(D,)] * 13 + [(4 * D,)]
    return pl.pallas_call(
        publish_kernel,
        out_shape=tuple(
            [jax.ShapeDtypeStruct(shape, F32) for shape in shapes]
            + [jax.ShapeDtypeStruct(array.shape, array.dtype) for array in kept]
        ),
        in_specs=[hbm, vmem] + [hbm] * 3,
        out_specs=tuple([hbm] * 10 + [vmem] * 14 + [hbm] * 3),
        scratch_shapes=[
            pltpu.VMEM((16, D, D), BF),
            pltpu.VMEM((16, D, D), F32),
            pltpu.SemaphoreType.DMA((16,)),
            pltpu.SemaphoreType.DMA((16,)),
            pltpu.SemaphoreType.DMA((3,)),
        ],
        compiler_params=pltpu.CompilerParams(vmem_limit_bytes=48 << 20),
    )(grads, dvec, *kept)


def layer_kernel(
    sizes,
    tlen,
    slen,
    tord,
    sord,
    own,
    cot,
    own_memory,
    vectors,
    w_small,
    w_in,
    w_out,
    result,
    dinputs,
    dmemory,
    dvec,
    grads,
    vec,
    nrm,
    memory,
    stream,
    weight,
    kv,
    queries,
    ckeys,
    cvalues,
    scores,
    powers,
    cpowers,
    inverses,
    cinverses,
    mixed,
    heard,
    unit,
    low,
    tinv,
    sinv,
    pairs,
    flats,
    edges,
    deeps,
    leaves,
    nears,
    planes,
    sem,
    send_sem,
    recv_sem,
    group_send,
    group_recv,
    group_sent,
    scatter_send,
    scatter_recv,
    small_send,
    small_recv,
    ready,
):
    rows, blocks, half, sblocks, shalf, ndoc, window = (
        sizes["rows"],
        sizes["blocks"],
        sizes["half"],
        sizes["sblocks"],
        sizes["shalf"],
        sizes["ndoc"],
        sizes["window"],
    )
    around = -(-window // half)
    pad = around * half - window
    sources = sblocks * shalf
    later = dinputs
    me = lax.axis_index("seq")
    scale = float(HDIM) ** -0.5
    thirds = half // PIECE
    cube = Cube(me, lax.axis_index("batch"), sizes["levels"])
    cube.greet()

    def raw(slot):
        return powers.at[lax.rem(slot, 4), pl.ds(lax.div(slot, 4) * thirds, thirds), :, 0:D]

    def raw_memory(slot):
        return memory.at[slot]

    gather_rows = Gather(cube, own, raw, send_sem.at[0], recv_sem.at[0])
    gather_sources = Gather(cube, own_memory, raw_memory, send_sem.at[1], recv_sem.at[1])
    gather_rows.open()
    def deliver(turn, first):
        def go():
            pltpu.make_async_copy(
                weight.at[pl.ds(first, 4)], grads.at[pl.ds(first, 4)], sem.at[turn]
            ).start()

        return go

    groups = []
    for turn, first in enumerate((8, 12, 4, 0)):
        groups.append(
            Reduce(
                cube, weight, first, pairs.at[turn % 2], flats.at[turn % 2], edges.at[turn % 2],
                deeps.at[turn % 2], leaves.at[turn % 2], group_send.at[turn], group_recv.at[turn],
                group_sent.at[turn], groups[turn - 2] if turn > 1 else None, deliver(turn, first),
            )
        )

    def spare_block(k):
        return powers.at[k % 4, pl.ds(k // 4 * thirds, thirds), :, 0:D]

    def end_rows():
        for part in range(2):
            own_unit, own_spread = centred(own[part].reshape(half, D).astype(F32))
            dnormed = rows_back.result(part).reshape(half, D)
            here = pl.ds(part * half, half)
            dinputs[here, :] = later[here, :] + norm_back(dnormed, own_unit, own_spread, vector(0))
            dvec[0:1, :] += column_sum(dnormed * own_unit)
            dvec[1:2, :] += column_sum(dnormed)

    def end_memory():
        for part in range(2):
            dmemory[part * shalf : (part + 1) * shalf, :] = memory_back.result(part)

    rows_back = Scatter(
        cube, lambda slot: nrm.at[slot], spare_block, scatter_send.at[0], scatter_recv.at[0],
        ready, end_rows,
    )
    memory_back = Scatter(
        cube,
        lambda slot: cvalues.at[pl.ds(pl.multiple_of(slot * shalf, shalf), shalf), :],
        lambda k: memory.at[k],
        scatter_send.at[1],
        scatter_recv.at[1],
        None,
        end_memory,
    )
    smalls = [
        Small(
            cube, dvec.at[pl.ds(start, 8 * size), :],
            nears.at[:, pl.ds(start, 8 * size), :], planes.at[:, pl.ds(start, 8 * size), :],
            small_send.at[turn], small_recv.at[turn],
        )
        for turn, (start, size) in enumerate(((0, 1), (8, 2)))
    ]
    exchanges = dict(
        A=groups[0], B=groups[1], C=groups[2], E=groups[3], R=rows_back, M=memory_back,
        S=smalls[0], V=smalls[1],
    )
    counts = dict(A=9, B=9, C=9, E=9, R=4, M=4, S=3, V=3)

    def pump(point):
        for name in SCHEDULE.get(point, ""):
            counts[name] -= 1
            exchanges[name].advance()

    dvec[...] = jnp.zeros((VECTORS, D), F32)
    row = 0
    for vector_ref in vectors:
        for start in range(0, vector_ref.shape[0], D):
            vec[row : row + 1, :] = vector_ref[start : start + D].astype(F32).reshape(1, D)
            row += 1

    copies = []
    for index, (source, target) in enumerate(
        [(w_small[i], weight.at[i]) for i in range(8)]
        + [(w_in.at[:, pl.ds(D * i, D)], weight.at[8 + 2 * i]) for i in range(4)]
        + [(w_out.at[pl.ds(D * i, D), :], weight.at[9 + 2 * i]) for i in range(4)]
    ):
        copy = pltpu.make_async_copy(source, target, sem.at[index])
        copy.start()
        copies.append(copy)

    for order, inverse_of, count in ((tord, tinv, blocks), (sord, sinv, sblocks)):
        for t in range(count):
            found = jnp.int32(0)
            for s in range(count):
                found = jnp.where(order[0, s] == t, s, found)
            inverse_of[t] = found
    tends, sends = [], []
    tend, send = jnp.int32(0), jnp.int32(0)
    for d in range(ndoc):
        tend, send = tend + tlen[0, d], send + slen[0, d]
        tends.append(tend)
        sends.append(send)
    base = [tord[0, 2 * me + b] for b in range(2)]

    def vector(index):
        return vec[index : index + 1, :]

    for copy in copies:
        copy.wait()

    states = own[...].reshape(rows, D)
    own_normed = (centred(states.astype(F32))[0] * vector(0) + vector(1)).astype(BF)
    queries[...] = ((nn(own_normed, weight[0]) + vector(2)) * scale).astype(BF)

    def project_block(s, block):
        found, _ = centred(block.astype(F32))
        normed = (found * vector(0) + vector(1)).astype(BF)
        nrm[s] = normed.reshape(thirds, PIECE, D)
        keys = nn(normed, weight[1]).astype(BF)
        values = (nn(normed, weight[2]) + vector(3)).astype(BF)
        for quad in range(2):
            kv[0, quad, s] = keys[:, quad * 256 : (quad + 1) * 256]
            kv[1, quad, s] = values[:, quad * 256 : (quad + 1) * 256]

    def project(code):
        def one(part, carry):
            s = 2 * cube.other(code) + part
            project_block(s, raw(s)[...].reshape(half, D))
            return carry

        lax.fori_loop(0, 2, one, 0)

    for part in range(2):
        project_block(2 * me + part, own[part].reshape(half, D))
    gather_rows.arrived(1)
    project(1)
    gather_rows.pass_on()
    gather_sources.open()
    project(2)
    project(4)
    gather_rows.arrived(3)
    project(3)
    gather_rows.arrived(5)
    project(5)
    gather_rows.finish()
    project(6)
    gather_rows.arrived(7)
    project(7)
    gather_rows.close()
    gather_sources.pass_on()

    def limits(b):
        index = lax.broadcasted_iota(jnp.int32, (1, 4 * half), 1)
        row = index
        for h in range(1, 4):
            row = jnp.where(index >= h * half, index - h * half, row)
        position = base[b] * half + row
        start = jnp.zeros_like(position)
        for end in tends:
            start = jnp.where(position >= end, end, start)
        shift = (base[b] + 1) * half - window
        return start - shift, position - shift + 1

    kwin, vwin = [
        cpowers.at[kind, pl.ds(0, window // PIECE), :, pl.ds(D, 4 * HDIM)] for kind in range(2)
    ]

    def fill(b, quad):
        skip = pad // PIECE
        for j in range(around):
            slot = tinv[jnp.maximum(base[b] - (around - 1) + j, 0)]
            for kind, target in ((0, kwin), (1, vwin)):
                block = kv[kind, quad, slot].reshape(thirds, PIECE, 4 * HDIM)
                if j == 0:
                    target[0 : thirds - skip] = block[skip:]
                else:
                    target[j * thirds - skip : (j + 1) * thirds - skip] = block

    for b in range(2):
        begin, stop = limits(b)

        def forward(quad, carry, b=b, begin=begin, stop=stop):
            fill(b, quad)
            lanes = pl.ds(pl.multiple_of(quad * 256, 256), 256)
            block = queries[b * half : (b + 1) * half, lanes].astype(F32)
            out, inverse = attend(
                spread_heads(block, 4).astype(BF),
                kwin,
                vwin,
                begin,
                stop,
                scores.at[pl.ds(0, window), :],
                powers.at[b * 2 + quad],
            )
            inverses[b * 2 + quad] = jnp.broadcast_to(inverse, (8, 4 * half))
            mixed[b * half : (b + 1) * half, lanes] = join_heads(out, 4)
            return carry

        lax.fori_loop(0, 2, forward, 0)

    middle = own[...].reshape(rows, D).astype(F32) + nn(mixed[...].astype(BF), weight[3]) + vector(4)
    found, spread = centred(middle)
    later[...] = middle
    unit[0] = found
    low[0] = (found * vector(5) + vector(6)).astype(BF)
    cross_spread = spread
    low[1] = ((nn(low[0], weight[4]) + vector(7)) * scale).astype(BF)

    gather_sources.finish()
    for code in (1, 3, 5, 7):
        gather_sources.arrived(code)
    for part in range(2):
        memory[2 * me + part] = own_memory[part]
    gather_sources.close()

    def place(t, carry):
        stream[t] = memory[sinv[t]]
        return carry

    lax.fori_loop(0, sblocks, place, 0)
    step = sources // 2
    some = sblocks // 2

    def sources_of(c, carry):
        part = pl.ds(pl.multiple_of(c * step, step), step)
        block = stream[pl.ds(c * some, some)].reshape(step, D)
        ckeys[part, :] = nn(block, weight[5]).astype(BF)
        cvalues[part, :] = (nn(block, weight[6]) + vector(8)).astype(BF)
        return carry

    lax.fori_loop(0, sources // step, sources_of, 0)
    index = lax.broadcasted_iota(jnp.int32, (1, 2 * rows), 1)
    row = jnp.where(index >= rows, index - rows, index)
    position = jnp.where(row >= half, base[1] * half + row - half, base[0] * half + row)
    begin = jnp.zeros_like(position)
    stop = jnp.full_like(position, sources)
    for end, send in zip(tends, sends):
        begin = jnp.where(position >= end, send, begin)
    for end, send in reversed(list(zip(tends, sends))):
        stop = jnp.where(position < end, send, stop)

    def cross_forward(pair, carry):
        lanes = pl.ds(pl.multiple_of(pair * 128, 128), 128)
        out, inverse = attend(
            spread_heads(low[1, :, lanes].astype(F32), 2).astype(BF),
            ckeys.at[:, lanes],
            cvalues.at[:, lanes],
            begin,
            stop,
            scores,
            cpowers.at[pair],
        )
        cinverses[pair] = jnp.broadcast_to(inverse, (8, 2 * rows))
        heard[:, lanes] = join_heads(out, 2)
        return carry

    lax.fori_loop(0, 4, cross_forward, 0)
    after_cross = later[...] + nn(heard[...].astype(BF), weight[7]) + vector(9)
    found, spread = centred(after_cross)
    unit[1] = found
    final_spread = spread
    low[2] = (found * vector(10) + vector(11)).astype(BF)
    later[...] = after_cross + vector(12)

    cotangent = cot[...]
    unit[2] = jnp.zeros((rows, D), F32)

    def feed(c, carry):
        fed = low[2]
        first, second = weight[8 + 2 * c], weight[9 + 2 * c]
        before = nn(fed, first) + vec[pl.ds(13 + c, 1), :]
        cumulative = 0.5 * (1.0 + lax.erf(before * (2.0**-0.5)))
        after = (before * cumulative).astype(BF)
        slope = cumulative + before * jnp.exp(-0.5 * before * before) * ((2.0 * math.pi) ** -0.5)
        later[...] += nn(after, second)
        change = nt(cotangent, second) * slope
        change_low = change.astype(BF)
        dvec[pl.ds(13 + c, 1), :] = column_sum(change_low.astype(F32))
        unit[2] += nt(change_low, first)
        weight[8 + 2 * c] = tn(fed, change_low).astype(BF)
        weight[9 + 2 * c] = tn(after, cotangent).astype(BF)

        @pl.when(c == 1)
        def _():
            pump("half")

        return carry

    lax.fori_loop(0, 4, feed, 0)
    pump("feed")
    result[...] = later[...].astype(BF)
    cot_f = cotangent.astype(F32)
    dvec[12:13, :] = column_sum(cot_f)
    dfed = unit[2]
    dvec[10:11, :] = column_sum(dfed * unit[1])
    dvec[11:12, :] = column_sum(dfed)
    dlater = cot_f + norm_back(dfed, unit[1], final_spread, vector(10))
    later[...] = dlater
    branch = dlater.astype(BF)
    dvec[9:10, :] = column_sum(branch.astype(F32))
    dheard = nt(branch, weight[7]).astype(BF)
    weight[7] = tn(heard[...].astype(BF), branch).astype(BF)
    low[2] = dheard
    heard[...] = heard[...] * dheard.astype(F32)
    pump("heard")

    def cross_backward(pair, carry):
        lanes = pl.ds(pl.multiple_of(pair * 128, 128), 128)

        def store(c, dkeys, dvalues):
            part = pl.ds(pl.multiple_of(c * dkeys.shape[0], dkeys.shape[0]), dkeys.shape[0])
            scores[part, 0:128] = dkeys
            cvalues[part, lanes] = dvalues.astype(BF)

        out = attend_back(
            spread_heads(low[1, :, lanes].astype(F32), 2).astype(BF),
            spread_heads(low[2, :, lanes].astype(F32), 2).astype(BF),
            spread_heads(heard[:, lanes], 2),
            ckeys.at[:, lanes],
            cvalues.at[:, lanes],
            cinverses[pair, 0:1, :],
            cpowers.at[pair],
            store,
        )
        ckeys[:, lanes] = scores[:, 0:128].astype(BF)
        unit[1, :, lanes] = join_heads(out, 2)

        for index in range(4):

            @pl.when(pair == index)
            def _(index=index):
                pump("pair" + str(index))

        return carry

    lax.fori_loop(0, 4, cross_backward, 0)

    dvec[8:9, :] = column_sum(cvalues[...].astype(F32))
    block = stream[...].reshape(sources, D)
    fresh = [tn(block, ckeys[...]).astype(BF), tn(block, cvalues[...]).astype(BF)]

    pump("sums")

    def sources_back(c, carry):
        part = pl.ds(pl.multiple_of(c * step, step), step)
        back = nt(ckeys[part, :], weight[5]) + nt(cvalues[part, :], weight[6])
        stream[pl.ds(c * some, some)] = back.astype(BF).reshape(some, shalf, D)
        return carry

    lax.fori_loop(0, sources // step, sources_back, 0)
    weight[5] = fresh[0]
    weight[6] = fresh[1]

    def place_back(s, carry):
        there = pl.ds(pl.multiple_of(s * shalf, shalf), shalf)
        cvalues[there, :] = stream[sord[0, s]]
        return carry

    lax.fori_loop(0, sblocks, place_back, 0)
    pump("sources")
    ckeys[0:D, :] = weight[1]
    ckeys[D : 2 * D, :] = weight[2]

    dcq = unit[1].astype(BF)
    dvec[7:8, :] = column_sum(dcq.astype(F32)) * scale
    dcrossed = nt(dcq, weight[4]) * scale
    weight[4] = (tn(low[0], dcq) * scale).astype(BF)
    dvec[5:6, :] = column_sum(dcrossed * unit[0])
    dvec[6:7, :] = column_sum(dcrossed)
    dmid = later[...] + norm_back(dcrossed, unit[0], cross_spread, vector(5))
    later[...] = dmid
    branch = dmid.astype(BF)
    dvec[4:5, :] = column_sum(branch.astype(F32))
    dmixed = nt(branch, weight[3]).astype(BF)
    weight[3] = tn(mixed[...].astype(BF), branch).astype(BF)
    low[2] = dmixed
    mixed[...] = mixed[...] * dmixed.astype(F32)
    pump("middle")

    for b in range(2):
        for kind in range(2):
            if pad:
                cpowers[2 * kind + b, 0 : pad // PIECE, :, 0:D] = jnp.zeros((pad // PIECE, PIECE, D), BF)

        def backward(quad, carry, b=b):
            fill(b, quad)
            lanes = pl.ds(pl.multiple_of(quad * 256, 256), 256)

            def store(c, dkeys, dvalues):
                pieces = dkeys.shape[0] // PIECE
                part = pl.ds(c * pieces + pad // PIECE, pieces)
                cpowers[b, part, :, lanes] = dkeys.astype(BF).reshape(pieces, PIECE, 256)
                cpowers[2 + b, part, :, lanes] = dvalues.astype(BF).reshape(pieces, PIECE, 256)

            out = attend_back(
                spread_heads(queries[b * half : (b + 1) * half, lanes].astype(F32), 4).astype(BF),
                spread_heads(low[2, b * half : (b + 1) * half, lanes].astype(F32), 4).astype(BF),
                spread_heads(mixed[b * half : (b + 1) * half, lanes], 4),
                kwin,
                vwin,
                inverses[b * 2 + quad, 0:1, :],
                powers.at[b * 2 + quad],
                store,
            )
            unit[1, b * half : (b + 1) * half, lanes] = join_heads(out, 4)

            for index in range(2):

                @pl.when(quad == index)
                def _(index=index):
                    pump("self" + str(2 * b + index))

            return carry

        lax.fori_loop(0, 2, backward, 0)

        ratio = half // shalf
        for j in range(around):
            slot = tinv[jnp.maximum(base[b] - (around - 1) + j, 0)]
            stream[j * ratio : (j + 1) * ratio] = nrm[slot].reshape(ratio, shalf, D)
        normed = stream[0 : around * ratio].reshape(around * half, D)
        for kind in range(2):
            change = cpowers[2 * kind + b, 0 : around * thirds, :, 0:D].reshape(around * half, D)
            if kind == 1:
                dvec[3:4, :] += column_sum(change.astype(F32))
            total = tn(normed, change)
            there = slice(kind * D, (kind + 1) * D)
            if b == 0:
                scores[there, 0:D] = total
            else:
                weight[1 + kind] = (scores[there, 0:D] + total).astype(BF)
        if b == 0:
            pump("window")
    for index in range(3):
        pl.semaphore_signal(
            ready.at[index],
            inc=1,
            device_id={"seq": cube.other(1 << index)},
            device_id_type=MESH,
        )

    dq = unit[1].astype(BF)
    dvec[2:3, :] = column_sum(dq.astype(F32)) * scale
    heard[...] = nt(dq, weight[0]) * scale
    own_normed = nrm[pl.ds(2 * me, 2)].reshape(rows, D)
    weight[0] = (tn(own_normed, dq) * scale).astype(BF)

    pump("weights")

    for b in range(2):

        def through(c, carry, b=b):
            part = pl.ds(c * around, around)
            dkeys = cpowers[b, part, :, 0:D].reshape(around * PIECE, D)
            dvalues = cpowers[2 + b, part, :, 0:D].reshape(around * PIECE, D)
            total = nt(dkeys, ckeys[0:D, :]) + nt(dvalues, ckeys[D : 2 * D, :])
            cpowers[b, part, :, 0:D] = total.astype(BF).reshape(around, PIECE, D)
            return carry

        lax.fori_loop(0, thirds, through, 0)
        pump("through" + str(b))

    def assemble(code):
        def one(part, carry):
            s = 2 * cube.other(code) + part
            for third in range(thirds):
                total = jnp.zeros((PIECE, D), F32)
                for b in range(2):
                    back = base[b] - tord[0, s]
                    inside = (back >= 0) & (back < around)
                    first = jnp.clip(around - 1 - back, 0, around - 1) * thirds
                    found = cpowers[b, first + third][:, 0:D]
                    total = total + jnp.where(inside, found.astype(F32), 0.0)
                if code == 0:
                    start = pl.multiple_of(part * half + third * PIECE, PIECE)
                    total = total + heard[pl.ds(start, PIECE), :]
                nrm[s, third] = total.astype(BF)
            return carry

        lax.fori_loop(0, 2, one, 0)

    for code in (1, 3, 5, 7):
        assemble(code)
    pump("theirs")
    for code in (6, 2, 4, 0):
        assemble(code)
    pump("end")
    assert not any(counts.values()), counts
    for turn, first in enumerate((8, 12, 4, 0)):
        pltpu.make_async_copy(
            weight.at[pl.ds(first, 4)], grads.at[pl.ds(first, 4)], sem.at[turn]
        ).wait()


def layer_call(sizes, small_ints, own, cot, own_memory, vectors, w_small, w_in, w_out):
    rows, blocks, half, sblocks, shalf, window = (
        sizes["rows"],
        sizes["blocks"],
        sizes["half"],
        sizes["sblocks"],
        sizes["shalf"],
        sizes["window"],
    )
    sources = sblocks * shalf
    levels = sizes["levels"]
    vmem = pl.BlockSpec(memory_space=pltpu.VMEM)
    smem = pl.BlockSpec(memory_space=pltpu.SMEM)
    hbm = pl.BlockSpec(memory_space=pl.ANY)

    count = len(vectors)

    def body(*refs):
        head, rest = refs[:7], refs[7:]
        vector_refs, rest = rest[:count], rest[count:]
        layer_kernel(sizes, *head, vector_refs, rest[:8], *rest[8:])

    return pl.pallas_call(
        body,
        out_shape=(
            jax.ShapeDtypeStruct((rows, D), BF),
            jax.ShapeDtypeStruct((rows, D), F32),
            jax.ShapeDtypeStruct((2 * shalf, D), F32),
            jax.ShapeDtypeStruct((VECTORS, D), F32),
            jax.ShapeDtypeStruct((16, D, D), BF),
        ),
        in_specs=[smem] * 4 + [vmem] * (3 + count) + [hbm] * 10,
        out_specs=(vmem, vmem, vmem, vmem, hbm),
        scratch_shapes=[
            pltpu.VMEM((VECTORS, D), F32),
            pltpu.VMEM((blocks, half // PIECE, PIECE, D), BF),
            pltpu.VMEM((sblocks, shalf, D), BF),
            pltpu.VMEM((sblocks, shalf, D), BF),
            pltpu.VMEM((16, D, D), BF),
            pltpu.VMEM((2, 2, blocks, half, 256), BF),
            pltpu.VMEM((rows, D), BF),
            pltpu.VMEM((sources, D), BF),
            pltpu.VMEM((sources, D), BF),
            pltpu.VMEM((sources, 2 * rows), F32),
            pltpu.VMEM((4, window // PIECE, PIECE, 4 * half), BF),
            pltpu.VMEM((4, sources // PIECE, PIECE, 2 * rows), BF),
            pltpu.VMEM((4, 8, 4 * half), F32),
            pltpu.VMEM((4, 8, 2 * rows), F32),
            pltpu.VMEM((rows, D), F32),
            pltpu.VMEM((rows, D), F32),
            pltpu.VMEM((3, rows, D), F32),
            pltpu.VMEM((3, rows, D), BF),
            pltpu.SMEM((blocks,), jnp.int32),
            pltpu.SMEM((sblocks,), jnp.int32),
            pltpu.VMEM((2, 4, D // 2, D), BF),
            pltpu.VMEM((2, 2, 4, D // 8, D), BF),
            pltpu.VMEM((2, 2, 4, D // 16, D), BF),
            pltpu.VMEM((2, levels - 1, 2, D // 16, D), BF),
            pltpu.VMEM((2, levels - 1, 2, D // 16, D), BF),
            pltpu.VMEM((8, VECTORS, D), F32),
            pltpu.VMEM((levels, VECTORS, D), F32),
            pltpu.SemaphoreType.DMA((16,)),
            pltpu.SemaphoreType.DMA((2, 16)),
            pltpu.SemaphoreType.DMA((2, 16)),
            pltpu.SemaphoreType.DMA((4, 22)),
            pltpu.SemaphoreType.DMA((4, 22)),
            pltpu.SemaphoreType.REGULAR((4, 3)),
            pltpu.SemaphoreType.DMA((2, 14)),
            pltpu.SemaphoreType.DMA((2, 14)),
            pltpu.SemaphoreType.DMA((2, 10)),
            pltpu.SemaphoreType.DMA((2, 10)),
            pltpu.SemaphoreType.REGULAR((3,)),
        ],
        compiler_params=pltpu.CompilerParams(
            vmem_limit_bytes=64 << 20, collective_id=0, has_side_effects=True
        ),
    )(*small_ints, own, cot, own_memory, *vectors, *w_small, w_in, w_out)


def fused_on_device(
    inputs, memory, target_lengths, source_lengths, target_order, source_order,
    self_gain, self_shift, self_query, query_bias, self_key, self_value, value_bias,
    self_output, output_bias, cross_gain, cross_shift, cross_query, cquery_bias, cross_key,
    cross_value, cvalue_bias, cross_output, coutput_bias, final_gain, final_shift,
    inner_weight, inner_bias, outer_weight, outer_bias, cotangent,
):
    rows = inputs.shape[1]
    blocks = target_order.shape[1]
    sblocks = source_order.shape[1]
    ranks = lax.axis_size("seq")
    half = ranks * rows // blocks
    shalf = ranks * memory.shape[1] // sblocks
    ndoc = target_lengths.shape[1]
    reach = max(LONGEST, blocks * half - LONGEST - SHORTEST * (ndoc - 1))
    window = -(-(reach - 1 + half) // CHUNK) * CHUNK
    sizes = dict(
        rows=rows, blocks=blocks, half=half, sblocks=sblocks, shalf=shalf, ndoc=ndoc, window=window,
        levels=lax.axis_size("batch"),
    )
    result, dinputs, dmemory, dvec, grads = layer_call(
        sizes, (target_lengths, source_lengths, target_order, source_order),
        inputs.reshape(2, half // PIECE, PIECE, D), cotangent[0], memory.reshape(2, shalf, D),
        (
            self_gain, self_shift, query_bias, value_bias, output_bias, cross_gain, cross_shift,
            cquery_bias, cvalue_bias, coutput_bias, final_gain, final_shift, outer_bias, inner_bias,
        ),
        (self_query, self_key, self_value, self_output, cross_query, cross_key, cross_value, cross_output),
        inner_weight, outer_weight,
    )
    made = publish(grads, dvec, (result, dinputs, dmemory))
    result, dinputs, dmemory = made[24:]
    squares, wide, tall, rows_of, units = made[:8], made[8], made[9], made[10:23], made[23]
    return (
        result[None], dinputs[None], dmemory[None],
        rows_of[0], rows_of[1], squares[0], rows_of[2], squares[1], squares[2], rows_of[3],
        squares[3], rows_of[4], rows_of[5], rows_of[6], squares[4], rows_of[7], squares[5],
        squares[6], rows_of[8], squares[7], rows_of[9], rows_of[10], rows_of[11],
        wide, units, tall, rows_of[12],
    )


def solution(mesh):
    in_specs = (
        P("batch", "seq", None),
        P("batch", "seq", None),
        P("batch", None),
        P("batch", None),
        P("batch", None),
        P("batch", None),
        P(),
        P(),
        P(),
        P(),
        P(),
        P(),
        P(),
        P(),
        P(),
        P(),
        P(),
        P(),
        P(),
        P(),
        P(),
        P(),
        P(),
        P(),
        P(),
        P(),
        P(),
        P(),
        P(),
        P(),
        P("batch", "seq", None),
    )
    out_specs = (
        P("batch", "seq", None),
        P("batch", "seq", None),
        P("batch", "seq", None),
        P(),
        P(),
        P(),
        P(),
        P(),
        P(),
        P(),
        P(),
        P(),
        P(),
        P(),
        P(),
        P(),
        P(),
        P(),
        P(),
        P(),
        P(),
        P(),
        P(),
        P(),
        P(),
        P(),
        P(),
    )
    return jax.shard_map(
        fused_on_device if (mesh.shape["seq"], mesh.shape["batch"]) == (8, 4) else on_device,
        mesh=mesh, in_specs=in_specs, out_specs=out_specs, check_vma=False,
    )
```

```python
import math

import jax
import jax.numpy as jnp
from jax import lax
from jax.experimental import pallas as pl
from jax.experimental.pallas import tpu as pltpu
from jax.sharding import PartitionSpec as P

D = 512
HEADS = 8


EPSILON = 1e-05
NEGATIVE = -1e30


def norm(values, gain, shift):
    center = values - jnp.mean(values, axis=-1, keepdims=True)
    spread = jnp.mean(center * center, axis=-1, keepdims=True)
    return center * lax.rsqrt(spread + EPSILON) * gain + shift


def product(left, right):
    return jnp.dot(left, right, preferred_element_type=jnp.float32)


def weight_grad(left, right):
    return jnp.einsum("ti,to->io", left, right, preferred_element_type=jnp.float32)


def input_grad(grad, weight):
    return jnp.einsum("to,io->ti", grad, weight, preferred_element_type=jnp.float32)


def split_heads(values):
    return values.reshape(values.shape[0], HEADS, -1)


def locate(order, lengths, blocksize, start, count):
    index = start + jnp.arange(count, dtype=jnp.int32)
    slot = index // blocksize
    picked = jnp.sum(
        jnp.where(
            slot[:, None] == jnp.arange(order.shape[0], dtype=jnp.int32)[None, :], order[None, :], 0
        ),
        axis=1,
    )
    position = picked * blocksize + index % blocksize
    ends = jnp.cumsum(lengths)
    document = jnp.sum((position[:, None] >= ends[None, :]).astype(jnp.int32), axis=1)
    return (document, position)


def visible(query_doc, query_pos, key_doc, key_pos, causal):
    same = query_doc[:, None] == key_doc[None, :]
    if causal:
        return same & (key_pos[None, :] <= query_pos[:, None])
    return same


def opening(rows):
    return (
        jnp.zeros((rows, HEADS, D // HEADS), jnp.float32),
        jnp.full((rows, HEADS), NEGATIVE, jnp.float32),
        jnp.zeros((rows, HEADS), jnp.float32),
    )


def online(carry, query_heads, piece_keys, piece_values, allowed):
    weighted, highest, total = carry
    scores = jnp.einsum(
        "qhd,khd->qhk", query_heads, split_heads(piece_keys), preferred_element_type=jnp.float32
    )
    allowed = allowed[:, None, :]
    raised = jnp.maximum(highest, jnp.max(jnp.where(allowed, scores, NEGATIVE), axis=-1))
    powers = jnp.exp(jnp.where(allowed, scores - raised[..., None], NEGATIVE))
    total = jnp.sum(powers, axis=-1)
    weighted = jnp.einsum(
        "qhk,khd->qhd",
        powers.astype(jnp.bfloat16),
        split_heads(piece_values),
        preferred_element_type=jnp.float32,
    )
    return (weighted, raised, total)


def finish(carry):
    weighted, highest, total = carry
    return (highest + jnp.log(total), (weighted / total[..., None]).reshape(weighted.shape[0], D))


def block_back(query_heads, grad_heads, log_total, delta, piece_keys, piece_values, allowed):
    key_heads = split_heads(piece_keys)
    value_heads = split_heads(piece_values)
    scores = jnp.einsum("qhd,khd->qhk", query_heads, key_heads, preferred_element_type=jnp.float32)
    weights = jnp.exp(jnp.where(allowed[:, None, :], scores - log_total[..., None], NEGATIVE))
    grad_weights = jnp.einsum(
        "qhd,khd->qhk", grad_heads, value_heads, preferred_element_type=jnp.float32
    )
    grad_scores = (weights * (grad_weights - delta[..., None])).astype(jnp.bfloat16)
    grad_values = jnp.einsum(
        "qhk,qhd->khd", weights.astype(jnp.bfloat16), grad_heads, preferred_element_type=jnp.float32
    )
    grad_keys = jnp.einsum(
        "qhk,qhd->khd", grad_scores, query_heads, preferred_element_type=jnp.float32
    )
    grad_query = jnp.einsum(
        "qhk,khd->qhd", grad_scores, key_heads, preferred_element_type=jnp.float32
    )
    return (grad_query, grad_keys, grad_values)


def scan_back(
    query_heads,
    grad_heads,
    log_total,
    delta,
    all_keys,
    all_values,
    row_doc,
    row_pos,
    order,
    lengths,
    blocksize,
    causal,
):
    total_keys = all_keys.shape[0]
    width = math.gcd(total_keys, 512)
    count = total_keys // width

    def step(grad_query, item):
        block_keys, block_values, number = item
        key_doc, key_pos = locate(order, lengths, blocksize, number * width, width)
        allowed = visible(row_doc, row_pos, key_doc, key_pos, causal)
        query_term, key_term, value_term = block_back(
            query_heads, grad_heads, log_total, delta, block_keys, block_values, allowed
        )
        return (grad_query + query_term, (key_term, value_term))

    grad_query, (grad_keys, grad_values) = lax.scan(
        step,
        jnp.zeros(query_heads.shape, jnp.float32),
        (
            all_keys.reshape(count, width, D),
            all_values.reshape(count, width, D),
            jnp.arange(count, dtype=jnp.int32),
        ),
    )
    return (grad_query, grad_keys.reshape(total_keys, D), grad_values.reshape(total_keys, D))


def on_device(
    inputs,
    memory,
    target_lengths,
    source_lengths,
    target_order,
    source_order,
    self_gain,
    self_shift,
    self_query,
    query_bias,
    self_key,
    self_value,
    value_bias,
    self_output,
    output_bias,
    cross_gain,
    cross_shift,
    cross_query,
    cquery_bias,
    cross_key,
    cross_value,
    cvalue_bias,
    cross_output,
    coutput_bias,
    final_gain,
    final_shift,
    inner_weight,
    inner_bias,
    outer_weight,
    outer_bias,
    cotangent,
):
    rows = inputs.shape[1]
    sources = memory.shape[1]
    target_half = rows // 2
    source_half = sources // 2
    own_lengths = target_lengths[0]
    memory_lengths = source_lengths[0]
    own_order = target_order[0]
    memory_order = source_order[0]
    scale = float(D // HEADS) ** (-0.5)
    place = lax.axis_index("seq")
    row_doc, row_pos = locate(own_order, own_lengths, target_half, place * rows, rows)
    inputs_f = inputs[0].astype(jnp.float32)
    encoded = memory[0]
    normed, norm_back = jax.vjp(
        norm, inputs_f, self_gain.astype(jnp.float32), self_shift.astype(jnp.float32)
    )
    normed_low = normed.astype(jnp.bfloat16)
    queries = ((product(normed_low, self_query) + query_bias) * scale).astype(jnp.bfloat16)
    keys = product(normed_low, self_key).astype(jnp.bfloat16)
    values = (product(normed_low, self_value) + value_bias).astype(jnp.bfloat16)
    query_heads = split_heads(queries)
    piece = (
        lax.all_gather(keys, "seq", axis=0, tiled=True),
        lax.all_gather(values, "seq", axis=0, tiled=True),
    )
    key_doc, key_pos = locate(own_order, own_lengths, target_half, jnp.int32(0), piece[0].shape[0])
    self_carry = online(
        opening(rows),
        query_heads,
        piece[0],
        piece[1],
        visible(row_doc, row_pos, key_doc, key_pos, True),
    )
    self_total, mixed = finish(self_carry)
    mixed_low = mixed.astype(jnp.bfloat16)
    middle = inputs_f + product(mixed_low, self_output) + output_bias
    crossed, cross_back = jax.vjp(
        norm, middle, cross_gain.astype(jnp.float32), cross_shift.astype(jnp.float32)
    )
    crossed_low = crossed.astype(jnp.bfloat16)
    cqueries = ((product(crossed_low, cross_query) + cquery_bias) * scale).astype(jnp.bfloat16)
    ckeys = product(encoded, cross_key).astype(jnp.bfloat16)
    cvalues = (product(encoded, cross_value) + cvalue_bias).astype(jnp.bfloat16)
    cquery_heads = split_heads(cqueries)
    piece = (
        lax.all_gather(ckeys, "seq", axis=0, tiled=True),
        lax.all_gather(cvalues, "seq", axis=0, tiled=True),
    )
    key_doc, key_pos = locate(
        memory_order, memory_lengths, source_half, jnp.int32(0), piece[0].shape[0]
    )
    cross_carry = online(
        opening(rows),
        cquery_heads,
        piece[0],
        piece[1],
        visible(row_doc, row_pos, key_doc, key_pos, False),
    )
    cross_total, heard = finish(cross_carry)
    heard_low = heard.astype(jnp.bfloat16)
    later = middle + product(heard_low, cross_output) + coutput_bias
    fed, final_back = jax.vjp(
        norm, later, final_gain.astype(jnp.float32), final_shift.astype(jnp.float32)
    )
    fed_low = fed.astype(jnp.bfloat16)
    before = product(fed_low, inner_weight) + inner_bias
    after, gelu_back = jax.vjp(lambda entry: jax.nn.gelu(entry, approximate=False), before)
    after_low = after.astype(jnp.bfloat16)
    result = later + product(after_low, outer_weight) + outer_bias
    grad_out = cotangent[0]
    outer_weight_grad = weight_grad(after_low, grad_out)
    outer_bias_grad = jnp.sum(grad_out.astype(jnp.float32), axis=0)
    grad_after = input_grad(grad_out, outer_weight)
    grad_before = gelu_back(grad_after)[0].astype(jnp.bfloat16)
    inner_weight_grad = weight_grad(fed_low, grad_before)
    inner_bias_grad = jnp.sum(grad_before.astype(jnp.float32), axis=0)
    grad_fed = input_grad(grad_before, inner_weight)
    grad_later_norm, final_gain_grad, final_shift_grad = final_back(grad_fed)
    grad_later = cotangent[0].astype(jnp.float32) + grad_later_norm
    grad_cbranch = grad_later.astype(jnp.bfloat16)
    cross_output_grad = weight_grad(heard_low, grad_cbranch)
    coutput_bias_grad = jnp.sum(grad_cbranch.astype(jnp.float32), axis=0)
    grad_heard = input_grad(grad_cbranch, cross_output).astype(jnp.bfloat16)
    grad_heard_heads = split_heads(grad_heard)
    cross_delta = jnp.sum(grad_heard_heads.astype(jnp.float32) * split_heads(heard), axis=-1)
    all_ckeys, all_cvalues = (
        lax.all_gather(ckeys, "seq", axis=0, tiled=True),
        lax.all_gather(cvalues, "seq", axis=0, tiled=True),
    )
    grad_cq, part_ckeys, part_cvalues = scan_back(
        cquery_heads,
        grad_heard_heads,
        cross_total,
        cross_delta,
        all_ckeys,
        all_cvalues,
        row_doc,
        row_pos,
        memory_order,
        memory_lengths,
        source_half,
        False,
    )
    own_ckeys, own_cvalues = (
        lax.psum_scatter(
            part_ckeys.astype(jnp.bfloat16), "seq", scatter_dimension=0, tiled=True
        ).astype(jnp.float32),
        lax.psum_scatter(
            part_cvalues.astype(jnp.bfloat16), "seq", scatter_dimension=0, tiled=True
        ).astype(jnp.float32),
    )
    own_ckeys_low = own_ckeys.astype(jnp.bfloat16)
    own_cvalues_low = own_cvalues.astype(jnp.bfloat16)
    cross_key_grad = weight_grad(encoded, own_ckeys_low)
    cross_value_grad = weight_grad(encoded, own_cvalues_low)
    cvalue_bias_grad = jnp.sum(own_cvalues_low.astype(jnp.float32), axis=0)
    memory_grad = input_grad(own_ckeys_low, cross_key) + input_grad(own_cvalues_low, cross_value)
    grad_cq_low = grad_cq.reshape(rows, D).astype(jnp.bfloat16)
    cross_query_grad = weight_grad(crossed_low, grad_cq_low) * scale
    cquery_bias_grad = jnp.sum(grad_cq_low.astype(jnp.float32), axis=0) * scale
    grad_crossed = input_grad(grad_cq_low, cross_query) * scale
    grad_middle_norm, cross_gain_grad, cross_shift_grad = cross_back(grad_crossed)
    grad_middle = grad_later + grad_middle_norm
    grad_sbranch = grad_middle.astype(jnp.bfloat16)
    self_output_grad = weight_grad(mixed_low, grad_sbranch)
    output_bias_grad = jnp.sum(grad_sbranch.astype(jnp.float32), axis=0)
    grad_mixed = input_grad(grad_sbranch, self_output).astype(jnp.bfloat16)
    grad_mixed_heads = split_heads(grad_mixed)
    self_delta = jnp.sum(grad_mixed_heads.astype(jnp.float32) * split_heads(mixed), axis=-1)
    all_keys, all_values = (
        lax.all_gather(keys, "seq", axis=0, tiled=True),
        lax.all_gather(values, "seq", axis=0, tiled=True),
    )
    grad_q, part_keys, part_values = scan_back(
        query_heads,
        grad_mixed_heads,
        self_total,
        self_delta,
        all_keys,
        all_values,
        row_doc,
        row_pos,
        own_order,
        own_lengths,
        target_half,
        True,
    )
    own_keys, own_values = (
        lax.psum_scatter(
            part_keys.astype(jnp.bfloat16), "seq", scatter_dimension=0, tiled=True
        ).astype(jnp.float32),
        lax.psum_scatter(
            part_values.astype(jnp.bfloat16), "seq", scatter_dimension=0, tiled=True
        ).astype(jnp.float32),
    )
    own_keys_low = own_keys.astype(jnp.bfloat16)
    own_values_low = own_values.astype(jnp.bfloat16)
    self_key_grad = weight_grad(normed_low, own_keys_low)
    self_value_grad = weight_grad(normed_low, own_values_low)
    value_bias_grad = jnp.sum(own_values_low.astype(jnp.float32), axis=0)
    grad_q_low = grad_q.reshape(rows, D).astype(jnp.bfloat16)
    self_query_grad = weight_grad(normed_low, grad_q_low) * scale
    query_bias_grad = jnp.sum(grad_q_low.astype(jnp.float32), axis=0) * scale
    grad_normed = (
        input_grad(grad_q_low, self_query) * scale
        + input_grad(own_keys_low, self_key)
        + input_grad(own_values_low, self_value)
    )
    grad_in_norm, self_gain_grad, self_shift_grad = norm_back(grad_normed)
    inputs_grad = grad_middle + grad_in_norm
    summed = lax.psum(
        (
            self_gain_grad,
            self_shift_grad,
            self_query_grad,
            query_bias_grad,
            self_key_grad,
            self_value_grad,
            value_bias_grad,
            self_output_grad,
            output_bias_grad,
            cross_gain_grad,
            cross_shift_grad,
            cross_query_grad,
            cquery_bias_grad,
            cross_key_grad,
            cross_value_grad,
            cvalue_bias_grad,
            cross_output_grad,
            coutput_bias_grad,
            final_gain_grad,
            final_shift_grad,
            inner_weight_grad,
            inner_bias_grad,
            outer_weight_grad,
            outer_bias_grad,
        ),
        ("seq", "batch"),
    )
    return (result.astype(jnp.bfloat16)[None], inputs_grad[None], memory_grad[None]) + tuple(summed)


HDIM = D // HEADS
SHORTEST = 32
LONGEST = 1024
CHUNK = 256
PIECE = 64

SCHEDULE = dict(
    half="A",
    feed="AB",
    pair1="A",
    pair2="B",
    pair3="A",
    middle="VBCMA",
    self0="C",
    self1="M",
    window="BA",
    self2="C",
    self3="AB",
    weights="ECME",
    through0="VB",
    through1="CE",
    theirs="BRMVA",
    end="ECRECERCEBRBASCESES",
)
MESH = pl.DeviceIdType.MESH
PARTS = 2
BF = jnp.bfloat16
F32 = jnp.float32
VECTORS = 24


def nn(left, right):
    return lax.dot_general(left, right, (((1,), (0,)), ((), ())), preferred_element_type=F32)


def nt(left, right):
    return lax.dot_general(left, right, (((1,), (1,)), ((), ())), preferred_element_type=F32)


def tn(left, right):
    return lax.dot_general(left, right, (((0,), (0,)), ((), ())), preferred_element_type=F32)


def centred(values):
    center = values - jnp.mean(values, axis=-1, keepdims=True)
    spread = lax.rsqrt(jnp.mean(center * center, axis=-1, keepdims=True) + EPSILON)
    return center * spread, spread


def norm_back(grad, unit, spread, gain):
    scaled = grad * gain
    return spread * (
        scaled
        - jnp.mean(scaled, axis=-1, keepdims=True)
        - unit * jnp.mean(scaled * unit, axis=-1, keepdims=True)
    )


def column_sum(values):
    return jnp.sum(values, axis=0, keepdims=True)


def spread_heads(block, heads):
    lane = lax.broadcasted_iota(jnp.int32, block.shape, 1)
    return jnp.concatenate(
        [
            jnp.where((lane >= h * HDIM) & (lane < (h + 1) * HDIM), block, 0.0)
            for h in range(heads)
        ],
        axis=0,
    )


def join_heads(stacked, heads):
    rows = stacked.shape[0] // heads
    lane = lax.broadcasted_iota(jnp.int32, (rows, stacked.shape[1]), 1)
    total = stacked[:rows]
    for h in range(1, heads):
        total = jnp.where(lane >= h * HDIM, stacked[h * rows : (h + 1) * rows], total)
    return total


def part_of(array, index, size):
    if len(array.shape) == 3:
        count = size // PIECE
        return array[pl.ds(index * count, count)].reshape(size, array.shape[2])
    return array[pl.ds(pl.multiple_of(index * size, size), size), :]


def whole_of(array):
    return array[...].reshape(-1, array.shape[-1])


def attend(queries, keys, values, low, high, scores, powers):
    total = math.prod(keys.shape[:-1])
    width = queries.shape[0]
    chunk = total // PARTS
    pieces = chunk // PIECE

    def first(c, highest):
        rows = pl.ds(pl.multiple_of(c * chunk, chunk), chunk)
        place = lax.broadcasted_iota(jnp.int32, (chunk, width), 0) - (low - c * chunk)
        found = jnp.where(
            place.astype(jnp.uint32) < length, nt(part_of(keys, c, chunk), queries), NEGATIVE
        )
        scores[rows, :] = found
        return jnp.maximum(highest, jnp.max(found, axis=0, keepdims=True))

    length = (high - low).astype(jnp.uint32)
    highest = lax.fori_loop(0, total // chunk, first, jnp.full((1, width), NEGATIVE, F32))

    def second(c, summed):
        rows = pl.ds(pl.multiple_of(c * chunk, chunk), chunk)
        power = jnp.exp(scores[rows, :] - highest)
        powers[pl.ds(c * pieces, pieces)] = power.astype(BF).reshape(pieces, PIECE, width)
        return summed + column_sum(power)

    summed = lax.fori_loop(0, total // chunk, second, jnp.zeros((1, width), F32))
    inverse = 1.0 / summed
    mixed = tn(whole_of(values), powers[0 : total // PIECE].reshape(total, width)) * inverse
    return mixed.T, inverse


def attend_back(queries, grads, product_of, keys, values, inverse, powers, store):
    total = math.prod(keys.shape[:-1])
    width = queries.shape[0]
    chunk = total // PARTS
    pieces = chunk // PIECE
    ones = jnp.ones((8, queries.shape[1]), BF)
    coarse = product_of.astype(BF)
    fine = (product_of - coarse.astype(F32)).astype(BF)
    delta = (nt(ones, coarse) + nt(ones, fine))[0:1]

    def step(c, carry):
        part = pl.ds(c * pieces, pieces)
        weights = powers[part].reshape(chunk, width).astype(F32) * inverse
        weights_low = weights.astype(BF)
        change = (weights * (nt(part_of(values, c, chunk), grads) - delta)).astype(BF)
        powers[part] = change.reshape(pieces, PIECE, width)
        store(c, nn(change, queries), nn(weights_low, grads))
        return carry

    lax.fori_loop(0, total // chunk, step, 0)
    return tn(whole_of(keys), powers[0 : total // PIECE].reshape(total, width)).T


class Cube:
    def __init__(self, me, level, levels):
        self.me, self.level, self.levels = me, level, levels
        self.bits = (lax.rem(me, 2), lax.rem(lax.div(me, 2), 2), lax.div(me, 4))

    def other(self, code):
        place = self.me
        for axis in range(3):
            if code >> axis & 1:
                place = place + (1 << axis) * (1 - 2 * self.bits[axis])
        return place

    def plane(self, step):
        return lax.rem(self.level + step, self.levels)

    def greet(self):
        barrier = pltpu.get_barrier_semaphore()
        for code in range(1, 8):
            pl.semaphore_signal(
                barrier, inc=1, device_id={"seq": self.other(code)}, device_id_type=MESH
            )
        for step in range(1, self.levels):
            pl.semaphore_signal(
                barrier, inc=1, device_id={"batch": self.plane(step)}, device_id_type=MESH
            )

    def await_all(self):
        pl.semaphore_wait(pltpu.get_barrier_semaphore(), 6 + self.levels)

    def send(self, code, source, target, send_sem, recv_sem):
        copy = pltpu.make_async_remote_copy(
            src_ref=source,
            dst_ref=target,
            send_sem=send_sem,
            recv_sem=recv_sem,
            device_id={"seq": self.other(code)},
            device_id_type=MESH,
        )
        copy.start()
        return copy


class Steps:
    def copies(self, step):
        return [
            pltpu.make_async_remote_copy(
                src_ref=source,
                dst_ref=target,
                send_sem=self.send_sem.at[index],
                recv_sem=self.recv_sem.at[index],
                device_id=device,
                device_id_type=MESH,
            )
            for device, source, target, index in self.moves(step)
        ]

    def begin(self, step):
        for copy in self.copies(step):
            copy.start()

    def end(self, step):
        for copy in self.copies(step):
            copy.wait()

    step, last = 0, 0

    def advance(self):
        if self.step:
            self.end(self.step)
            self.take(self.step)
        self.step += 1
        if self.step <= self.last:
            self.begin(self.step)

    def take(self, step):
        pass


class Reduce(Steps):
    last = 8

    def __init__(self, cube, panels, first, pair, flat, edge, deep, leave, send_sem, recv_sem, sent, before, finish):
        self.before, self.finish, self.freed = before, finish, set()
        self.cube, self.panels, self.first = cube, panels, first
        self.pair, self.flat, self.edge, self.deep, self.leave = pair, flat, edge, deep, leave
        self.send_sem, self.recv_sem, self.sent = send_sem, recv_sem, sent

    def await_free(self, index):
        if index not in self.freed:
            self.freed.add(index)
            pl.semaphore_wait(self.sent.at[index], 1)

    def begin(self, step):
        for index in {6: (1, 2), 8: (0,)}.get(step, ()):
            self.await_free(index)
        if self.before is not None:
            for index in {1: (0,), 2: (1, 2)}.get(step, ()):
                self.before.await_free(index)
        if step == 4:
            for k in range(1, self.cube.levels):
                there = self.first + self.cube.plane(k)
                for axis in (1, 2):
                    self.leave[k - 1, axis - 1] = self.panels[there, self.rows(axis=axis, further=0), :]
        super().begin(step)

    def rows(self, core=0, axis=None, far=0, further=None):
        bits = self.cube.bits
        flip = lambda bit, other: 1 - bit if other else bit
        start, size = flip(bits[0], core) * (D // 2), D // 2
        if axis is not None:
            size = D // 8
            start = start + (axis - 1) * (D // 4) + flip(bits[axis], far) * size
            if further is not None:
                size = D // 16
                start = start + flip(bits[3 - axis], further) * size
        return pl.ds(pl.multiple_of(start, D // 16), size)

    def all(self, rows):
        return self.panels.at[pl.ds(self.first, 4), rows, :]

    def moves(self, step):
        cube = self.cube
        near = lambda code: {"seq": cube.other(code)}
        if step == 1:
            return [(near(1), self.all(self.rows(core=1)), self.pair, 0)]
        if step == 2:
            return [
                (near(2 * axis), self.all(self.rows(axis=axis, far=1)), self.flat.at[axis - 1], axis)
                for axis in (1, 2)
            ]
        if step == 3:
            return [
                (
                    near(6 - 2 * axis),
                    self.all(self.rows(axis=axis, further=1)),
                    self.edge.at[axis - 1],
                    2 + axis,
                )
                for axis in (1, 2)
            ]
        if step == 4:
            return [
                (
                    {"batch": cube.plane(k)},
                    self.leave.at[k - 1, axis - 1],
                    self.deep.at[k - 1, axis - 1],
                    3 + 2 * k + axis - 1,
                )
                for k in range(1, cube.levels)
                for axis in (1, 2)
            ]
        if step == 5:
            there = self.first + cube.level
            return [
                (
                    {"batch": cube.plane(k)},
                    self.panels.at[there, self.rows(axis=axis, further=0), :],
                    self.panels.at[there, self.rows(axis=axis, further=0), :],
                    9 + 2 * k + axis - 1,
                )
                for k in range(1, cube.levels)
                for axis in (1, 2)
            ]
        if step == 6:
            parts = [(6 - 2 * axis, self.all(self.rows(axis=axis, further=0)), 16 + axis) for axis in (1, 2)]
        elif step == 7:
            parts = [(2 * axis, self.all(self.rows(axis=axis)), 18 + axis) for axis in (1, 2)]
        else:
            parts = [(1, self.all(self.rows()), 21)]
        return [(near(code), part, part, index) for code, part, index in parts]

    def add(self, rows, found):
        def one(i, carry):
            there = self.first + i
            total = self.panels[there, rows, :].astype(F32) + found[i].astype(F32)
            self.panels[there, rows, :] = total.astype(BF)
            return carry

        lax.fori_loop(0, 4, one, 0)

    def take(self, step):
        if step == 1:
            self.add(self.rows(), self.pair)
        elif step == 2:
            for axis in (1, 2):
                self.add(self.rows(axis=axis), self.flat.at[axis - 1])
        elif step == 3:
            for axis in (1, 2):
                self.add(self.rows(axis=axis, further=0), self.edge.at[axis - 1])
        elif step == 4:
            there = self.first + self.cube.level
            for axis in (1, 2):
                rows = self.rows(axis=axis, further=0)
                total = self.panels[there, rows, :].astype(F32)
                for k in range(self.cube.levels - 1):
                    total = total + self.deep[k, axis - 1].astype(F32)
                self.panels[there, rows, :] = total.astype(BF)
        elif step == 8:
            self.finish()
        for index in {1: (0,), 3: (1, 2)}.get(step, ()):
            pl.semaphore_signal(
                self.sent.at[index],
                inc=1,
                device_id={"seq": self.cube.other(1 << index)},
                device_id_type=MESH,
            )


class Scatter(Steps):
    last = 3

    def __init__(self, cube, block, spare, send_sem, recv_sem, ready, finish):
        self.cube, self.block, self.spare = cube, block, spare
        self.ready, self.finish = ready, finish
        self.send_sem, self.recv_sem = send_sem, recv_sem

    def begin(self, step):
        if self.ready is not None:
            for index in {1: (0,), 2: (1, 2)}.get(step, ()):
                pl.semaphore_wait(self.ready.at[index], 1)
        super().begin(step)

    def at(self, code, part):
        return self.block(2 * self.cube.other(code) + part)

    def moves(self, step):
        near = lambda code: {"seq": self.cube.other(code)}
        if step == 1:
            parts = [(1, 2 * i + 1, part, 2 * i + part) for i in range(4) for part in range(2)]
        elif step == 2:
            parts = [(2, 2, 0, 8), (2, 6, 0, 9), (4, 4, 1, 10), (4, 6, 1, 11)]
        else:
            parts = [(4, 4, 0, 12), (2, 2, 1, 13)]
        return [(near(to), self.at(code, part), self.spare(k), k) for to, code, part, k in parts]

    def take(self, step):
        if step == 3:
            self.finish()
            return
        if step == 1:
            parts = [(2 * i, part, 2 * i + part) for i in range(4) for part in range(2)]
        else:
            parts = [(0, 0, 8), (4, 0, 9), (0, 1, 10), (2, 1, 11)]
        for code, part, k in parts:
            here = self.at(code, part)
            here[...] = (here[...].astype(F32) + self.spare(k)[...].astype(F32)).astype(BF)

    def result(self, part):
        return self.at(0, part)[...].astype(F32) + self.spare(12 + part)[...].astype(F32)


class Small(Steps):
    last = 2

    def __init__(self, cube, array, near, planes, send_sem, recv_sem):
        self.cube, self.array, self.near, self.planes = cube, array, near, planes
        self.send_sem, self.recv_sem = send_sem, recv_sem

    def moves(self, step):
        cube = self.cube
        if step == 1:
            here = self.near.at[cube.me]
            return [({"seq": cube.other(code)}, here, here, code - 1) for code in range(1, 8)]
        here = self.planes.at[cube.level]
        return [({"batch": cube.plane(k)}, here, here, 6 + k) for k in range(1, cube.levels)]

    def begin(self, step):
        if step == 1:
            self.near[self.cube.me] = self.array[...]
        super().begin(step)

    def take(self, step):
        found = self.near if step == 1 else self.planes
        total = found[0]
        for k in range(1, found.shape[0]):
            total = total + found[k]
        if step == 1:
            self.planes[self.cube.level] = total
        else:
            self.array[...] = total


class Gather:
    def __init__(self, cube, own, slot_ref, send_sem, recv_sem):
        self.cube, self.own, self.slot_ref = cube, own, slot_ref
        self.send_sem, self.recv_sem = send_sem, recv_sem
        self.sent = []

    def push(self, step, code, part):
        slot = 2 * self.cube.other(code) + part
        target = self.slot_ref(slot)
        source = self.own.at[part] if code == 0 else target
        self.sent.append(
            self.cube.send(
                step,
                source,
                target,
                self.send_sem.at[len(self.sent)],
                self.recv_sem.at[2 * (code ^ step) + part],
            )
        )

    def take(self, code, part):
        slot = self.slot_ref(2 * self.cube.other(code) + part)
        pltpu.make_async_remote_copy(
            src_ref=slot,
            dst_ref=slot,
            send_sem=self.send_sem.at[0],
            recv_sem=self.recv_sem.at[2 * code + part],
            device_id={"seq": self.cube.other(1)},
            device_id_type=MESH,
        ).wait_recv()

    def arrived(self, code):
        for part in range(2):
            self.take(code, part)

    def open(self):
        for step, part in ((2, 0), (4, 1), (1, 0), (1, 1)):
            self.push(step, 0, part)

    def more(self):
        for step, part in ((2, 1), (4, 0)):
            self.push(step, 0, part)

    def pass_on(self):
        self.take(2, 0)
        self.push(4, 2, 0)
        self.take(4, 1)
        self.push(2, 4, 1)
        self.push(1, 2, 0)
        self.push(1, 4, 1)
        self.take(2, 1)
        self.push(1, 2, 1)
        self.take(4, 0)
        self.push(1, 4, 0)

    def finish(self):
        for part in range(2):
            self.take(6, part)
            self.push(1, 6, part)

    def close(self):
        for copy in self.sent:
            copy.wait_send()


def publish_kernel(grads, dvec, *refs):
    kept, outs, stages = refs[:3], refs[3:-8], refs[-8:-5]
    narrow, broad, load_sem, store_sem, keep_sem = refs[-5:]
    fetches = [pltpu.make_async_copy(kept[i], stages[i], keep_sem.at[i]) for i in range(3)]
    keeps = [pltpu.make_async_copy(stages[i], outs[24 + i], keep_sem.at[i]) for i in range(3)]
    order = list(range(8, 16)) + list(range(4, 8)) + list(range(4))
    loads = [pltpu.make_async_copy(grads.at[i], narrow.at[i], load_sem.at[i]) for i in order]
    ahead = 4
    for load in loads[:ahead] + fetches:
        load.start()
    for i in range(13):
        outs[10 + i][...] = dvec[i, :]
    for i in range(4):
        outs[23][i * D : (i + 1) * D] = dvec[13 + i, :]
    stores = []
    for turn, (load, i) in enumerate(zip(loads, order)):
        load.wait()
        if turn + ahead < len(loads):
            loads[turn + ahead].start()
        broad[i] = narrow[i].astype(F32)
        if i < 8:
            target = outs[i]
        elif i % 2 == 0:
            target = outs[8].at[:, pl.ds((i - 8) // 2 * D, D)]
        else:
            target = outs[9].at[pl.ds((i - 8) // 2 * D, D), :]
        store = pltpu.make_async_copy(broad.at[i], target, store_sem.at[i])
        store.start()
        stores.append(store)
    for fetch, keep in zip(fetches, keeps):
        fetch.wait()
        keep.start()
    for store in stores + keeps:
        store.wait()


def publish(grads, dvec, kept):
    vmem = pl.BlockSpec(memory_space=pltpu.VMEM)
    hbm = pl.BlockSpec(memory_space=pl.ANY)
    shapes = [(D, D)] * 8 + [(D, 4 * D), (4 * D, D)] + [(D,)] * 13 + [(4 * D,)]
    return pl.pallas_call(
        publish_kernel,
        out_shape=tuple(
            [jax.ShapeDtypeStruct(shape, F32) for shape in shapes]
            + [jax.ShapeDtypeStruct(array.shape, array.dtype) for array in kept]
        ),
        in_specs=[hbm, vmem] + [hbm] * 3,
        out_specs=tuple([hbm] * 10 + [vmem] * 14 + [hbm] * 3),
        scratch_shapes=[pltpu.VMEM(array.shape, array.dtype) for array in kept]
        + [
            pltpu.VMEM((16, D, D), BF),
            pltpu.VMEM((16, D, D), F32),
            pltpu.SemaphoreType.DMA((16,)),
            pltpu.SemaphoreType.DMA((16,)),
            pltpu.SemaphoreType.DMA((3,)),
        ],
        compiler_params=pltpu.CompilerParams(vmem_limit_bytes=64 << 20),
    )(grads, dvec, *kept)


def layer_kernel(
    sizes,
    tlen,
    slen,
    tord,
    sord,
    own_far,
    cot_far,
    own_memory,
    vectors_far,
    w_small,
    w_in,
    w_out,
    result,
    dinputs,
    dmemory,
    dvec,
    grads,
    own,
    cot,
    vectors,
    vec,
    nrm,
    memory,
    stream,
    weight,
    kv,
    queries,
    ckeys,
    cvalues,
    scores,
    powers,
    cpowers,
    inverses,
    cinverses,
    mixed,
    heard,
    unit,
    low,
    tinv,
    sinv,
    pairs,
    flats,
    edges,
    deeps,
    leaves,
    nears,
    planes,
    sem,
    send_sem,
    recv_sem,
    group_send,
    group_recv,
    group_sent,
    scatter_send,
    scatter_recv,
    small_send,
    small_recv,
    ready,
):
    rows, blocks, half, sblocks, shalf, ndoc, window = (
        sizes["rows"],
        sizes["blocks"],
        sizes["half"],
        sizes["sblocks"],
        sizes["shalf"],
        sizes["ndoc"],
        sizes["window"],
    )
    around = -(-window // half)
    pad = around * half - window
    sources = sblocks * shalf
    later = dinputs
    me = lax.axis_index("seq")
    scale = float(HDIM) ** -0.5
    thirds = half // PIECE
    cube = Cube(me, lax.axis_index("batch"), sizes["levels"])
    cube.greet()

    def raw(slot):
        return powers.at[lax.rem(slot, 4), pl.ds(lax.div(slot, 4) * thirds, thirds), :, 0:D]

    def raw_memory(slot):
        return memory.at[slot]

    gather_rows = Gather(cube, own_far, raw, send_sem.at[0], recv_sem.at[0])
    gather_sources = Gather(cube, own_memory, raw_memory, send_sem.at[1], recv_sem.at[1])
    copies = []
    for index, (source, target) in enumerate(
        [(own_far, own)]
        + list(zip(vectors_far, vectors))
        + [(w_small[i], weight.at[i]) for i in range(8)]
        + [(w_in.at[:, pl.ds(D * i, D)], weight.at[8 + 2 * i]) for i in range(4)]
        + [(w_out.at[pl.ds(D * i, D), :], weight.at[9 + 2 * i]) for i in range(4)]
        + [(cot_far, cot)]
    ):
        copy = pltpu.make_async_copy(source, target, sem.at[index])
        copy.start()
        copies.append(copy)
    cube.await_all()
    gather_rows.open()
    def deliver(turn, first):
        def go():
            pltpu.make_async_copy(
                weight.at[pl.ds(first, 4)], grads.at[pl.ds(first, 4)], sem.at[turn]
            ).start()

        return go

    groups = []
    for turn, first in enumerate((8, 12, 4, 0)):
        groups.append(
            Reduce(
                cube, weight, first, pairs.at[turn % 2], flats.at[turn % 2], edges.at[turn % 2],
                deeps.at[turn % 2], leaves.at[turn % 2], group_send.at[turn], group_recv.at[turn],
                group_sent.at[turn], groups[turn - 2] if turn > 1 else None, deliver(turn, first),
            )
        )

    def spare_block(k):
        return powers.at[k % 4, pl.ds(k // 4 * thirds, thirds), :, 0:D]

    def end_rows():
        for part in range(2):
            own_unit, own_spread = centred(own[part].reshape(half, D).astype(F32))
            dnormed = rows_back.result(part).reshape(half, D)
            here = pl.ds(part * half, half)
            dinputs[here, :] = later[here, :] + norm_back(dnormed, own_unit, own_spread, vector(0))
            dvec[0:1, :] += column_sum(dnormed * own_unit)
            dvec[1:2, :] += column_sum(dnormed)

    def end_memory():
        for part in range(2):
            dmemory[part * shalf : (part + 1) * shalf, :] = memory_back.result(part)

    rows_back = Scatter(
        cube, lambda slot: nrm.at[slot], spare_block, scatter_send.at[0], scatter_recv.at[0],
        ready, end_rows,
    )
    memory_back = Scatter(
        cube,
        lambda slot: cvalues.at[pl.ds(pl.multiple_of(slot * shalf, shalf), shalf), :],
        lambda k: memory.at[k],
        scatter_send.at[1],
        scatter_recv.at[1],
        None,
        end_memory,
    )
    smalls = [
        Small(
            cube, dvec.at[pl.ds(start, 8 * size), :],
            nears.at[:, pl.ds(start, 8 * size), :], planes.at[:, pl.ds(start, 8 * size), :],
            small_send.at[turn], small_recv.at[turn],
        )
        for turn, (start, size) in enumerate(((0, 1), (8, 2)))
    ]
    exchanges = dict(
        A=groups[0], B=groups[1], C=groups[2], E=groups[3], R=rows_back, M=memory_back,
        S=smalls[0], V=smalls[1],
    )
    counts = dict(A=9, B=9, C=9, E=9, R=4, M=4, S=3, V=3)

    def pump(point):
        for name in SCHEDULE.get(point, ""):
            counts[name] -= 1
            exchanges[name].advance()

    dvec[...] = jnp.zeros((VECTORS, D), F32)
    for order, inverse_of, count in ((tord, tinv, blocks), (sord, sinv, sblocks)):
        for t in range(count):
            found = jnp.int32(0)
            for s in range(count):
                found = jnp.where(order[0, s] == t, s, found)
            inverse_of[t] = found
    tends, sends = [], []
    tend, send = jnp.int32(0), jnp.int32(0)
    for d in range(ndoc):
        tend, send = tend + tlen[0, d], send + slen[0, d]
        tends.append(tend)
        sends.append(send)
    base = [tord[0, 2 * me + b] for b in range(2)]

    def vector(index):
        return vec[index : index + 1, :]

    for copy in copies:
        copy.wait()
    gather_rows.more()
    row = 0
    for vector_ref in vectors:
        for start in range(0, vector_ref.shape[0], D):
            vec[row : row + 1, :] = vector_ref[start : start + D].astype(F32).reshape(1, D)
            row += 1

    states = own[...].reshape(rows, D)
    own_normed = (centred(states.astype(F32))[0] * vector(0) + vector(1)).astype(BF)
    queries[...] = ((nn(own_normed, weight[0]) + vector(2)) * scale).astype(BF)

    def project_block(s, block):
        found, _ = centred(block.astype(F32))
        normed = (found * vector(0) + vector(1)).astype(BF)
        nrm[s] = normed.reshape(thirds, PIECE, D)
        keys = nn(normed, weight[1]).astype(BF)
        values = (nn(normed, weight[2]) + vector(3)).astype(BF)
        for quad in range(2):
            kv[0, quad, s] = keys[:, quad * 256 : (quad + 1) * 256]
            kv[1, quad, s] = values[:, quad * 256 : (quad + 1) * 256]

    def project(code):
        def one(part, carry):
            s = 2 * cube.other(code) + part
            project_block(s, raw(s)[...].reshape(half, D))
            return carry

        lax.fori_loop(0, 2, one, 0)

    for part in range(2):
        project_block(2 * me + part, own[part].reshape(half, D))
    gather_rows.arrived(1)
    project(1)
    gather_rows.pass_on()
    gather_sources.open()
    gather_sources.more()
    project(2)
    project(4)
    gather_rows.arrived(3)
    project(3)
    gather_rows.arrived(5)
    project(5)
    gather_rows.finish()
    project(6)
    gather_rows.arrived(7)
    project(7)
    gather_rows.close()
    gather_sources.pass_on()

    def limits(b):
        index = lax.broadcasted_iota(jnp.int32, (1, 4 * half), 1)
        row = index
        for h in range(1, 4):
            row = jnp.where(index >= h * half, index - h * half, row)
        position = base[b] * half + row
        start = jnp.zeros_like(position)
        for end in tends:
            start = jnp.where(position >= end, end, start)
        shift = (base[b] + 1) * half - window
        return start - shift, position - shift + 1

    kwin, vwin = [
        cpowers.at[kind, pl.ds(0, window // PIECE), :, pl.ds(D, 4 * HDIM)] for kind in range(2)
    ]

    def fill(b, quad):
        skip = pad // PIECE
        for j in range(around):
            slot = tinv[jnp.maximum(base[b] - (around - 1) + j, 0)]
            for kind, target in ((0, kwin), (1, vwin)):
                block = kv[kind, quad, slot].reshape(thirds, PIECE, 4 * HDIM)
                if j == 0:
                    target[0 : thirds - skip] = block[skip:]
                else:
                    target[j * thirds - skip : (j + 1) * thirds - skip] = block

    for b in range(2):
        begin, stop = limits(b)

        def forward(quad, carry, b=b, begin=begin, stop=stop):
            fill(b, quad)
            lanes = pl.ds(pl.multiple_of(quad * 256, 256), 256)
            block = queries[b * half : (b + 1) * half, lanes].astype(F32)
            out, inverse = attend(
                spread_heads(block, 4).astype(BF),
                kwin,
                vwin,
                begin,
                stop,
                scores.at[pl.ds(0, window), :],
                powers.at[b * 2 + quad],
            )
            inverses[b * 2 + quad] = jnp.broadcast_to(inverse, (8, 4 * half))
            mixed[b * half : (b + 1) * half, lanes] = join_heads(out, 4)
            return carry

        lax.fori_loop(0, 2, forward, 0)
        if b == 0:
            gather_sources.finish()

    middle = own[...].reshape(rows, D).astype(F32) + nn(mixed[...].astype(BF), weight[3]) + vector(4)
    found, spread = centred(middle)
    later[...] = middle
    unit[0] = found
    low[0] = (found * vector(5) + vector(6)).astype(BF)
    cross_spread = spread
    low[1] = ((nn(low[0], weight[4]) + vector(7)) * scale).astype(BF)

    for code in (1, 3, 5, 7):
        gather_sources.arrived(code)
    for part in range(2):
        memory[2 * me + part] = own_memory[part]
    gather_sources.close()

    def place(t, carry):
        stream[t] = memory[sinv[t]]
        return carry

    lax.fori_loop(0, sblocks, place, 0)
    step = sources // 2
    some = sblocks // 2

    def sources_of(c, carry):
        part = pl.ds(pl.multiple_of(c * step, step), step)
        block = stream[pl.ds(c * some, some)].reshape(step, D)
        ckeys[part, :] = nn(block, weight[5]).astype(BF)
        cvalues[part, :] = (nn(block, weight[6]) + vector(8)).astype(BF)
        return carry

    lax.fori_loop(0, sources // step, sources_of, 0)
    index = lax.broadcasted_iota(jnp.int32, (1, 2 * rows), 1)
    row = jnp.where(index >= rows, index - rows, index)
    position = jnp.where(row >= half, base[1] * half + row - half, base[0] * half + row)
    begin = jnp.zeros_like(position)
    stop = jnp.full_like(position, sources)
    for end, send in zip(tends, sends):
        begin = jnp.where(position >= end, send, begin)
    for end, send in reversed(list(zip(tends, sends))):
        stop = jnp.where(position < end, send, stop)

    def cross_forward(pair, carry):
        lanes = pl.ds(pl.multiple_of(pair * 128, 128), 128)
        out, inverse = attend(
            spread_heads(low[1, :, lanes].astype(F32), 2).astype(BF),
            ckeys.at[:, lanes],
            cvalues.at[:, lanes],
            begin,
            stop,
            scores,
            cpowers.at[pair],
        )
        cinverses[pair] = jnp.broadcast_to(inverse, (8, 2 * rows))
        heard[:, lanes] = join_heads(out, 2)
        return carry

    lax.fori_loop(0, 4, cross_forward, 0)
    after_cross = later[...] + nn(heard[...].astype(BF), weight[7]) + vector(9)
    found, spread = centred(after_cross)
    unit[1] = found
    final_spread = spread
    low[2] = (found * vector(10) + vector(11)).astype(BF)
    later[...] = after_cross + vector(12)

    cotangent = cot[...]
    unit[2] = jnp.zeros((rows, D), F32)

    def feed(c, carry):
        fed = low[2]
        first, second = weight[8 + 2 * c], weight[9 + 2 * c]
        before = nn(fed, first) + vec[pl.ds(13 + c, 1), :]
        cumulative = 0.5 * (1.0 + lax.erf(before * (2.0**-0.5)))
        after = (before * cumulative).astype(BF)
        slope = cumulative + before * jnp.exp(-0.5 * before * before) * ((2.0 * math.pi) ** -0.5)
        later[...] += nn(after, second)
        change = nt(cotangent, second) * slope
        change_low = change.astype(BF)
        dvec[pl.ds(13 + c, 1), :] = column_sum(change_low.astype(F32))
        unit[2] += nt(change_low, first)
        weight[8 + 2 * c] = tn(fed, change_low).astype(BF)
        weight[9 + 2 * c] = tn(after, cotangent).astype(BF)

        @pl.when(c == 1)
        def _():
            pump("half")

        return carry

    lax.fori_loop(0, 4, feed, 0)
    pump("feed")
    result[...] = later[...].astype(BF)
    cot_f = cotangent.astype(F32)
    dvec[12:13, :] = column_sum(cot_f)
    dfed = unit[2]
    dvec[10:11, :] = column_sum(dfed * unit[1])
    dvec[11:12, :] = column_sum(dfed)
    dlater = cot_f + norm_back(dfed, unit[1], final_spread, vector(10))
    later[...] = dlater
    branch = dlater.astype(BF)
    dvec[9:10, :] = column_sum(branch.astype(F32))
    dheard = nt(branch, weight[7]).astype(BF)
    weight[7] = tn(heard[...].astype(BF), branch).astype(BF)
    low[2] = dheard
    heard[...] = heard[...] * dheard.astype(F32)
    pump("heard")

    def cross_backward(pair, carry):
        lanes = pl.ds(pl.multiple_of(pair * 128, 128), 128)

        def store(c, dkeys, dvalues):
            part = pl.ds(pl.multiple_of(c * dkeys.shape[0], dkeys.shape[0]), dkeys.shape[0])
            scores[part, 0:128] = dkeys
            cvalues[part, lanes] = dvalues.astype(BF)

        out = attend_back(
            spread_heads(low[1, :, lanes].astype(F32), 2).astype(BF),
            spread_heads(low[2, :, lanes].astype(F32), 2).astype(BF),
            spread_heads(heard[:, lanes], 2),
            ckeys.at[:, lanes],
            cvalues.at[:, lanes],
            cinverses[pair, 0:1, :],
            cpowers.at[pair],
            store,
        )
        ckeys[:, lanes] = scores[:, 0:128].astype(BF)
        unit[1, :, lanes] = join_heads(out, 2)

        for index in range(4):

            @pl.when(pair == index)
            def _(index=index):
                pump("pair" + str(index))

        return carry

    lax.fori_loop(0, 4, cross_backward, 0)

    dvec[8:9, :] = column_sum(cvalues[...].astype(F32))
    block = stream[...].reshape(sources, D)
    fresh = [tn(block, ckeys[...]).astype(BF), tn(block, cvalues[...]).astype(BF)]

    pump("sums")

    def sources_back(c, carry):
        part = pl.ds(pl.multiple_of(c * step, step), step)
        back = nt(ckeys[part, :], weight[5]) + nt(cvalues[part, :], weight[6])
        stream[pl.ds(c * some, some)] = back.astype(BF).reshape(some, shalf, D)
        return carry

    lax.fori_loop(0, sources // step, sources_back, 0)
    weight[5] = fresh[0]
    weight[6] = fresh[1]

    def place_back(s, carry):
        there = pl.ds(pl.multiple_of(s * shalf, shalf), shalf)
        cvalues[there, :] = stream[sord[0, s]]
        return carry

    lax.fori_loop(0, sblocks, place_back, 0)
    pump("sources")
    ckeys[0:D, :] = weight[1]
    ckeys[D : 2 * D, :] = weight[2]

    dcq = unit[1].astype(BF)
    dvec[7:8, :] = column_sum(dcq.astype(F32)) * scale
    dcrossed = nt(dcq, weight[4]) * scale
    weight[4] = (tn(low[0], dcq) * scale).astype(BF)
    dvec[5:6, :] = column_sum(dcrossed * unit[0])
    dvec[6:7, :] = column_sum(dcrossed)
    dmid = later[...] + norm_back(dcrossed, unit[0], cross_spread, vector(5))
    later[...] = dmid
    branch = dmid.astype(BF)
    dvec[4:5, :] = column_sum(branch.astype(F32))
    dmixed = nt(branch, weight[3]).astype(BF)
    weight[3] = tn(mixed[...].astype(BF), branch).astype(BF)
    low[2] = dmixed
    mixed[...] = mixed[...] * dmixed.astype(F32)
    pump("middle")

    for b in range(2):
        for kind in range(2):
            if pad:
                cpowers[2 * kind + b, 0 : pad // PIECE, :, 0:D] = jnp.zeros((pad // PIECE, PIECE, D), BF)

        def backward(quad, carry, b=b):
            fill(b, quad)
            lanes = pl.ds(pl.multiple_of(quad * 256, 256), 256)

            def store(c, dkeys, dvalues):
                pieces = dkeys.shape[0] // PIECE
                part = pl.ds(c * pieces + pad // PIECE, pieces)
                cpowers[b, part, :, lanes] = dkeys.astype(BF).reshape(pieces, PIECE, 256)
                cpowers[2 + b, part, :, lanes] = dvalues.astype(BF).reshape(pieces, PIECE, 256)

            out = attend_back(
                spread_heads(queries[b * half : (b + 1) * half, lanes].astype(F32), 4).astype(BF),
                spread_heads(low[2, b * half : (b + 1) * half, lanes].astype(F32), 4).astype(BF),
                spread_heads(mixed[b * half : (b + 1) * half, lanes], 4),
                kwin,
                vwin,
                inverses[b * 2 + quad, 0:1, :],
                powers.at[b * 2 + quad],
                store,
            )
            unit[1, b * half : (b + 1) * half, lanes] = join_heads(out, 4)

            for index in range(2):

                @pl.when(quad == index)
                def _(index=index):
                    pump("self" + str(2 * b + index))

            return carry

        lax.fori_loop(0, 2, backward, 0)

        ratio = half // shalf
        for j in range(around):
            slot = tinv[jnp.maximum(base[b] - (around - 1) + j, 0)]
            stream[j * ratio : (j + 1) * ratio] = nrm[slot].reshape(ratio, shalf, D)
        normed = stream[0 : around * ratio].reshape(around * half, D)
        for kind in range(2):
            change = cpowers[2 * kind + b, 0 : around * thirds, :, 0:D].reshape(around * half, D)
            if kind == 1:
                dvec[3:4, :] += column_sum(change.astype(F32))
            total = tn(normed, change)
            there = slice(kind * D, (kind + 1) * D)
            if b == 0:
                scores[there, 0:D] = total
            else:
                weight[1 + kind] = (scores[there, 0:D] + total).astype(BF)
        if b == 0:
            pump("window")
    for index in range(3):
        pl.semaphore_signal(
            ready.at[index],
            inc=1,
            device_id={"seq": cube.other(1 << index)},
            device_id_type=MESH,
        )

    dq = unit[1].astype(BF)
    dvec[2:3, :] = column_sum(dq.astype(F32)) * scale
    heard[...] = nt(dq, weight[0]) * scale
    own_normed = nrm[pl.ds(2 * me, 2)].reshape(rows, D)
    weight[0] = (tn(own_normed, dq) * scale).astype(BF)

    pump("weights")

    for b in range(2):

        def through(c, carry, b=b):
            part = pl.ds(c * around, around)
            dkeys = cpowers[b, part, :, 0:D].reshape(around * PIECE, D)
            dvalues = cpowers[2 + b, part, :, 0:D].reshape(around * PIECE, D)
            total = nt(dkeys, ckeys[0:D, :]) + nt(dvalues, ckeys[D : 2 * D, :])
            cpowers[b, part, :, 0:D] = total.astype(BF).reshape(around, PIECE, D)
            return carry

        lax.fori_loop(0, thirds, through, 0)
        pump("through" + str(b))

    def assemble(code):
        def one(part, carry):
            s = 2 * cube.other(code) + part
            for third in range(thirds):
                total = jnp.zeros((PIECE, D), F32)
                for b in range(2):
                    back = base[b] - tord[0, s]
                    inside = (back >= 0) & (back < around)
                    first = jnp.clip(around - 1 - back, 0, around - 1) * thirds
                    found = cpowers[b, first + third][:, 0:D]
                    total = total + jnp.where(inside, found.astype(F32), 0.0)
                if code == 0:
                    start = pl.multiple_of(part * half + third * PIECE, PIECE)
                    total = total + heard[pl.ds(start, PIECE), :]
                nrm[s, third] = total.astype(BF)
            return carry

        lax.fori_loop(0, 2, one, 0)

    for code in (1, 3, 5, 7):
        assemble(code)
    pump("theirs")
    for code in (6, 2, 4, 0):
        assemble(code)
    pump("end")
    assert not any(counts.values()), counts
    for turn, first in enumerate((8, 12, 4, 0)):
        pltpu.make_async_copy(
            weight.at[pl.ds(first, 4)], grads.at[pl.ds(first, 4)], sem.at[turn]
        ).wait()


def layer_call(sizes, small_ints, own, cot, own_memory, vectors, w_small, w_in, w_out):
    rows, blocks, half, sblocks, shalf, window = (
        sizes["rows"],
        sizes["blocks"],
        sizes["half"],
        sizes["sblocks"],
        sizes["shalf"],
        sizes["window"],
    )
    sources = sblocks * shalf
    levels = sizes["levels"]
    vmem = pl.BlockSpec(memory_space=pltpu.VMEM)
    smem = pl.BlockSpec(memory_space=pltpu.SMEM)
    hbm = pl.BlockSpec(memory_space=pl.ANY)

    count = len(vectors)

    def body(*refs):
        head, rest = refs[:7], refs[7:]
        vector_refs, rest = rest[:count], rest[count:]
        scratch = rest[17:]
        layer_kernel(
            sizes, *head, vector_refs, rest[:8], *rest[8:15],
            *rest[15:17], scratch[:count], *scratch[count:],
        )

    return pl.pallas_call(
        body,
        out_shape=(
            jax.ShapeDtypeStruct((rows, D), BF),
            jax.ShapeDtypeStruct((rows, D), F32),
            jax.ShapeDtypeStruct((2 * shalf, D), F32),
            jax.ShapeDtypeStruct((VECTORS, D), F32),
            jax.ShapeDtypeStruct((16, D, D), BF),
        ),
        in_specs=[smem] * 4 + [hbm] * 2 + [vmem] + [hbm] * (count + 10),
        out_specs=(vmem, vmem, vmem, vmem, hbm),
        scratch_shapes=[pltpu.VMEM(own.shape, BF), pltpu.VMEM(cot.shape, BF)]
        + [pltpu.VMEM(vector.shape, BF) for vector in vectors]
        + [
            pltpu.VMEM((VECTORS, D), F32),
            pltpu.VMEM((blocks, half // PIECE, PIECE, D), BF),
            pltpu.VMEM((sblocks, shalf, D), BF),
            pltpu.VMEM((sblocks, shalf, D), BF),
            pltpu.VMEM((16, D, D), BF),
            pltpu.VMEM((2, 2, blocks, half, 256), BF),
            pltpu.VMEM((rows, D), BF),
            pltpu.VMEM((sources, D), BF),
            pltpu.VMEM((sources, D), BF),
            pltpu.VMEM((sources, 2 * rows), F32),
            pltpu.VMEM((4, window // PIECE, PIECE, 4 * half), BF),
            pltpu.VMEM((4, sources // PIECE, PIECE, 2 * rows), BF),
            pltpu.VMEM((4, 8, 4 * half), F32),
            pltpu.VMEM((4, 8, 2 * rows), F32),
            pltpu.VMEM((rows, D), F32),
            pltpu.VMEM((rows, D), F32),
            pltpu.VMEM((3, rows, D), F32),
            pltpu.VMEM((3, rows, D), BF),
            pltpu.SMEM((blocks,), jnp.int32),
            pltpu.SMEM((sblocks,), jnp.int32),
            pltpu.VMEM((2, 4, D // 2, D), BF),
            pltpu.VMEM((2, 2, 4, D // 8, D), BF),
            pltpu.VMEM((2, 2, 4, D // 16, D), BF),
            pltpu.VMEM((2, levels - 1, 2, D // 16, D), BF),
            pltpu.VMEM((2, levels - 1, 2, D // 16, D), BF),
            pltpu.VMEM((8, VECTORS, D), F32),
            pltpu.VMEM((levels, VECTORS, D), F32),
            pltpu.SemaphoreType.DMA((32,)),
            pltpu.SemaphoreType.DMA((2, 16)),
            pltpu.SemaphoreType.DMA((2, 16)),
            pltpu.SemaphoreType.DMA((4, 22)),
            pltpu.SemaphoreType.DMA((4, 22)),
            pltpu.SemaphoreType.REGULAR((4, 3)),
            pltpu.SemaphoreType.DMA((2, 14)),
            pltpu.SemaphoreType.DMA((2, 14)),
            pltpu.SemaphoreType.DMA((2, 10)),
            pltpu.SemaphoreType.DMA((2, 10)),
            pltpu.SemaphoreType.REGULAR((3,)),
        ],
        compiler_params=pltpu.CompilerParams(
            vmem_limit_bytes=64 << 20, collective_id=0, has_side_effects=True
        ),
    )(*small_ints, own, cot, own_memory, *vectors, *w_small, w_in, w_out)


def fused_on_device(
    inputs, memory, target_lengths, source_lengths, target_order, source_order,
    self_gain, self_shift, self_query, query_bias, self_key, self_value, value_bias,
    self_output, output_bias, cross_gain, cross_shift, cross_query, cquery_bias, cross_key,
    cross_value, cvalue_bias, cross_output, coutput_bias, final_gain, final_shift,
    inner_weight, inner_bias, outer_weight, outer_bias, cotangent,
):
    rows = inputs.shape[1]
    blocks = target_order.shape[1]
    sblocks = source_order.shape[1]
    ranks = lax.axis_size("seq")
    half = ranks * rows // blocks
    shalf = ranks * memory.shape[1] // sblocks
    ndoc = target_lengths.shape[1]
    reach = max(LONGEST, blocks * half - LONGEST - SHORTEST * (ndoc - 1))
    window = -(-(reach - 1 + half) // CHUNK) * CHUNK
    sizes = dict(
        rows=rows, blocks=blocks, half=half, sblocks=sblocks, shalf=shalf, ndoc=ndoc, window=window,
        levels=lax.axis_size("batch"),
    )
    result, dinputs, dmemory, dvec, grads = layer_call(
        sizes, (target_lengths, source_lengths, target_order, source_order),
        inputs.reshape(2, half // PIECE, PIECE, D), cotangent[0], memory.reshape(2, shalf, D),
        (
            self_gain, self_shift, query_bias, value_bias, output_bias, cross_gain, cross_shift,
            cquery_bias, cvalue_bias, coutput_bias, final_gain, final_shift, outer_bias, inner_bias,
        ),
        (self_query, self_key, self_value, self_output, cross_query, cross_key, cross_value, cross_output),
        inner_weight, outer_weight,
    )
    made = publish(grads, dvec, (result, dinputs, dmemory))
    result, dinputs, dmemory = made[24:]
    squares, wide, tall, rows_of, units = made[:8], made[8], made[9], made[10:23], made[23]
    return (
        result[None], dinputs[None], dmemory[None],
        rows_of[0], rows_of[1], squares[0], rows_of[2], squares[1], squares[2], rows_of[3],
        squares[3], rows_of[4], rows_of[5], rows_of[6], squares[4], rows_of[7], squares[5],
        squares[6], rows_of[8], squares[7], rows_of[9], rows_of[10], rows_of[11],
        wide, units, tall, rows_of[12],
    )


def solution(mesh):
    in_specs = (
        P("batch", "seq", None),
        P("batch", "seq", None),
        P("batch", None),
        P("batch", None),
        P("batch", None),
        P("batch", None),
        P(),
        P(),
        P(),
        P(),
        P(),
        P(),
        P(),
        P(),
        P(),
        P(),
        P(),
        P(),
        P(),
        P(),
        P(),
        P(),
        P(),
        P(),
        P(),
        P(),
        P(),
        P(),
        P(),
        P(),
        P("batch", "seq", None),
    )
    out_specs = (
        P("batch", "seq", None),
        P("batch", "seq", None),
        P("batch", "seq", None),
        P(),
        P(),
        P(),
        P(),
        P(),
        P(),
        P(),
        P(),
        P(),
        P(),
        P(),
        P(),
        P(),
        P(),
        P(),
        P(),
        P(),
        P(),
        P(),
        P(),
        P(),
        P(),
        P(),
        P(),
    )
    return jax.shard_map(
        fused_on_device if (mesh.shape["seq"], mesh.shape["batch"]) == (8, 4) else on_device,
        mesh=mesh, in_specs=in_specs, out_specs=out_specs, check_vma=False,
    )
```

```python
import math

import jax
import jax.numpy as jnp
from jax import lax
from jax.experimental import pallas as pl
from jax.experimental.pallas import tpu as pltpu
from jax.sharding import PartitionSpec as P

D = 512
HEADS = 8


EPSILON = 1e-05
NEGATIVE = -1e30


def norm(values, gain, shift):
    center = values - jnp.mean(values, axis=-1, keepdims=True)
    spread = jnp.mean(center * center, axis=-1, keepdims=True)
    return center * lax.rsqrt(spread + EPSILON) * gain + shift


def product(left, right):
    return jnp.dot(left, right, preferred_element_type=jnp.float32)


def weight_grad(left, right):
    return jnp.einsum("ti,to->io", left, right, preferred_element_type=jnp.float32)


def input_grad(grad, weight):
    return jnp.einsum("to,io->ti", grad, weight, preferred_element_type=jnp.float32)


def split_heads(values):
    return values.reshape(values.shape[0], HEADS, -1)


def locate(order, lengths, blocksize, start, count):
    index = start + jnp.arange(count, dtype=jnp.int32)
    slot = index // blocksize
    picked = jnp.sum(
        jnp.where(
            slot[:, None] == jnp.arange(order.shape[0], dtype=jnp.int32)[None, :], order[None, :], 0
        ),
        axis=1,
    )
    position = picked * blocksize + index % blocksize
    ends = jnp.cumsum(lengths)
    document = jnp.sum((position[:, None] >= ends[None, :]).astype(jnp.int32), axis=1)
    return (document, position)


def visible(query_doc, query_pos, key_doc, key_pos, causal):
    same = query_doc[:, None] == key_doc[None, :]
    if causal:
        return same & (key_pos[None, :] <= query_pos[:, None])
    return same


def opening(rows):
    return (
        jnp.zeros((rows, HEADS, D // HEADS), jnp.float32),
        jnp.full((rows, HEADS), NEGATIVE, jnp.float32),
        jnp.zeros((rows, HEADS), jnp.float32),
    )


def online(carry, query_heads, piece_keys, piece_values, allowed):
    weighted, highest, total = carry
    scores = jnp.einsum(
        "qhd,khd->qhk", query_heads, split_heads(piece_keys), preferred_element_type=jnp.float32
    )
    allowed = allowed[:, None, :]
    raised = jnp.maximum(highest, jnp.max(jnp.where(allowed, scores, NEGATIVE), axis=-1))
    powers = jnp.exp(jnp.where(allowed, scores - raised[..., None], NEGATIVE))
    total = jnp.sum(powers, axis=-1)
    weighted = jnp.einsum(
        "qhk,khd->qhd",
        powers.astype(jnp.bfloat16),
        split_heads(piece_values),
        preferred_element_type=jnp.float32,
    )
    return (weighted, raised, total)


def finish(carry):
    weighted, highest, total = carry
    return (highest + jnp.log(total), (weighted / total[..., None]).reshape(weighted.shape[0], D))


def block_back(query_heads, grad_heads, log_total, delta, piece_keys, piece_values, allowed):
    key_heads = split_heads(piece_keys)
    value_heads = split_heads(piece_values)
    scores = jnp.einsum("qhd,khd->qhk", query_heads, key_heads, preferred_element_type=jnp.float32)
    weights = jnp.exp(jnp.where(allowed[:, None, :], scores - log_total[..., None], NEGATIVE))
    grad_weights = jnp.einsum(
        "qhd,khd->qhk", grad_heads, value_heads, preferred_element_type=jnp.float32
    )
    grad_scores = (weights * (grad_weights - delta[..., None])).astype(jnp.bfloat16)
    grad_values = jnp.einsum(
        "qhk,qhd->khd", weights.astype(jnp.bfloat16), grad_heads, preferred_element_type=jnp.float32
    )
    grad_keys = jnp.einsum(
        "qhk,qhd->khd", grad_scores, query_heads, preferred_element_type=jnp.float32
    )
    grad_query = jnp.einsum(
        "qhk,khd->qhd", grad_scores, key_heads, preferred_element_type=jnp.float32
    )
    return (grad_query, grad_keys, grad_values)


def scan_back(
    query_heads,
    grad_heads,
    log_total,
    delta,
    all_keys,
    all_values,
    row_doc,
    row_pos,
    order,
    lengths,
    blocksize,
    causal,
):
    total_keys = all_keys.shape[0]
    width = math.gcd(total_keys, 512)
    count = total_keys // width

    def step(grad_query, item):
        block_keys, block_values, number = item
        key_doc, key_pos = locate(order, lengths, blocksize, number * width, width)
        allowed = visible(row_doc, row_pos, key_doc, key_pos, causal)
        query_term, key_term, value_term = block_back(
            query_heads, grad_heads, log_total, delta, block_keys, block_values, allowed
        )
        return (grad_query + query_term, (key_term, value_term))

    grad_query, (grad_keys, grad_values) = lax.scan(
        step,
        jnp.zeros(query_heads.shape, jnp.float32),
        (
            all_keys.reshape(count, width, D),
            all_values.reshape(count, width, D),
            jnp.arange(count, dtype=jnp.int32),
        ),
    )
    return (grad_query, grad_keys.reshape(total_keys, D), grad_values.reshape(total_keys, D))


def on_device(
    inputs,
    memory,
    target_lengths,
    source_lengths,
    target_order,
    source_order,
    self_gain,
    self_shift,
    self_query,
    query_bias,
    self_key,
    self_value,
    value_bias,
    self_output,
    output_bias,
    cross_gain,
    cross_shift,
    cross_query,
    cquery_bias,
    cross_key,
    cross_value,
    cvalue_bias,
    cross_output,
    coutput_bias,
    final_gain,
    final_shift,
    inner_weight,
    inner_bias,
    outer_weight,
    outer_bias,
    cotangent,
):
    rows = inputs.shape[1]
    sources = memory.shape[1]
    target_half = rows // 2
    source_half = sources // 2
    own_lengths = target_lengths[0]
    memory_lengths = source_lengths[0]
    own_order = target_order[0]
    memory_order = source_order[0]
    scale = float(D // HEADS) ** (-0.5)
    place = lax.axis_index("seq")
    row_doc, row_pos = locate(own_order, own_lengths, target_half, place * rows, rows)
    inputs_f = inputs[0].astype(jnp.float32)
    encoded = memory[0]
    normed, norm_back = jax.vjp(
        norm, inputs_f, self_gain.astype(jnp.float32), self_shift.astype(jnp.float32)
    )
    normed_low = normed.astype(jnp.bfloat16)
    queries = ((product(normed_low, self_query) + query_bias) * scale).astype(jnp.bfloat16)
    keys = product(normed_low, self_key).astype(jnp.bfloat16)
    values = (product(normed_low, self_value) + value_bias).astype(jnp.bfloat16)
    query_heads = split_heads(queries)
    piece = (
        lax.all_gather(keys, "seq", axis=0, tiled=True),
        lax.all_gather(values, "seq", axis=0, tiled=True),
    )
    key_doc, key_pos = locate(own_order, own_lengths, target_half, jnp.int32(0), piece[0].shape[0])
    self_carry = online(
        opening(rows),
        query_heads,
        piece[0],
        piece[1],
        visible(row_doc, row_pos, key_doc, key_pos, True),
    )
    self_total, mixed = finish(self_carry)
    mixed_low = mixed.astype(jnp.bfloat16)
    middle = inputs_f + product(mixed_low, self_output) + output_bias
    crossed, cross_back = jax.vjp(
        norm, middle, cross_gain.astype(jnp.float32), cross_shift.astype(jnp.float32)
    )
    crossed_low = crossed.astype(jnp.bfloat16)
    cqueries = ((product(crossed_low, cross_query) + cquery_bias) * scale).astype(jnp.bfloat16)
    ckeys = product(encoded, cross_key).astype(jnp.bfloat16)
    cvalues = (product(encoded, cross_value) + cvalue_bias).astype(jnp.bfloat16)
    cquery_heads = split_heads(cqueries)
    piece = (
        lax.all_gather(ckeys, "seq", axis=0, tiled=True),
        lax.all_gather(cvalues, "seq", axis=0, tiled=True),
    )
    key_doc, key_pos = locate(
        memory_order, memory_lengths, source_half, jnp.int32(0), piece[0].shape[0]
    )
    cross_carry = online(
        opening(rows),
        cquery_heads,
        piece[0],
        piece[1],
        visible(row_doc, row_pos, key_doc, key_pos, False),
    )
    cross_total, heard = finish(cross_carry)
    heard_low = heard.astype(jnp.bfloat16)
    later = middle + product(heard_low, cross_output) + coutput_bias
    fed, final_back = jax.vjp(
        norm, later, final_gain.astype(jnp.float32), final_shift.astype(jnp.float32)
    )
    fed_low = fed.astype(jnp.bfloat16)
    before = product(fed_low, inner_weight) + inner_bias
    after, gelu_back = jax.vjp(lambda entry: jax.nn.gelu(entry, approximate=False), before)
    after_low = after.astype(jnp.bfloat16)
    result = later + product(after_low, outer_weight) + outer_bias
    grad_out = cotangent[0]
    outer_weight_grad = weight_grad(after_low, grad_out)
    outer_bias_grad = jnp.sum(grad_out.astype(jnp.float32), axis=0)
    grad_after = input_grad(grad_out, outer_weight)
    grad_before = gelu_back(grad_after)[0].astype(jnp.bfloat16)
    inner_weight_grad = weight_grad(fed_low, grad_before)
    inner_bias_grad = jnp.sum(grad_before.astype(jnp.float32), axis=0)
    grad_fed = input_grad(grad_before, inner_weight)
    grad_later_norm, final_gain_grad, final_shift_grad = final_back(grad_fed)
    grad_later = cotangent[0].astype(jnp.float32) + grad_later_norm
    grad_cbranch = grad_later.astype(jnp.bfloat16)
    cross_output_grad = weight_grad(heard_low, grad_cbranch)
    coutput_bias_grad = jnp.sum(grad_cbranch.astype(jnp.float32), axis=0)
    grad_heard = input_grad(grad_cbranch, cross_output).astype(jnp.bfloat16)
    grad_heard_heads = split_heads(grad_heard)
    cross_delta = jnp.sum(grad_heard_heads.astype(jnp.float32) * split_heads(heard), axis=-1)
    all_ckeys, all_cvalues = (
        lax.all_gather(ckeys, "seq", axis=0, tiled=True),
        lax.all_gather(cvalues, "seq", axis=0, tiled=True),
    )
    grad_cq, part_ckeys, part_cvalues = scan_back(
        cquery_heads,
        grad_heard_heads,
        cross_total,
        cross_delta,
        all_ckeys,
        all_cvalues,
        row_doc,
        row_pos,
        memory_order,
        memory_lengths,
        source_half,
        False,
    )
    own_ckeys, own_cvalues = (
        lax.psum_scatter(
            part_ckeys.astype(jnp.bfloat16), "seq", scatter_dimension=0, tiled=True
        ).astype(jnp.float32),
        lax.psum_scatter(
            part_cvalues.astype(jnp.bfloat16), "seq", scatter_dimension=0, tiled=True
        ).astype(jnp.float32),
    )
    own_ckeys_low = own_ckeys.astype(jnp.bfloat16)
    own_cvalues_low = own_cvalues.astype(jnp.bfloat16)
    cross_key_grad = weight_grad(encoded, own_ckeys_low)
    cross_value_grad = weight_grad(encoded, own_cvalues_low)
    cvalue_bias_grad = jnp.sum(own_cvalues_low.astype(jnp.float32), axis=0)
    memory_grad = input_grad(own_ckeys_low, cross_key) + input_grad(own_cvalues_low, cross_value)
    grad_cq_low = grad_cq.reshape(rows, D).astype(jnp.bfloat16)
    cross_query_grad = weight_grad(crossed_low, grad_cq_low) * scale
    cquery_bias_grad = jnp.sum(grad_cq_low.astype(jnp.float32), axis=0) * scale
    grad_crossed = input_grad(grad_cq_low, cross_query) * scale
    grad_middle_norm, cross_gain_grad, cross_shift_grad = cross_back(grad_crossed)
    grad_middle = grad_later + grad_middle_norm
    grad_sbranch = grad_middle.astype(jnp.bfloat16)
    self_output_grad = weight_grad(mixed_low, grad_sbranch)
    output_bias_grad = jnp.sum(grad_sbranch.astype(jnp.float32), axis=0)
    grad_mixed = input_grad(grad_sbranch, self_output).astype(jnp.bfloat16)
    grad_mixed_heads = split_heads(grad_mixed)
    self_delta = jnp.sum(grad_mixed_heads.astype(jnp.float32) * split_heads(mixed), axis=-1)
    all_keys, all_values = (
        lax.all_gather(keys, "seq", axis=0, tiled=True),
        lax.all_gather(values, "seq", axis=0, tiled=True),
    )
    grad_q, part_keys, part_values = scan_back(
        query_heads,
        grad_mixed_heads,
        self_total,
        self_delta,
        all_keys,
        all_values,
        row_doc,
        row_pos,
        own_order,
        own_lengths,
        target_half,
        True,
    )
    own_keys, own_values = (
        lax.psum_scatter(
            part_keys.astype(jnp.bfloat16), "seq", scatter_dimension=0, tiled=True
        ).astype(jnp.float32),
        lax.psum_scatter(
            part_values.astype(jnp.bfloat16), "seq", scatter_dimension=0, tiled=True
        ).astype(jnp.float32),
    )
    own_keys_low = own_keys.astype(jnp.bfloat16)
    own_values_low = own_values.astype(jnp.bfloat16)
    self_key_grad = weight_grad(normed_low, own_keys_low)
    self_value_grad = weight_grad(normed_low, own_values_low)
    value_bias_grad = jnp.sum(own_values_low.astype(jnp.float32), axis=0)
    grad_q_low = grad_q.reshape(rows, D).astype(jnp.bfloat16)
    self_query_grad = weight_grad(normed_low, grad_q_low) * scale
    query_bias_grad = jnp.sum(grad_q_low.astype(jnp.float32), axis=0) * scale
    grad_normed = (
        input_grad(grad_q_low, self_query) * scale
        + input_grad(own_keys_low, self_key)
        + input_grad(own_values_low, self_value)
    )
    grad_in_norm, self_gain_grad, self_shift_grad = norm_back(grad_normed)
    inputs_grad = grad_middle + grad_in_norm
    summed = lax.psum(
        (
            self_gain_grad,
            self_shift_grad,
            self_query_grad,
            query_bias_grad,
            self_key_grad,
            self_value_grad,
            value_bias_grad,
            self_output_grad,
            output_bias_grad,
            cross_gain_grad,
            cross_shift_grad,
            cross_query_grad,
            cquery_bias_grad,
            cross_key_grad,
            cross_value_grad,
            cvalue_bias_grad,
            cross_output_grad,
            coutput_bias_grad,
            final_gain_grad,
            final_shift_grad,
            inner_weight_grad,
            inner_bias_grad,
            outer_weight_grad,
            outer_bias_grad,
        ),
        ("seq", "batch"),
    )
    return (result.astype(jnp.bfloat16)[None], inputs_grad[None], memory_grad[None]) + tuple(summed)


HDIM = D // HEADS
SHORTEST = 32
LONGEST = 1024
CHUNK = 256
PIECE = 64

GROUPS = ((8, 4), (12, 4), (3, 5), (0, 3))
SCHEDULE = dict(
    half="A",
    feed="A",
    heard="B",
    pair1="AB",
    pair3="A",
    sums="V",
    sources="MB",
    middle="ACM",
    self0="CB",
    window="AM",
    self2="BCA",
    weights="CEB",
    through0="EA",
    through1="BA",
    theirs="RV",
    end="CEREVCRBECRESBEMCSCESE",
)
MESH = pl.DeviceIdType.MESH
PARTS = 2
BF = jnp.bfloat16
F32 = jnp.float32
VECTORS = 24


def nn(left, right):
    return lax.dot_general(left, right, (((1,), (0,)), ((), ())), preferred_element_type=F32)


def nt(left, right):
    return lax.dot_general(left, right, (((1,), (1,)), ((), ())), preferred_element_type=F32)


def tn(left, right):
    return lax.dot_general(left, right, (((0,), (0,)), ((), ())), preferred_element_type=F32)


def centred(values):
    center = values - jnp.mean(values, axis=-1, keepdims=True)
    spread = lax.rsqrt(jnp.mean(center * center, axis=-1, keepdims=True) + EPSILON)
    return center * spread, spread


def norm_back(grad, unit, spread, gain):
    scaled = grad * gain
    return spread * (
        scaled
        - jnp.mean(scaled, axis=-1, keepdims=True)
        - unit * jnp.mean(scaled * unit, axis=-1, keepdims=True)
    )


def column_sum(values):
    return jnp.sum(values, axis=0, keepdims=True)


def spread_heads(block, heads):
    lane = lax.broadcasted_iota(jnp.int32, block.shape, 1)
    return jnp.concatenate(
        [
            jnp.where((lane >= h * HDIM) & (lane < (h + 1) * HDIM), block, 0.0)
            for h in range(heads)
        ],
        axis=0,
    )


def join_heads(stacked, heads):
    rows = stacked.shape[0] // heads
    lane = lax.broadcasted_iota(jnp.int32, (rows, stacked.shape[1]), 1)
    total = stacked[:rows]
    for h in range(1, heads):
        total = jnp.where(lane >= h * HDIM, stacked[h * rows : (h + 1) * rows], total)
    return total


def part_of(array, index, size):
    if len(array.shape) == 3:
        count = size // PIECE
        return array[pl.ds(index * count, count)].reshape(size, array.shape[2])
    return array[pl.ds(pl.multiple_of(index * size, size), size), :]


def whole_of(array):
    return array[...].reshape(-1, array.shape[-1])


def attend(queries, keys, values, low, high, scores, powers):
    total = math.prod(keys.shape[:-1])
    width = queries.shape[0]
    chunk = total // PARTS
    pieces = chunk // PIECE

    def first(c, highest):
        rows = pl.ds(pl.multiple_of(c * chunk, chunk), chunk)
        place = lax.broadcasted_iota(jnp.int32, (chunk, width), 0) - (low - c * chunk)
        found = jnp.where(
            place.astype(jnp.uint32) < length, nt(part_of(keys, c, chunk), queries), NEGATIVE
        )
        scores[rows, :] = found
        return jnp.maximum(highest, jnp.max(found, axis=0, keepdims=True))

    length = (high - low).astype(jnp.uint32)
    highest = lax.fori_loop(0, total // chunk, first, jnp.full((1, width), NEGATIVE, F32))

    def second(c, summed):
        rows = pl.ds(pl.multiple_of(c * chunk, chunk), chunk)
        power = jnp.exp(scores[rows, :] - highest)
        powers[pl.ds(c * pieces, pieces)] = power.astype(BF).reshape(pieces, PIECE, width)
        return summed + column_sum(power)

    summed = lax.fori_loop(0, total // chunk, second, jnp.zeros((1, width), F32))
    inverse = 1.0 / summed
    mixed = tn(whole_of(values), powers[0 : total // PIECE].reshape(total, width)) * inverse
    return mixed.T, inverse


def attend_back(queries, grads, product_of, keys, values, inverse, powers, store):
    total = math.prod(keys.shape[:-1])
    width = queries.shape[0]
    chunk = total // PARTS
    pieces = chunk // PIECE
    ones = jnp.ones((8, queries.shape[1]), BF)
    coarse = product_of.astype(BF)
    fine = (product_of - coarse.astype(F32)).astype(BF)
    delta = (nt(ones, coarse) + nt(ones, fine))[0:1]

    def step(c, carry):
        part = pl.ds(c * pieces, pieces)
        weights = powers[part].reshape(chunk, width).astype(F32) * inverse
        weights_low = weights.astype(BF)
        change = (weights * (nt(part_of(values, c, chunk), grads) - delta)).astype(BF)
        powers[part] = change.reshape(pieces, PIECE, width)
        store(c, nn(change, queries), nn(weights_low, grads))
        return carry

    lax.fori_loop(0, total // chunk, step, 0)
    return tn(whole_of(keys), powers[0 : total // PIECE].reshape(total, width)).T


class Cube:
    def __init__(self, me, level, levels):
        self.me, self.level, self.levels = me, level, levels
        self.bits = (lax.rem(me, 2), lax.rem(lax.div(me, 2), 2), lax.div(me, 4))

    def other(self, code):
        place = self.me
        for axis in range(3):
            if code >> axis & 1:
                place = place + (1 << axis) * (1 - 2 * self.bits[axis])
        return place

    def plane(self, step):
        return lax.rem(self.level + step, self.levels)

    def greet(self):
        barrier = pltpu.get_barrier_semaphore()
        for code in range(1, 8):
            pl.semaphore_signal(
                barrier, inc=1, device_id={"seq": self.other(code)}, device_id_type=MESH
            )
        for step in range(1, self.levels):
            pl.semaphore_signal(
                barrier, inc=1, device_id={"batch": self.plane(step)}, device_id_type=MESH
            )

    def await_all(self):
        pl.semaphore_wait(pltpu.get_barrier_semaphore(), 6 + self.levels)

    def send(self, code, source, target, send_sem, recv_sem):
        copy = pltpu.make_async_remote_copy(
            src_ref=source,
            dst_ref=target,
            send_sem=send_sem,
            recv_sem=recv_sem,
            device_id={"seq": self.other(code)},
            device_id_type=MESH,
        )
        copy.start()
        return copy


class Steps:
    def copies(self, step):
        return [
            pltpu.make_async_remote_copy(
                src_ref=source,
                dst_ref=target,
                send_sem=self.send_sem.at[index],
                recv_sem=self.recv_sem.at[index],
                device_id=device,
                device_id_type=MESH,
            )
            for device, source, target, index in self.moves(step)
        ]

    def begin(self, step):
        for copy in self.copies(step):
            copy.start()

    def end(self, step):
        for copy in self.copies(step):
            copy.wait()

    step, last = 0, 0

    def advance(self):
        if self.step:
            self.end(self.step)
            self.take(self.step)
        self.step += 1
        if self.step <= self.last:
            self.begin(self.step)

    def take(self, step):
        pass


class Reduce(Steps):
    last = 8

    def __init__(self, cube, panels, first, count, pair, flat, edge, deep, leave, send_sem, recv_sem, sent, before, finish):
        self.before, self.finish, self.freed = before, finish, set()
        self.cube, self.panels, self.first, self.count = cube, panels, first, count
        self.pair, self.flat, self.edge, self.deep, self.leave = pair, flat, edge, deep, leave
        self.send_sem, self.recv_sem, self.sent = send_sem, recv_sem, sent

    def await_free(self, index):
        if index not in self.freed:
            self.freed.add(index)
            pl.semaphore_wait(self.sent.at[index], 1)

    def begin(self, step):
        for index in {6: (1, 2), 8: (0,)}.get(step, ()):
            self.await_free(index)
        if self.before is not None:
            for index in {1: (0,), 2: (1, 2)}.get(step, ()):
                self.before.await_free(index)
        if step == 4:
            for k in range(1, self.cube.levels):
                for axis in (1, 2):
                    self.leave[k - 1, axis - 1] = self.share(self.cube.plane(k), axis)[...]
        super().begin(step)

    def rows(self, core=0, axis=None, far=0, further=None):
        bits = self.cube.bits
        flip = lambda bit, other: 1 - bit if other else bit
        start, size = flip(bits[0], core) * (D // 2), D // 2
        if axis is not None:
            size = D // 8
            start = start + (axis - 1) * (D // 4) + flip(bits[axis], far) * size
            if further is not None:
                size = D // 16
                start = start + flip(bits[3 - axis], further) * size
        return pl.ds(pl.multiple_of(start, D // 16), size)

    def all(self, rows):
        return self.panels.at[pl.ds(self.first, self.count), rows, :]

    def share(self, plane, axis):
        width = D // self.cube.levels
        lanes = pl.ds(pl.multiple_of(plane * width, width), width)
        return self.panels.at[pl.ds(self.first, self.count), self.rows(axis=axis, further=0), lanes]

    def moves(self, step):
        cube = self.cube
        near = lambda code: {"seq": cube.other(code)}
        if step == 1:
            return [(near(1), self.all(self.rows(core=1)), self.pair, 0)]
        if step == 2:
            return [
                (near(2 * axis), self.all(self.rows(axis=axis, far=1)), self.flat.at[axis - 1], axis)
                for axis in (1, 2)
            ]
        if step == 3:
            return [
                (
                    near(6 - 2 * axis),
                    self.all(self.rows(axis=axis, further=1)),
                    self.edge.at[axis - 1],
                    2 + axis,
                )
                for axis in (1, 2)
            ]
        if step == 4:
            return [
                (
                    {"batch": cube.plane(k)},
                    self.leave.at[k - 1, axis - 1],
                    self.deep.at[k - 1, axis - 1],
                    3 + 2 * k + axis - 1,
                )
                for k in range(1, cube.levels)
                for axis in (1, 2)
            ]
        if step == 5:
            return [
                (
                    {"batch": cube.plane(k)},
                    self.share(cube.level, axis),
                    self.share(cube.level, axis),
                    9 + 2 * k + axis - 1,
                )
                for k in range(1, cube.levels)
                for axis in (1, 2)
            ]
        if step == 6:
            parts = [(6 - 2 * axis, self.all(self.rows(axis=axis, further=0)), 16 + axis) for axis in (1, 2)]
        elif step == 7:
            parts = [(2 * axis, self.all(self.rows(axis=axis)), 18 + axis) for axis in (1, 2)]
        else:
            parts = [(1, self.all(self.rows()), 21)]
        return [(near(code), part, part, index) for code, part, index in parts]

    def add(self, rows, found):
        def one(i, carry):
            there = self.first + i
            total = self.panels[there, rows, :].astype(F32) + found[i].astype(F32)
            self.panels[there, rows, :] = total.astype(BF)
            return carry

        lax.fori_loop(0, self.count, one, 0)

    def take(self, step):
        if step == 1:
            self.add(self.rows(), self.pair)
        elif step == 2:
            for axis in (1, 2):
                self.add(self.rows(axis=axis), self.flat.at[axis - 1])
        elif step == 3:
            for axis in (1, 2):
                self.add(self.rows(axis=axis, further=0), self.edge.at[axis - 1])
        elif step == 4:
            for axis in (1, 2):
                here = self.share(self.cube.level, axis)
                total = here[...].astype(F32)
                for k in range(self.cube.levels - 1):
                    total = total + self.deep[k, axis - 1].astype(F32)
                here[...] = total.astype(BF)
        elif step == 8:
            self.finish()
        for index in {1: (0,), 3: (1, 2)}.get(step, ()):
            pl.semaphore_signal(
                self.sent.at[index],
                inc=1,
                device_id={"seq": self.cube.other(1 << index)},
                device_id_type=MESH,
            )


class Scatter(Steps):
    last = 3

    def __init__(self, cube, block, spare, send_sem, recv_sem, ready, finish):
        self.cube, self.block, self.spare = cube, block, spare
        self.ready, self.finish = ready, finish
        self.send_sem, self.recv_sem = send_sem, recv_sem

    def begin(self, step):
        if self.ready is not None:
            for index in {1: (0,), 2: (1, 2)}.get(step, ()):
                pl.semaphore_wait(self.ready.at[index], 1)
        super().begin(step)

    def at(self, code, part):
        return self.block(2 * self.cube.other(code) + part)

    def moves(self, step):
        near = lambda code: {"seq": self.cube.other(code)}
        if step == 1:
            parts = [(1, 2 * i + 1, part, 2 * i + part) for i in range(4) for part in range(2)]
        elif step == 2:
            parts = [(2, 2, 0, 8), (2, 6, 0, 9), (4, 4, 1, 10), (4, 6, 1, 11)]
        else:
            parts = [(4, 4, 0, 12), (2, 2, 1, 13)]
        return [(near(to), self.at(code, part), self.spare(k), k) for to, code, part, k in parts]

    def take(self, step):
        if step == 3:
            self.finish()
            return
        if step == 1:
            parts = [(2 * i, part, 2 * i + part) for i in range(4) for part in range(2)]
        else:
            parts = [(0, 0, 8), (4, 0, 9), (0, 1, 10), (2, 1, 11)]
        for code, part, k in parts:
            here = self.at(code, part)
            here[...] = (here[...].astype(F32) + self.spare(k)[...].astype(F32)).astype(BF)

    def result(self, part):
        return self.at(0, part)[...].astype(F32) + self.spare(12 + part)[...].astype(F32)


class Small(Steps):
    last = 2

    def __init__(self, cube, array, near, planes, send_sem, recv_sem):
        self.cube, self.array, self.near, self.planes = cube, array, near, planes
        self.send_sem, self.recv_sem = send_sem, recv_sem

    def moves(self, step):
        cube = self.cube
        if step == 1:
            here = self.near.at[cube.me]
            return [({"seq": cube.other(code)}, here, here, code - 1) for code in range(1, 8)]
        here = self.planes.at[cube.level]
        return [({"batch": cube.plane(k)}, here, here, 6 + k) for k in range(1, cube.levels)]

    def begin(self, step):
        if step == 1:
            self.near[self.cube.me] = self.array[...]
        super().begin(step)

    def take(self, step):
        found = self.near if step == 1 else self.planes
        total = found[0]
        for k in range(1, found.shape[0]):
            total = total + found[k]
        if step == 1:
            self.planes[self.cube.level] = total
        else:
            self.array[...] = total


class Gather:
    def __init__(self, cube, own, slot_ref, send_sem, recv_sem):
        self.cube, self.own, self.slot_ref = cube, own, slot_ref
        self.send_sem, self.recv_sem = send_sem, recv_sem
        self.sent = []

    def push(self, step, code, part):
        slot = 2 * self.cube.other(code) + part
        target = self.slot_ref(slot)
        source = self.own.at[part] if code == 0 else target
        self.sent.append(
            self.cube.send(
                step,
                source,
                target,
                self.send_sem.at[len(self.sent)],
                self.recv_sem.at[2 * (code ^ step) + part],
            )
        )

    def take(self, code, part):
        slot = self.slot_ref(2 * self.cube.other(code) + part)
        pltpu.make_async_remote_copy(
            src_ref=slot,
            dst_ref=slot,
            send_sem=self.send_sem.at[0],
            recv_sem=self.recv_sem.at[2 * code + part],
            device_id={"seq": self.cube.other(1)},
            device_id_type=MESH,
        ).wait_recv()

    def arrived(self, code):
        for part in range(2):
            self.take(code, part)

    def open(self):
        for step, part in ((2, 0), (4, 1), (1, 0), (1, 1)):
            self.push(step, 0, part)

    def more(self):
        for step, part in ((2, 1), (4, 0)):
            self.push(step, 0, part)

    def pass_on(self):
        self.take(2, 0)
        self.push(4, 2, 0)
        self.take(4, 1)
        self.push(2, 4, 1)
        self.push(1, 2, 0)
        self.push(1, 4, 1)
        self.take(2, 1)
        self.push(1, 2, 1)
        self.take(4, 0)
        self.push(1, 4, 0)

    def finish(self):
        for part in range(2):
            self.take(6, part)
            self.push(1, 6, part)

    def close(self):
        for copy in self.sent:
            copy.wait_send()


def publish_kernel(grads, dvec, *refs):
    kept, outs, stages = refs[:3], refs[3:-8], refs[-8:-5]
    narrow, broad, load_sem, store_sem, keep_sem = refs[-5:]
    fetches = [pltpu.make_async_copy(kept[i], stages[i], keep_sem.at[i]) for i in range(3)]
    keeps = [pltpu.make_async_copy(stages[i], outs[24 + i], keep_sem.at[i]) for i in range(3)]
    order = list(range(8, 16)) + list(range(4, 8)) + list(range(4))
    loads = [pltpu.make_async_copy(grads.at[i], narrow.at[i], load_sem.at[i]) for i in order]
    ahead = 16
    for load in loads[:ahead] + fetches:
        load.start()
    for i in range(13):
        outs[10 + i][...] = dvec[i, :]
    for i in range(4):
        outs[23][i * D : (i + 1) * D] = dvec[13 + i, :]
    stores = []
    for turn, (load, i) in enumerate(zip(loads, order)):
        load.wait()
        if turn + ahead < len(loads):
            loads[turn + ahead].start()
        broad[i] = narrow[i].astype(F32)
        if i < 8:
            target = outs[i]
        elif i % 2 == 0:
            target = outs[8].at[:, pl.ds((i - 8) // 2 * D, D)]
        else:
            target = outs[9].at[pl.ds((i - 8) // 2 * D, D), :]
        store = pltpu.make_async_copy(broad.at[i], target, store_sem.at[i])
        store.start()
        stores.append(store)
    for fetch, keep in zip(fetches, keeps):
        fetch.wait()
        keep.start()
    for store in stores + keeps:
        store.wait()


def publish(grads, dvec, kept):
    vmem = pl.BlockSpec(memory_space=pltpu.VMEM)
    hbm = pl.BlockSpec(memory_space=pl.ANY)
    shapes = [(D, D)] * 8 + [(D, 4 * D), (4 * D, D)] + [(D,)] * 13 + [(4 * D,)]
    return pl.pallas_call(
        publish_kernel,
        out_shape=tuple(
            [jax.ShapeDtypeStruct(shape, F32) for shape in shapes]
            + [jax.ShapeDtypeStruct(array.shape, array.dtype) for array in kept]
        ),
        in_specs=[hbm, vmem] + [hbm] * 3,
        out_specs=tuple([hbm] * 10 + [vmem] * 14 + [hbm] * 3),
        scratch_shapes=[pltpu.VMEM(array.shape, array.dtype) for array in kept]
        + [
            pltpu.VMEM((16, D, D), BF),
            pltpu.VMEM((16, D, D), F32),
            pltpu.SemaphoreType.DMA((16,)),
            pltpu.SemaphoreType.DMA((16,)),
            pltpu.SemaphoreType.DMA((3,)),
        ],
        compiler_params=pltpu.CompilerParams(vmem_limit_bytes=64 << 20),
    )(grads, dvec, *kept)


def layer_kernel(
    sizes,
    tlen,
    slen,
    tord,
    sord,
    own_far,
    cot_far,
    own_memory,
    vectors_far,
    w_small,
    w_in,
    w_out,
    result,
    dinputs,
    dmemory,
    dvec,
    grads,
    own,
    cot,
    vectors,
    vec,
    nrm,
    memory,
    stream,
    weight,
    kv,
    queries,
    ckeys,
    cvalues,
    scores,
    powers,
    cpowers,
    inverses,
    cinverses,
    mixed,
    heard,
    unit,
    low,
    tinv,
    sinv,
    pairs,
    flats,
    edges,
    deeps,
    leaves,
    nears,
    planes,
    sem,
    send_sem,
    recv_sem,
    group_send,
    group_recv,
    group_sent,
    scatter_send,
    scatter_recv,
    small_send,
    small_recv,
    ready,
):
    rows, blocks, half, sblocks, shalf, ndoc, window = (
        sizes["rows"],
        sizes["blocks"],
        sizes["half"],
        sizes["sblocks"],
        sizes["shalf"],
        sizes["ndoc"],
        sizes["window"],
    )
    around = -(-window // half)
    pad = around * half - window
    sources = sblocks * shalf
    later = dinputs
    me = lax.axis_index("seq")
    scale = float(HDIM) ** -0.5
    thirds = half // PIECE
    cube = Cube(me, lax.axis_index("batch"), sizes["levels"])
    cube.greet()

    def raw(slot):
        return powers.at[lax.rem(slot, 4), pl.ds(lax.div(slot, 4) * thirds, thirds), :, 0:D]

    def raw_memory(slot):
        return memory.at[slot]

    gather_rows = Gather(cube, own_far, raw, send_sem.at[0], recv_sem.at[0])
    gather_sources = Gather(cube, own_memory, raw_memory, send_sem.at[1], recv_sem.at[1])
    copies = []
    for index, (source, target) in enumerate(
        [(own_far, own)]
        + list(zip(vectors_far, vectors))
        + [(w_small[i], weight.at[i]) for i in range(8)]
        + [(w_in.at[:, pl.ds(D * i, D)], weight.at[8 + 2 * i]) for i in range(4)]
        + [(w_out.at[pl.ds(D * i, D), :], weight.at[9 + 2 * i]) for i in range(4)]
        + [(cot_far, cot)]
    ):
        copy = pltpu.make_async_copy(source, target, sem.at[index])
        copy.start()
        copies.append(copy)
    cube.await_all()
    gather_rows.open()
    def deliver(turn, first, count):
        def go():
            pltpu.make_async_copy(
                weight.at[pl.ds(first, count)], grads.at[pl.ds(first, count)], sem.at[turn]
            ).start()

        return go

    groups = []
    for turn, (first, count) in enumerate(GROUPS):
        side = turn % 2
        some = pl.ds(0, count)
        groups.append(
            Reduce(
                cube, weight, first, count, pairs.at[side, some], flats.at[side, :, some],
                edges.at[side, :, some], deeps.at[side, :, :, some], leaves.at[side, :, :, some],
                group_send.at[turn], group_recv.at[turn], group_sent.at[turn],
                groups[turn - 2] if turn > 1 else None, deliver(turn, first, count),
            )
        )

    def spare_block(k):
        return powers.at[k % 4, pl.ds(k // 4 * thirds, thirds), :, 0:D]

    def end_rows():
        for part in range(2):
            own_unit, own_spread = centred(own[part].reshape(half, D).astype(F32))
            dnormed = rows_back.result(part).reshape(half, D)
            here = pl.ds(part * half, half)
            dinputs[here, :] = later[here, :] + norm_back(dnormed, own_unit, own_spread, vector(0))
            dvec[0:1, :] += column_sum(dnormed * own_unit)
            dvec[1:2, :] += column_sum(dnormed)

    def end_memory():
        for part in range(2):
            dmemory[part * shalf : (part + 1) * shalf, :] = memory_back.result(part)

    rows_back = Scatter(
        cube, lambda slot: nrm.at[slot], spare_block, scatter_send.at[0], scatter_recv.at[0],
        ready, end_rows,
    )
    memory_back = Scatter(
        cube,
        lambda slot: cvalues.at[pl.ds(pl.multiple_of(slot * shalf, shalf), shalf), :],
        lambda k: memory.at[k],
        scatter_send.at[1],
        scatter_recv.at[1],
        None,
        end_memory,
    )
    smalls = [
        Small(
            cube, dvec.at[pl.ds(start, 8 * size), :],
            nears.at[:, pl.ds(start, 8 * size), :], planes.at[:, pl.ds(start, 8 * size), :],
            small_send.at[turn], small_recv.at[turn],
        )
        for turn, (start, size) in enumerate(((0, 1), (8, 2)))
    ]
    exchanges = dict(
        A=groups[0], B=groups[1], C=groups[2], E=groups[3], R=rows_back, M=memory_back,
        S=smalls[0], V=smalls[1],
    )
    counts = dict(A=9, B=9, C=9, E=9, R=4, M=4, S=3, V=3)

    def pump(point):
        for name in SCHEDULE.get(point, ""):
            counts[name] -= 1
            exchanges[name].advance()

    dvec[...] = jnp.zeros((VECTORS, D), F32)
    for order, inverse_of, count in ((tord, tinv, blocks), (sord, sinv, sblocks)):
        for t in range(count):
            found = jnp.int32(0)
            for s in range(count):
                found = jnp.where(order[0, s] == t, s, found)
            inverse_of[t] = found
    tends, sends = [], []
    tend, send = jnp.int32(0), jnp.int32(0)
    for d in range(ndoc):
        tend, send = tend + tlen[0, d], send + slen[0, d]
        tends.append(tend)
        sends.append(send)
    base = [tord[0, 2 * me + b] for b in range(2)]

    def vector(index):
        return vec[index : index + 1, :]

    for copy in copies:
        copy.wait()
    gather_rows.more()
    row = 0
    for vector_ref in vectors:
        for start in range(0, vector_ref.shape[0], D):
            vec[row : row + 1, :] = vector_ref[start : start + D].astype(F32).reshape(1, D)
            row += 1

    states = own[...].reshape(rows, D)
    own_normed = (centred(states.astype(F32))[0] * vector(0) + vector(1)).astype(BF)
    queries[...] = ((nn(own_normed, weight[0]) + vector(2)) * scale).astype(BF)

    def project_block(s, block):
        found, _ = centred(block.astype(F32))
        normed = (found * vector(0) + vector(1)).astype(BF)
        nrm[s] = normed.reshape(thirds, PIECE, D)
        keys = nn(normed, weight[1]).astype(BF)
        values = (nn(normed, weight[2]) + vector(3)).astype(BF)
        for quad in range(2):
            kv[0, quad, s] = keys[:, quad * 256 : (quad + 1) * 256]
            kv[1, quad, s] = values[:, quad * 256 : (quad + 1) * 256]

    def project(code):
        def one(part, carry):
            s = 2 * cube.other(code) + part
            project_block(s, raw(s)[...].reshape(half, D))
            return carry

        lax.fori_loop(0, 2, one, 0)

    for part in range(2):
        project_block(2 * me + part, own[part].reshape(half, D))
    gather_rows.arrived(1)
    project(1)
    gather_rows.pass_on()
    gather_sources.open()
    gather_sources.more()
    project(2)
    project(4)
    gather_rows.arrived(3)
    project(3)
    gather_rows.arrived(5)
    project(5)
    gather_rows.finish()
    project(6)
    gather_rows.arrived(7)
    project(7)
    gather_rows.close()
    gather_sources.pass_on()

    def limits(b):
        index = lax.broadcasted_iota(jnp.int32, (1, 4 * half), 1)
        row = index
        for h in range(1, 4):
            row = jnp.where(index >= h * half, index - h * half, row)
        position = base[b] * half + row
        start = jnp.zeros_like(position)
        for end in tends:
            start = jnp.where(position >= end, end, start)
        shift = (base[b] + 1) * half - window
        return start - shift, position - shift + 1

    kwin, vwin = [
        cpowers.at[kind, pl.ds(0, window // PIECE), :, pl.ds(D, 4 * HDIM)] for kind in range(2)
    ]

    def fill(b, quad):
        skip = pad // PIECE
        for j in range(around):
            slot = tinv[jnp.maximum(base[b] - (around - 1) + j, 0)]
            for kind, target in ((0, kwin), (1, vwin)):
                block = kv[kind, quad, slot].reshape(thirds, PIECE, 4 * HDIM)
                if j == 0:
                    target[0 : thirds - skip] = block[skip:]
                else:
                    target[j * thirds - skip : (j + 1) * thirds - skip] = block

    for b in range(2):
        begin, stop = limits(b)

        def forward(quad, carry, b=b, begin=begin, stop=stop):
            fill(b, quad)
            lanes = pl.ds(pl.multiple_of(quad * 256, 256), 256)
            block = queries[b * half : (b + 1) * half, lanes].astype(F32)
            out, inverse = attend(
                spread_heads(block, 4).astype(BF),
                kwin,
                vwin,
                begin,
                stop,
                scores.at[pl.ds(0, window), :],
                powers.at[b * 2 + quad],
            )
            inverses[b * 2 + quad] = jnp.broadcast_to(inverse, (8, 4 * half))
            mixed[b * half : (b + 1) * half, lanes] = join_heads(out, 4)
            return carry

        lax.fori_loop(0, 2, forward, 0)
        if b == 0:
            gather_sources.finish()

    middle = own[...].reshape(rows, D).astype(F32) + nn(mixed[...].astype(BF), weight[3]) + vector(4)
    found, spread = centred(middle)
    later[...] = middle
    unit[0] = found
    low[0] = (found * vector(5) + vector(6)).astype(BF)
    cross_spread = spread
    low[1] = ((nn(low[0], weight[4]) + vector(7)) * scale).astype(BF)

    for code in (1, 3, 5, 7):
        gather_sources.arrived(code)
    for part in range(2):
        memory[2 * me + part] = own_memory[part]
    gather_sources.close()

    def place(t, carry):
        stream[t] = memory[sinv[t]]
        return carry

    lax.fori_loop(0, sblocks, place, 0)
    step = sources // 2
    some = sblocks // 2

    def sources_of(c, carry):
        part = pl.ds(pl.multiple_of(c * step, step), step)
        block = stream[pl.ds(c * some, some)].reshape(step, D)
        ckeys[part, :] = nn(block, weight[5]).astype(BF)
        cvalues[part, :] = (nn(block, weight[6]) + vector(8)).astype(BF)
        return carry

    lax.fori_loop(0, sources // step, sources_of, 0)
    index = lax.broadcasted_iota(jnp.int32, (1, 2 * rows), 1)
    row = jnp.where(index >= rows, index - rows, index)
    position = jnp.where(row >= half, base[1] * half + row - half, base[0] * half + row)
    begin = jnp.zeros_like(position)
    stop = jnp.full_like(position, sources)
    for end, send in zip(tends, sends):
        begin = jnp.where(position >= end, send, begin)
    for end, send in reversed(list(zip(tends, sends))):
        stop = jnp.where(position < end, send, stop)

    def cross_forward(pair, carry):
        lanes = pl.ds(pl.multiple_of(pair * 128, 128), 128)
        out, inverse = attend(
            spread_heads(low[1, :, lanes].astype(F32), 2).astype(BF),
            ckeys.at[:, lanes],
            cvalues.at[:, lanes],
            begin,
            stop,
            scores,
            cpowers.at[pair],
        )
        cinverses[pair] = jnp.broadcast_to(inverse, (8, 2 * rows))
        heard[:, lanes] = join_heads(out, 2)
        return carry

    lax.fori_loop(0, 4, cross_forward, 0)
    after_cross = later[...] + nn(heard[...].astype(BF), weight[7]) + vector(9)
    found, spread = centred(after_cross)
    unit[1] = found
    final_spread = spread
    low[2] = (found * vector(10) + vector(11)).astype(BF)
    later[...] = after_cross + vector(12)

    cotangent = cot[...]
    unit[2] = jnp.zeros((rows, D), F32)

    def feed(c, carry):
        fed = low[2]
        first, second = weight[8 + 2 * c], weight[9 + 2 * c]
        before = nn(fed, first) + vec[pl.ds(13 + c, 1), :]
        cumulative = 0.5 * (1.0 + lax.erf(before * (2.0**-0.5)))
        after = (before * cumulative).astype(BF)
        slope = cumulative + before * jnp.exp(-0.5 * before * before) * ((2.0 * math.pi) ** -0.5)
        later[...] += nn(after, second)
        change = nt(cotangent, second) * slope
        change_low = change.astype(BF)
        dvec[pl.ds(13 + c, 1), :] = column_sum(change_low.astype(F32))
        unit[2] += nt(change_low, first)
        weight[8 + 2 * c] = tn(fed, change_low).astype(BF)
        weight[9 + 2 * c] = tn(after, cotangent).astype(BF)

        @pl.when(c == 1)
        def _():
            pump("half")

        return carry

    lax.fori_loop(0, 4, feed, 0)
    pump("feed")
    result[...] = later[...].astype(BF)
    cot_f = cotangent.astype(F32)
    dvec[12:13, :] = column_sum(cot_f)
    dfed = unit[2]
    dvec[10:11, :] = column_sum(dfed * unit[1])
    dvec[11:12, :] = column_sum(dfed)
    dlater = cot_f + norm_back(dfed, unit[1], final_spread, vector(10))
    later[...] = dlater
    branch = dlater.astype(BF)
    dvec[9:10, :] = column_sum(branch.astype(F32))
    dheard = nt(branch, weight[7]).astype(BF)
    weight[7] = tn(heard[...].astype(BF), branch).astype(BF)
    low[2] = dheard
    heard[...] = heard[...] * dheard.astype(F32)
    pump("heard")

    def cross_backward(pair, carry):
        lanes = pl.ds(pl.multiple_of(pair * 128, 128), 128)

        def store(c, dkeys, dvalues):
            part = pl.ds(pl.multiple_of(c * dkeys.shape[0], dkeys.shape[0]), dkeys.shape[0])
            scores[part, 0:128] = dkeys
            cvalues[part, lanes] = dvalues.astype(BF)

        out = attend_back(
            spread_heads(low[1, :, lanes].astype(F32), 2).astype(BF),
            spread_heads(low[2, :, lanes].astype(F32), 2).astype(BF),
            spread_heads(heard[:, lanes], 2),
            ckeys.at[:, lanes],
            cvalues.at[:, lanes],
            cinverses[pair, 0:1, :],
            cpowers.at[pair],
            store,
        )
        ckeys[:, lanes] = scores[:, 0:128].astype(BF)
        unit[1, :, lanes] = join_heads(out, 2)

        for index in range(4):

            @pl.when(pair == index)
            def _(index=index):
                pump("pair" + str(index))

        return carry

    lax.fori_loop(0, 4, cross_backward, 0)

    dvec[8:9, :] = column_sum(cvalues[...].astype(F32))
    block = stream[...].reshape(sources, D)
    fresh = [tn(block, ckeys[...]).astype(BF), tn(block, cvalues[...]).astype(BF)]

    pump("sums")

    def sources_back(c, carry):
        part = pl.ds(pl.multiple_of(c * step, step), step)
        back = nt(ckeys[part, :], weight[5]) + nt(cvalues[part, :], weight[6])
        stream[pl.ds(c * some, some)] = back.astype(BF).reshape(some, shalf, D)
        return carry

    lax.fori_loop(0, sources // step, sources_back, 0)
    weight[5] = fresh[0]
    weight[6] = fresh[1]

    def place_back(s, carry):
        there = pl.ds(pl.multiple_of(s * shalf, shalf), shalf)
        cvalues[there, :] = stream[sord[0, s]]
        return carry

    lax.fori_loop(0, sblocks, place_back, 0)
    pump("sources")
    ckeys[0:D, :] = weight[1]
    ckeys[D : 2 * D, :] = weight[2]

    dcq = unit[1].astype(BF)
    dvec[7:8, :] = column_sum(dcq.astype(F32)) * scale
    dcrossed = nt(dcq, weight[4]) * scale
    weight[4] = (tn(low[0], dcq) * scale).astype(BF)
    dvec[5:6, :] = column_sum(dcrossed * unit[0])
    dvec[6:7, :] = column_sum(dcrossed)
    dmid = later[...] + norm_back(dcrossed, unit[0], cross_spread, vector(5))
    later[...] = dmid
    branch = dmid.astype(BF)
    dvec[4:5, :] = column_sum(branch.astype(F32))
    dmixed = nt(branch, weight[3]).astype(BF)
    weight[3] = tn(mixed[...].astype(BF), branch).astype(BF)
    low[2] = dmixed
    mixed[...] = mixed[...] * dmixed.astype(F32)
    pump("middle")

    for b in range(2):
        for kind in range(2):
            if pad:
                cpowers[2 * kind + b, 0 : pad // PIECE, :, 0:D] = jnp.zeros((pad // PIECE, PIECE, D), BF)

        def backward(quad, carry, b=b):
            fill(b, quad)
            lanes = pl.ds(pl.multiple_of(quad * 256, 256), 256)

            def store(c, dkeys, dvalues):
                pieces = dkeys.shape[0] // PIECE
                part = pl.ds(c * pieces + pad // PIECE, pieces)
                cpowers[b, part, :, lanes] = dkeys.astype(BF).reshape(pieces, PIECE, 256)
                cpowers[2 + b, part, :, lanes] = dvalues.astype(BF).reshape(pieces, PIECE, 256)

            out = attend_back(
                spread_heads(queries[b * half : (b + 1) * half, lanes].astype(F32), 4).astype(BF),
                spread_heads(low[2, b * half : (b + 1) * half, lanes].astype(F32), 4).astype(BF),
                spread_heads(mixed[b * half : (b + 1) * half, lanes], 4),
                kwin,
                vwin,
                inverses[b * 2 + quad, 0:1, :],
                powers.at[b * 2 + quad],
                store,
            )
            unit[1, b * half : (b + 1) * half, lanes] = join_heads(out, 4)

            for index in range(2):

                @pl.when(quad == index)
                def _(index=index):
                    pump("self" + str(2 * b + index))

            return carry

        lax.fori_loop(0, 2, backward, 0)

        ratio = half // shalf
        for j in range(around):
            slot = tinv[jnp.maximum(base[b] - (around - 1) + j, 0)]
            stream[j * ratio : (j + 1) * ratio] = nrm[slot].reshape(ratio, shalf, D)
        normed = stream[0 : around * ratio].reshape(around * half, D)
        for kind in range(2):
            change = cpowers[2 * kind + b, 0 : around * thirds, :, 0:D].reshape(around * half, D)
            if kind == 1:
                dvec[3:4, :] += column_sum(change.astype(F32))
            total = tn(normed, change)
            there = slice(kind * D, (kind + 1) * D)
            if b == 0:
                scores[there, 0:D] = total
            else:
                weight[1 + kind] = (scores[there, 0:D] + total).astype(BF)
        if b == 0:
            pump("window")
    for index in range(3):
        pl.semaphore_signal(
            ready.at[index],
            inc=1,
            device_id={"seq": cube.other(1 << index)},
            device_id_type=MESH,
        )

    dq = unit[1].astype(BF)
    dvec[2:3, :] = column_sum(dq.astype(F32)) * scale
    heard[...] = nt(dq, weight[0]) * scale
    own_normed = nrm[pl.ds(2 * me, 2)].reshape(rows, D)
    weight[0] = (tn(own_normed, dq) * scale).astype(BF)

    pump("weights")

    for b in range(2):

        def through(c, carry, b=b):
            part = pl.ds(c * around, around)
            dkeys = cpowers[b, part, :, 0:D].reshape(around * PIECE, D)
            dvalues = cpowers[2 + b, part, :, 0:D].reshape(around * PIECE, D)
            total = nt(dkeys, ckeys[0:D, :]) + nt(dvalues, ckeys[D : 2 * D, :])
            cpowers[b, part, :, 0:D] = total.astype(BF).reshape(around, PIECE, D)
            return carry

        lax.fori_loop(0, thirds, through, 0)
        pump("through" + str(b))

    def assemble(code):
        def one(part, carry):
            s = 2 * cube.other(code) + part
            for third in range(thirds):
                total = jnp.zeros((PIECE, D), F32)
                for b in range(2):
                    back = base[b] - tord[0, s]
                    inside = (back >= 0) & (back < around)
                    first = jnp.clip(around - 1 - back, 0, around - 1) * thirds
                    found = cpowers[b, first + third][:, 0:D]
                    total = total + jnp.where(inside, found.astype(F32), 0.0)
                if code == 0:
                    start = pl.multiple_of(part * half + third * PIECE, PIECE)
                    total = total + heard[pl.ds(start, PIECE), :]
                nrm[s, third] = total.astype(BF)
            return carry

        lax.fori_loop(0, 2, one, 0)

    for code in (1, 3, 5, 7):
        assemble(code)
    pump("theirs")
    for code in (6, 2, 4, 0):
        assemble(code)
    pump("end")
    assert not any(counts.values()), counts
    for turn, (first, count) in enumerate(GROUPS):
        pltpu.make_async_copy(
            weight.at[pl.ds(first, count)], grads.at[pl.ds(first, count)], sem.at[turn]
        ).wait()


def layer_call(sizes, small_ints, own, cot, own_memory, vectors, w_small, w_in, w_out):
    rows, blocks, half, sblocks, shalf, window = (
        sizes["rows"],
        sizes["blocks"],
        sizes["half"],
        sizes["sblocks"],
        sizes["shalf"],
        sizes["window"],
    )
    sources = sblocks * shalf
    levels = sizes["levels"]
    most = max(count for _, count in GROUPS)
    vmem = pl.BlockSpec(memory_space=pltpu.VMEM)
    smem = pl.BlockSpec(memory_space=pltpu.SMEM)
    hbm = pl.BlockSpec(memory_space=pl.ANY)

    count = len(vectors)

    def body(*refs):
        head, rest = refs[:7], refs[7:]
        vector_refs, rest = rest[:count], rest[count:]
        scratch = rest[17:]
        layer_kernel(
            sizes, *head, vector_refs, rest[:8], *rest[8:15],
            *rest[15:17], scratch[:count], *scratch[count:],
        )

    return pl.pallas_call(
        body,
        out_shape=(
            jax.ShapeDtypeStruct((rows, D), BF),
            jax.ShapeDtypeStruct((rows, D), F32),
            jax.ShapeDtypeStruct((2 * shalf, D), F32),
            jax.ShapeDtypeStruct((VECTORS, D), F32),
            jax.ShapeDtypeStruct((16, D, D), BF),
        ),
        in_specs=[smem] * 4 + [hbm] * 2 + [vmem] + [hbm] * (count + 10),
        out_specs=(vmem, vmem, vmem, vmem, hbm),
        scratch_shapes=[pltpu.VMEM(own.shape, BF), pltpu.VMEM(cot.shape, BF)]
        + [pltpu.VMEM(vector.shape, BF) for vector in vectors]
        + [
            pltpu.VMEM((VECTORS, D), F32),
            pltpu.VMEM((blocks, half // PIECE, PIECE, D), BF),
            pltpu.VMEM((sblocks, shalf, D), BF),
            pltpu.VMEM((sblocks, shalf, D), BF),
            pltpu.VMEM((16, D, D), BF),
            pltpu.VMEM((2, 2, blocks, half, 256), BF),
            pltpu.VMEM((rows, D), BF),
            pltpu.VMEM((sources, D), BF),
            pltpu.VMEM((sources, D), BF),
            pltpu.VMEM((sources, 2 * rows), F32),
            pltpu.VMEM((4, window // PIECE, PIECE, 4 * half), BF),
            pltpu.VMEM((4, sources // PIECE, PIECE, 2 * rows), BF),
            pltpu.VMEM((4, 8, 4 * half), F32),
            pltpu.VMEM((4, 8, 2 * rows), F32),
            pltpu.VMEM((rows, D), F32),
            pltpu.VMEM((rows, D), F32),
            pltpu.VMEM((3, rows, D), F32),
            pltpu.VMEM((3, rows, D), BF),
            pltpu.SMEM((blocks,), jnp.int32),
            pltpu.SMEM((sblocks,), jnp.int32),
            pltpu.VMEM((2, most, D // 2, D), BF),
            pltpu.VMEM((2, 2, most, D // 8, D), BF),
            pltpu.VMEM((2, 2, most, D // 16, D), BF),
            pltpu.VMEM((2, levels - 1, 2, most, D // 16, D // levels), BF),
            pltpu.VMEM((2, levels - 1, 2, most, D // 16, D // levels), BF),
            pltpu.VMEM((8, VECTORS, D), F32),
            pltpu.VMEM((levels, VECTORS, D), F32),
            pltpu.SemaphoreType.DMA((32,)),
            pltpu.SemaphoreType.DMA((2, 16)),
            pltpu.SemaphoreType.DMA((2, 16)),
            pltpu.SemaphoreType.DMA((4, 22)),
            pltpu.SemaphoreType.DMA((4, 22)),
            pltpu.SemaphoreType.REGULAR((4, 3)),
            pltpu.SemaphoreType.DMA((2, 14)),
            pltpu.SemaphoreType.DMA((2, 14)),
            pltpu.SemaphoreType.DMA((2, 10)),
            pltpu.SemaphoreType.DMA((2, 10)),
            pltpu.SemaphoreType.REGULAR((3,)),
        ],
        compiler_params=pltpu.CompilerParams(
            vmem_limit_bytes=64 << 20, collective_id=0, has_side_effects=True
        ),
    )(*small_ints, own, cot, own_memory, *vectors, *w_small, w_in, w_out)


def fused_on_device(
    inputs, memory, target_lengths, source_lengths, target_order, source_order,
    self_gain, self_shift, self_query, query_bias, self_key, self_value, value_bias,
    self_output, output_bias, cross_gain, cross_shift, cross_query, cquery_bias, cross_key,
    cross_value, cvalue_bias, cross_output, coutput_bias, final_gain, final_shift,
    inner_weight, inner_bias, outer_weight, outer_bias, cotangent,
):
    rows = inputs.shape[1]
    blocks = target_order.shape[1]
    sblocks = source_order.shape[1]
    ranks = lax.axis_size("seq")
    half = ranks * rows // blocks
    shalf = ranks * memory.shape[1] // sblocks
    ndoc = target_lengths.shape[1]
    reach = max(LONGEST, blocks * half - LONGEST - SHORTEST * (ndoc - 1))
    window = -(-(reach - 1 + half) // CHUNK) * CHUNK
    sizes = dict(
        rows=rows, blocks=blocks, half=half, sblocks=sblocks, shalf=shalf, ndoc=ndoc, window=window,
        levels=lax.axis_size("batch"),
    )
    result, dinputs, dmemory, dvec, grads = layer_call(
        sizes, (target_lengths, source_lengths, target_order, source_order),
        inputs.reshape(2, half // PIECE, PIECE, D), cotangent[0], memory.reshape(2, shalf, D),
        (
            self_gain, self_shift, query_bias, value_bias, output_bias, cross_gain, cross_shift,
            cquery_bias, cvalue_bias, coutput_bias, final_gain, final_shift, outer_bias, inner_bias,
        ),
        (self_query, self_key, self_value, self_output, cross_query, cross_key, cross_value, cross_output),
        inner_weight, outer_weight,
    )
    made = publish(grads, dvec, (result, dinputs, dmemory))
    result, dinputs, dmemory = made[24:]
    squares, wide, tall, rows_of, units = made[:8], made[8], made[9], made[10:23], made[23]
    return (
        result[None], dinputs[None], dmemory[None],
        rows_of[0], rows_of[1], squares[0], rows_of[2], squares[1], squares[2], rows_of[3],
        squares[3], rows_of[4], rows_of[5], rows_of[6], squares[4], rows_of[7], squares[5],
        squares[6], rows_of[8], squares[7], rows_of[9], rows_of[10], rows_of[11],
        wide, units, tall, rows_of[12],
    )


def solution(mesh):
    in_specs = (
        P("batch", "seq", None),
        P("batch", "seq", None),
        P("batch", None),
        P("batch", None),
        P("batch", None),
        P("batch", None),
        P(),
        P(),
        P(),
        P(),
        P(),
        P(),
        P(),
        P(),
        P(),
        P(),
        P(),
        P(),
        P(),
        P(),
        P(),
        P(),
        P(),
        P(),
        P(),
        P(),
        P(),
        P(),
        P(),
        P(),
        P("batch", "seq", None),
    )
    out_specs = (
        P("batch", "seq", None),
        P("batch", "seq", None),
        P("batch", "seq", None),
        P(),
        P(),
        P(),
        P(),
        P(),
        P(),
        P(),
        P(),
        P(),
        P(),
        P(),
        P(),
        P(),
        P(),
        P(),
        P(),
        P(),
        P(),
        P(),
        P(),
        P(),
        P(),
        P(),
        P(),
    )
    return jax.shard_map(
        fused_on_device if (mesh.shape["seq"], mesh.shape["batch"]) == (8, 4) else on_device,
        mesh=mesh, in_specs=in_specs, out_specs=out_specs, check_vma=False,
    )
```

```python
import math

import jax
import jax.numpy as jnp
from jax import lax
from jax.experimental import pallas as pl
from jax.experimental.pallas import tpu as pltpu
from jax.sharding import PartitionSpec as P

D = 512
HEADS = 8


EPSILON = 1e-05
NEGATIVE = -1e30


def norm(values, gain, shift):
    center = values - jnp.mean(values, axis=-1, keepdims=True)
    spread = jnp.mean(center * center, axis=-1, keepdims=True)
    return center * lax.rsqrt(spread + EPSILON) * gain + shift


def product(left, right):
    return jnp.dot(left, right, preferred_element_type=jnp.float32)


def weight_grad(left, right):
    return jnp.einsum("ti,to->io", left, right, preferred_element_type=jnp.float32)


def input_grad(grad, weight):
    return jnp.einsum("to,io->ti", grad, weight, preferred_element_type=jnp.float32)


def split_heads(values):
    return values.reshape(values.shape[0], HEADS, -1)


def locate(order, lengths, blocksize, start, count):
    index = start + jnp.arange(count, dtype=jnp.int32)
    slot = index // blocksize
    picked = jnp.sum(
        jnp.where(
            slot[:, None] == jnp.arange(order.shape[0], dtype=jnp.int32)[None, :], order[None, :], 0
        ),
        axis=1,
    )
    position = picked * blocksize + index % blocksize
    ends = jnp.cumsum(lengths)
    document = jnp.sum((position[:, None] >= ends[None, :]).astype(jnp.int32), axis=1)
    return (document, position)


def visible(query_doc, query_pos, key_doc, key_pos, causal):
    same = query_doc[:, None] == key_doc[None, :]
    if causal:
        return same & (key_pos[None, :] <= query_pos[:, None])
    return same


def opening(rows):
    return (
        jnp.zeros((rows, HEADS, D // HEADS), jnp.float32),
        jnp.full((rows, HEADS), NEGATIVE, jnp.float32),
        jnp.zeros((rows, HEADS), jnp.float32),
    )


def online(carry, query_heads, piece_keys, piece_values, allowed):
    weighted, highest, total = carry
    scores = jnp.einsum(
        "qhd,khd->qhk", query_heads, split_heads(piece_keys), preferred_element_type=jnp.float32
    )
    allowed = allowed[:, None, :]
    raised = jnp.maximum(highest, jnp.max(jnp.where(allowed, scores, NEGATIVE), axis=-1))
    powers = jnp.exp(jnp.where(allowed, scores - raised[..., None], NEGATIVE))
    total = jnp.sum(powers, axis=-1)
    weighted = jnp.einsum(
        "qhk,khd->qhd",
        powers.astype(jnp.bfloat16),
        split_heads(piece_values),
        preferred_element_type=jnp.float32,
    )
    return (weighted, raised, total)


def finish(carry):
    weighted, highest, total = carry
    return (highest + jnp.log(total), (weighted / total[..., None]).reshape(weighted.shape[0], D))


def block_back(query_heads, grad_heads, log_total, delta, piece_keys, piece_values, allowed):
    key_heads = split_heads(piece_keys)
    value_heads = split_heads(piece_values)
    scores = jnp.einsum("qhd,khd->qhk", query_heads, key_heads, preferred_element_type=jnp.float32)
    weights = jnp.exp(jnp.where(allowed[:, None, :], scores - log_total[..., None], NEGATIVE))
    grad_weights = jnp.einsum(
        "qhd,khd->qhk", grad_heads, value_heads, preferred_element_type=jnp.float32
    )
    grad_scores = (weights * (grad_weights - delta[..., None])).astype(jnp.bfloat16)
    grad_values = jnp.einsum(
        "qhk,qhd->khd", weights.astype(jnp.bfloat16), grad_heads, preferred_element_type=jnp.float32
    )
    grad_keys = jnp.einsum(
        "qhk,qhd->khd", grad_scores, query_heads, preferred_element_type=jnp.float32
    )
    grad_query = jnp.einsum(
        "qhk,khd->qhd", grad_scores, key_heads, preferred_element_type=jnp.float32
    )
    return (grad_query, grad_keys, grad_values)


def scan_back(
    query_heads,
    grad_heads,
    log_total,
    delta,
    all_keys,
    all_values,
    row_doc,
    row_pos,
    order,
    lengths,
    blocksize,
    causal,
):
    total_keys = all_keys.shape[0]
    width = math.gcd(total_keys, 512)
    count = total_keys // width

    def step(grad_query, item):
        block_keys, block_values, number = item
        key_doc, key_pos = locate(order, lengths, blocksize, number * width, width)
        allowed = visible(row_doc, row_pos, key_doc, key_pos, causal)
        query_term, key_term, value_term = block_back(
            query_heads, grad_heads, log_total, delta, block_keys, block_values, allowed
        )
        return (grad_query + query_term, (key_term, value_term))

    grad_query, (grad_keys, grad_values) = lax.scan(
        step,
        jnp.zeros(query_heads.shape, jnp.float32),
        (
            all_keys.reshape(count, width, D),
            all_values.reshape(count, width, D),
            jnp.arange(count, dtype=jnp.int32),
        ),
    )
    return (grad_query, grad_keys.reshape(total_keys, D), grad_values.reshape(total_keys, D))


def on_device(
    inputs,
    memory,
    target_lengths,
    source_lengths,
    target_order,
    source_order,
    self_gain,
    self_shift,
    self_query,
    query_bias,
    self_key,
    self_value,
    value_bias,
    self_output,
    output_bias,
    cross_gain,
    cross_shift,
    cross_query,
    cquery_bias,
    cross_key,
    cross_value,
    cvalue_bias,
    cross_output,
    coutput_bias,
    final_gain,
    final_shift,
    inner_weight,
    inner_bias,
    outer_weight,
    outer_bias,
    cotangent,
):
    rows = inputs.shape[1]
    sources = memory.shape[1]
    target_half = rows // 2
    source_half = sources // 2
    own_lengths = target_lengths[0]
    memory_lengths = source_lengths[0]
    own_order = target_order[0]
    memory_order = source_order[0]
    scale = float(D // HEADS) ** (-0.5)
    place = lax.axis_index("seq")
    row_doc, row_pos = locate(own_order, own_lengths, target_half, place * rows, rows)
    inputs_f = inputs[0].astype(jnp.float32)
    encoded = memory[0]
    normed, norm_back = jax.vjp(
        norm, inputs_f, self_gain.astype(jnp.float32), self_shift.astype(jnp.float32)
    )
    normed_low = normed.astype(jnp.bfloat16)
    queries = ((product(normed_low, self_query) + query_bias) * scale).astype(jnp.bfloat16)
    keys = product(normed_low, self_key).astype(jnp.bfloat16)
    values = (product(normed_low, self_value) + value_bias).astype(jnp.bfloat16)
    query_heads = split_heads(queries)
    piece = (
        lax.all_gather(keys, "seq", axis=0, tiled=True),
        lax.all_gather(values, "seq", axis=0, tiled=True),
    )
    key_doc, key_pos = locate(own_order, own_lengths, target_half, jnp.int32(0), piece[0].shape[0])
    self_carry = online(
        opening(rows),
        query_heads,
        piece[0],
        piece[1],
        visible(row_doc, row_pos, key_doc, key_pos, True),
    )
    self_total, mixed = finish(self_carry)
    mixed_low = mixed.astype(jnp.bfloat16)
    middle = inputs_f + product(mixed_low, self_output) + output_bias
    crossed, cross_back = jax.vjp(
        norm, middle, cross_gain.astype(jnp.float32), cross_shift.astype(jnp.float32)
    )
    crossed_low = crossed.astype(jnp.bfloat16)
    cqueries = ((product(crossed_low, cross_query) + cquery_bias) * scale).astype(jnp.bfloat16)
    ckeys = product(encoded, cross_key).astype(jnp.bfloat16)
    cvalues = (product(encoded, cross_value) + cvalue_bias).astype(jnp.bfloat16)
    cquery_heads = split_heads(cqueries)
    piece = (
        lax.all_gather(ckeys, "seq", axis=0, tiled=True),
        lax.all_gather(cvalues, "seq", axis=0, tiled=True),
    )
    key_doc, key_pos = locate(
        memory_order, memory_lengths, source_half, jnp.int32(0), piece[0].shape[0]
    )
    cross_carry = online(
        opening(rows),
        cquery_heads,
        piece[0],
        piece[1],
        visible(row_doc, row_pos, key_doc, key_pos, False),
    )
    cross_total, heard = finish(cross_carry)
    heard_low = heard.astype(jnp.bfloat16)
    later = middle + product(heard_low, cross_output) + coutput_bias
    fed, final_back = jax.vjp(
        norm, later, final_gain.astype(jnp.float32), final_shift.astype(jnp.float32)
    )
    fed_low = fed.astype(jnp.bfloat16)
    before = product(fed_low, inner_weight) + inner_bias
    after, gelu_back = jax.vjp(lambda entry: jax.nn.gelu(entry, approximate=False), before)
    after_low = after.astype(jnp.bfloat16)
    result = later + product(after_low, outer_weight) + outer_bias
    grad_out = cotangent[0]
    outer_weight_grad = weight_grad(after_low, grad_out)
    outer_bias_grad = jnp.sum(grad_out.astype(jnp.float32), axis=0)
    grad_after = input_grad(grad_out, outer_weight)
    grad_before = gelu_back(grad_after)[0].astype(jnp.bfloat16)
    inner_weight_grad = weight_grad(fed_low, grad_before)
    inner_bias_grad = jnp.sum(grad_before.astype(jnp.float32), axis=0)
    grad_fed = input_grad(grad_before, inner_weight)
    grad_later_norm, final_gain_grad, final_shift_grad = final_back(grad_fed)
    grad_later = cotangent[0].astype(jnp.float32) + grad_later_norm
    grad_cbranch = grad_later.astype(jnp.bfloat16)
    cross_output_grad = weight_grad(heard_low, grad_cbranch)
    coutput_bias_grad = jnp.sum(grad_cbranch.astype(jnp.float32), axis=0)
    grad_heard = input_grad(grad_cbranch, cross_output).astype(jnp.bfloat16)
    grad_heard_heads = split_heads(grad_heard)
    cross_delta = jnp.sum(grad_heard_heads.astype(jnp.float32) * split_heads(heard), axis=-1)
    all_ckeys, all_cvalues = (
        lax.all_gather(ckeys, "seq", axis=0, tiled=True),
        lax.all_gather(cvalues, "seq", axis=0, tiled=True),
    )
    grad_cq, part_ckeys, part_cvalues = scan_back(
        cquery_heads,
        grad_heard_heads,
        cross_total,
        cross_delta,
        all_ckeys,
        all_cvalues,
        row_doc,
        row_pos,
        memory_order,
        memory_lengths,
        source_half,
        False,
    )
    own_ckeys, own_cvalues = (
        lax.psum_scatter(
            part_ckeys.astype(jnp.bfloat16), "seq", scatter_dimension=0, tiled=True
        ).astype(jnp.float32),
        lax.psum_scatter(
            part_cvalues.astype(jnp.bfloat16), "seq", scatter_dimension=0, tiled=True
        ).astype(jnp.float32),
    )
    own_ckeys_low = own_ckeys.astype(jnp.bfloat16)
    own_cvalues_low = own_cvalues.astype(jnp.bfloat16)
    cross_key_grad = weight_grad(encoded, own_ckeys_low)
    cross_value_grad = weight_grad(encoded, own_cvalues_low)
    cvalue_bias_grad = jnp.sum(own_cvalues_low.astype(jnp.float32), axis=0)
    memory_grad = input_grad(own_ckeys_low, cross_key) + input_grad(own_cvalues_low, cross_value)
    grad_cq_low = grad_cq.reshape(rows, D).astype(jnp.bfloat16)
    cross_query_grad = weight_grad(crossed_low, grad_cq_low) * scale
    cquery_bias_grad = jnp.sum(grad_cq_low.astype(jnp.float32), axis=0) * scale
    grad_crossed = input_grad(grad_cq_low, cross_query) * scale
    grad_middle_norm, cross_gain_grad, cross_shift_grad = cross_back(grad_crossed)
    grad_middle = grad_later + grad_middle_norm
    grad_sbranch = grad_middle.astype(jnp.bfloat16)
    self_output_grad = weight_grad(mixed_low, grad_sbranch)
    output_bias_grad = jnp.sum(grad_sbranch.astype(jnp.float32), axis=0)
    grad_mixed = input_grad(grad_sbranch, self_output).astype(jnp.bfloat16)
    grad_mixed_heads = split_heads(grad_mixed)
    self_delta = jnp.sum(grad_mixed_heads.astype(jnp.float32) * split_heads(mixed), axis=-1)
    all_keys, all_values = (
        lax.all_gather(keys, "seq", axis=0, tiled=True),
        lax.all_gather(values, "seq", axis=0, tiled=True),
    )
    grad_q, part_keys, part_values = scan_back(
        query_heads,
        grad_mixed_heads,
        self_total,
        self_delta,
        all_keys,
        all_values,
        row_doc,
        row_pos,
        own_order,
        own_lengths,
        target_half,
        True,
    )
    own_keys, own_values = (
        lax.psum_scatter(
            part_keys.astype(jnp.bfloat16), "seq", scatter_dimension=0, tiled=True
        ).astype(jnp.float32),
        lax.psum_scatter(
            part_values.astype(jnp.bfloat16), "seq", scatter_dimension=0, tiled=True
        ).astype(jnp.float32),
    )
    own_keys_low = own_keys.astype(jnp.bfloat16)
    own_values_low = own_values.astype(jnp.bfloat16)
    self_key_grad = weight_grad(normed_low, own_keys_low)
    self_value_grad = weight_grad(normed_low, own_values_low)
    value_bias_grad = jnp.sum(own_values_low.astype(jnp.float32), axis=0)
    grad_q_low = grad_q.reshape(rows, D).astype(jnp.bfloat16)
    self_query_grad = weight_grad(normed_low, grad_q_low) * scale
    query_bias_grad = jnp.sum(grad_q_low.astype(jnp.float32), axis=0) * scale
    grad_normed = (
        input_grad(grad_q_low, self_query) * scale
        + input_grad(own_keys_low, self_key)
        + input_grad(own_values_low, self_value)
    )
    grad_in_norm, self_gain_grad, self_shift_grad = norm_back(grad_normed)
    inputs_grad = grad_middle + grad_in_norm
    summed = lax.psum(
        (
            self_gain_grad,
            self_shift_grad,
            self_query_grad,
            query_bias_grad,
            self_key_grad,
            self_value_grad,
            value_bias_grad,
            self_output_grad,
            output_bias_grad,
            cross_gain_grad,
            cross_shift_grad,
            cross_query_grad,
            cquery_bias_grad,
            cross_key_grad,
            cross_value_grad,
            cvalue_bias_grad,
            cross_output_grad,
            coutput_bias_grad,
            final_gain_grad,
            final_shift_grad,
            inner_weight_grad,
            inner_bias_grad,
            outer_weight_grad,
            outer_bias_grad,
        ),
        ("seq", "batch"),
    )
    return (result.astype(jnp.bfloat16)[None], inputs_grad[None], memory_grad[None]) + tuple(summed)


HDIM = D // HEADS
SHORTEST = 32
LONGEST = 1024
CHUNK = 256
PIECE = 64

GROUPS = ((8, 4), (12, 4), (3, 5), (0, 3))
SCHEDULE = dict(
    half="A",
    feed="A",
    heard="B",
    pair1="AB",
    pair3="A",
    sums="V",
    sources="MB",
    middle="ACM",
    self0="CB",
    window="AM",
    self2="BCA",
    weights="CEB",
    through0="EA",
    through1="BA",
    theirs="RV",
    end="CEREVCRBECRESBEMCSCESE",
)
MESH = pl.DeviceIdType.MESH
PARTS = 2
BF = jnp.bfloat16
F32 = jnp.float32
VECTORS = 24


def nn(left, right):
    return lax.dot_general(left, right, (((1,), (0,)), ((), ())), preferred_element_type=F32)


def nt(left, right):
    return lax.dot_general(left, right, (((1,), (1,)), ((), ())), preferred_element_type=F32)


def tn(left, right):
    return lax.dot_general(left, right, (((0,), (0,)), ((), ())), preferred_element_type=F32)


def centred(values):
    center = values - jnp.mean(values, axis=-1, keepdims=True)
    spread = lax.rsqrt(jnp.mean(center * center, axis=-1, keepdims=True) + EPSILON)
    return center * spread, spread


def norm_back(grad, unit, spread, gain):
    scaled = grad * gain
    return spread * (
        scaled
        - jnp.mean(scaled, axis=-1, keepdims=True)
        - unit * jnp.mean(scaled * unit, axis=-1, keepdims=True)
    )


def column_sum(values):
    return jnp.sum(values, axis=0, keepdims=True)


def spread_heads(block, heads):
    lane = lax.broadcasted_iota(jnp.int32, block.shape, 1)
    return jnp.concatenate(
        [
            jnp.where((lane >= h * HDIM) & (lane < (h + 1) * HDIM), block, 0.0)
            for h in range(heads)
        ],
        axis=0,
    )


def join_heads(stacked, heads):
    rows = stacked.shape[0] // heads
    lane = lax.broadcasted_iota(jnp.int32, (rows, stacked.shape[1]), 1)
    total = stacked[:rows]
    for h in range(1, heads):
        total = jnp.where(lane >= h * HDIM, stacked[h * rows : (h + 1) * rows], total)
    return total


def part_of(array, index, size):
    if len(array.shape) == 3:
        count = size // PIECE
        return array[pl.ds(index * count, count)].reshape(size, array.shape[2])
    return array[pl.ds(pl.multiple_of(index * size, size), size), :]


def whole_of(array):
    return array[...].reshape(-1, array.shape[-1])


def attend(queries, keys, values, low, high, scores, powers):
    total = math.prod(keys.shape[:-1])
    width = queries.shape[0]
    chunk = total // PARTS
    pieces = chunk // PIECE

    def first(c, highest):
        rows = pl.ds(pl.multiple_of(c * chunk, chunk), chunk)
        place = lax.broadcasted_iota(jnp.int32, (chunk, width), 0) - (low - c * chunk)
        found = jnp.where(
            place.astype(jnp.uint32) < length, nt(part_of(keys, c, chunk), queries), NEGATIVE
        )
        scores[rows, :] = found
        return jnp.maximum(highest, jnp.max(found, axis=0, keepdims=True))

    length = (high - low).astype(jnp.uint32)
    highest = lax.fori_loop(0, total // chunk, first, jnp.full((1, width), NEGATIVE, F32))

    def second(c, summed):
        rows = pl.ds(pl.multiple_of(c * chunk, chunk), chunk)
        power = jnp.exp(scores[rows, :] - highest)
        powers[pl.ds(c * pieces, pieces)] = power.astype(BF).reshape(pieces, PIECE, width)
        return summed + column_sum(power)

    summed = lax.fori_loop(0, total // chunk, second, jnp.zeros((1, width), F32))
    inverse = 1.0 / summed
    mixed = tn(whole_of(values), powers[0 : total // PIECE].reshape(total, width)) * inverse
    return mixed.T, inverse


def attend_back(queries, grads, product_of, keys, values, inverse, powers, store):
    total = math.prod(keys.shape[:-1])
    width = queries.shape[0]
    chunk = total // PARTS
    pieces = chunk // PIECE
    ones = jnp.ones((8, queries.shape[1]), BF)
    coarse = product_of.astype(BF)
    fine = (product_of - coarse.astype(F32)).astype(BF)
    delta = (nt(ones, coarse) + nt(ones, fine))[0:1]

    def step(c, carry):
        part = pl.ds(c * pieces, pieces)
        weights = powers[part].reshape(chunk, width).astype(F32) * inverse
        weights_low = weights.astype(BF)
        change = (weights * (nt(part_of(values, c, chunk), grads) - delta)).astype(BF)
        powers[part] = change.reshape(pieces, PIECE, width)
        store(c, nn(change, queries), nn(weights_low, grads))
        return carry

    lax.fori_loop(0, total // chunk, step, 0)
    return tn(whole_of(keys), powers[0 : total // PIECE].reshape(total, width)).T


class Cube:
    def __init__(self, me, level, levels):
        self.me, self.level, self.levels = me, level, levels
        self.bits = (lax.rem(me, 2), lax.rem(lax.div(me, 2), 2), lax.div(me, 4))

    def other(self, code):
        place = self.me
        for axis in range(3):
            if code >> axis & 1:
                place = place + (1 << axis) * (1 - 2 * self.bits[axis])
        return place

    def plane(self, step):
        return lax.rem(self.level + step, self.levels)

    def greet(self):
        barrier = pltpu.get_barrier_semaphore()
        for code in range(1, 8):
            pl.semaphore_signal(
                barrier, inc=1, device_id={"seq": self.other(code)}, device_id_type=MESH
            )
        for step in range(1, self.levels):
            pl.semaphore_signal(
                barrier, inc=1, device_id={"batch": self.plane(step)}, device_id_type=MESH
            )

    def await_all(self):
        pl.semaphore_wait(pltpu.get_barrier_semaphore(), 6 + self.levels)

    def send(self, code, source, target, send_sem, recv_sem):
        copy = pltpu.make_async_remote_copy(
            src_ref=source,
            dst_ref=target,
            send_sem=send_sem,
            recv_sem=recv_sem,
            device_id={"seq": self.other(code)},
            device_id_type=MESH,
        )
        copy.start()
        return copy


class Steps:
    def copies(self, step):
        return [
            pltpu.make_async_remote_copy(
                src_ref=source,
                dst_ref=target,
                send_sem=self.send_sem.at[index],
                recv_sem=self.recv_sem.at[index],
                device_id=device,
                device_id_type=MESH,
            )
            for device, source, target, index in self.moves(step)
        ]

    def begin(self, step):
        for copy in self.copies(step):
            copy.start()

    def end(self, step):
        for copy in self.copies(step):
            copy.wait()

    step, last = 0, 0

    def advance(self):
        if self.step:
            self.end(self.step)
            self.take(self.step)
        self.step += 1
        if self.step <= self.last:
            self.begin(self.step)

    def take(self, step):
        pass


class Reduce(Steps):
    last = 8

    def __init__(self, cube, panels, first, count, pair, flat, edge, deep, leave, send_sem, recv_sem, sent, before, finish):
        self.before, self.finish, self.freed = before, finish, set()
        self.cube, self.panels, self.first, self.count = cube, panels, first, count
        self.pair, self.flat, self.edge, self.deep, self.leave = pair, flat, edge, deep, leave
        self.send_sem, self.recv_sem, self.sent = send_sem, recv_sem, sent

    def await_free(self, index):
        if index not in self.freed:
            self.freed.add(index)
            pl.semaphore_wait(self.sent.at[index], 1)

    def begin(self, step):
        for index in {6: (1, 2), 8: (0,)}.get(step, ()):
            self.await_free(index)
        if self.before is not None:
            for index in {1: (0,), 2: (1, 2)}.get(step, ()):
                self.before.await_free(index)
        if step == 4:
            for k in range(1, self.cube.levels):
                for axis in (1, 2):
                    self.leave[k - 1, axis - 1] = self.share(self.cube.plane(k), axis)[...]
        super().begin(step)

    def rows(self, core=0, axis=None, far=0, further=None):
        bits = self.cube.bits
        flip = lambda bit, other: 1 - bit if other else bit
        start, size = flip(bits[0], core) * (D // 2), D // 2
        if axis is not None:
            size = D // 8
            start = start + (axis - 1) * (D // 4) + flip(bits[axis], far) * size
            if further is not None:
                size = D // 16
                start = start + flip(bits[3 - axis], further) * size
        return pl.ds(pl.multiple_of(start, D // 16), size)

    def all(self, rows):
        return self.panels.at[pl.ds(self.first, self.count), rows, :]

    def share(self, plane, axis):
        width = D // self.cube.levels
        lanes = pl.ds(pl.multiple_of(plane * width, width), width)
        return self.panels.at[pl.ds(self.first, self.count), self.rows(axis=axis, further=0), lanes]

    def moves(self, step):
        cube = self.cube
        near = lambda code: {"seq": cube.other(code)}
        if step == 1:
            return [(near(1), self.all(self.rows(core=1)), self.pair, 0)]
        if step == 2:
            return [
                (near(2 * axis), self.all(self.rows(axis=axis, far=1)), self.flat.at[axis - 1], axis)
                for axis in (1, 2)
            ]
        if step == 3:
            return [
                (
                    near(6 - 2 * axis),
                    self.all(self.rows(axis=axis, further=1)),
                    self.edge.at[axis - 1],
                    2 + axis,
                )
                for axis in (1, 2)
            ]
        if step == 4:
            return [
                (
                    {"batch": cube.plane(k)},
                    self.leave.at[k - 1, axis - 1],
                    self.deep.at[k - 1, axis - 1],
                    3 + 2 * k + axis - 1,
                )
                for k in range(1, cube.levels)
                for axis in (1, 2)
            ]
        if step == 5:
            return [
                (
                    {"batch": cube.plane(k)},
                    self.share(cube.level, axis),
                    self.share(cube.level, axis),
                    9 + 2 * k + axis - 1,
                )
                for k in range(1, cube.levels)
                for axis in (1, 2)
            ]
        if step == 6:
            parts = [(6 - 2 * axis, self.all(self.rows(axis=axis, further=0)), 16 + axis) for axis in (1, 2)]
        elif step == 7:
            parts = [(2 * axis, self.all(self.rows(axis=axis)), 18 + axis) for axis in (1, 2)]
        else:
            parts = [(1, self.all(self.rows()), 21)]
        return [(near(code), part, part, index) for code, part, index in parts]

    def add(self, rows, found):
        def one(i, carry):
            there = self.first + i
            total = self.panels[there, rows, :].astype(F32) + found[i].astype(F32)
            self.panels[there, rows, :] = total.astype(BF)
            return carry

        lax.fori_loop(0, self.count, one, 0)

    def take(self, step):
        if step == 1:
            self.add(self.rows(), self.pair)
        elif step == 2:
            for axis in (1, 2):
                self.add(self.rows(axis=axis), self.flat.at[axis - 1])
        elif step == 3:
            for axis in (1, 2):
                self.add(self.rows(axis=axis, further=0), self.edge.at[axis - 1])
        elif step == 4:
            for axis in (1, 2):
                here = self.share(self.cube.level, axis)
                total = here[...].astype(F32)
                for k in range(self.cube.levels - 1):
                    total = total + self.deep[k, axis - 1].astype(F32)
                here[...] = total.astype(BF)
        elif step == 8:
            self.finish()
        for index in {1: (0,), 3: (1, 2)}.get(step, ()):
            pl.semaphore_signal(
                self.sent.at[index],
                inc=1,
                device_id={"seq": self.cube.other(1 << index)},
                device_id_type=MESH,
            )


class Scatter(Steps):
    last = 3

    def __init__(self, cube, block, spare, send_sem, recv_sem, ready, finish):
        self.cube, self.block, self.spare = cube, block, spare
        self.ready, self.finish = ready, finish
        self.send_sem, self.recv_sem = send_sem, recv_sem

    def begin(self, step):
        if self.ready is not None:
            for index in {1: (0,), 2: (1, 2)}.get(step, ()):
                pl.semaphore_wait(self.ready.at[index], 1)
        super().begin(step)

    def at(self, code, part):
        return self.block(2 * self.cube.other(code) + part)

    def moves(self, step):
        near = lambda code: {"seq": self.cube.other(code)}
        if step == 1:
            parts = [(1, 2 * i + 1, part, 2 * i + part) for i in range(4) for part in range(2)]
        elif step == 2:
            parts = [(2, 2, 0, 8), (2, 6, 0, 9), (4, 4, 1, 10), (4, 6, 1, 11)]
        else:
            parts = [(4, 4, 0, 12), (2, 2, 1, 13)]
        return [(near(to), self.at(code, part), self.spare(k), k) for to, code, part, k in parts]

    def take(self, step):
        if step == 3:
            self.finish()
            return
        if step == 1:
            parts = [(2 * i, part, 2 * i + part) for i in range(4) for part in range(2)]
        else:
            parts = [(0, 0, 8), (4, 0, 9), (0, 1, 10), (2, 1, 11)]
        for code, part, k in parts:
            here = self.at(code, part)
            here[...] = (here[...].astype(F32) + self.spare(k)[...].astype(F32)).astype(BF)

    def result(self, part):
        return self.at(0, part)[...].astype(F32) + self.spare(12 + part)[...].astype(F32)


class Small(Steps):
    last = 2

    def __init__(self, cube, array, near, planes, send_sem, recv_sem):
        self.cube, self.array, self.near, self.planes = cube, array, near, planes
        self.send_sem, self.recv_sem = send_sem, recv_sem

    def moves(self, step):
        cube = self.cube
        if step == 1:
            here = self.near.at[cube.me]
            return [({"seq": cube.other(code)}, here, here, code - 1) for code in range(1, 8)]
        here = self.planes.at[cube.level]
        return [({"batch": cube.plane(k)}, here, here, 6 + k) for k in range(1, cube.levels)]

    def begin(self, step):
        if step == 1:
            self.near[self.cube.me] = self.array[...]
        super().begin(step)

    def take(self, step):
        found = self.near if step == 1 else self.planes
        total = found[0]
        for k in range(1, found.shape[0]):
            total = total + found[k]
        if step == 1:
            self.planes[self.cube.level] = total
        else:
            self.array[...] = total


class Gather:
    def __init__(self, cube, own, slot_ref, send_sem, recv_sem):
        self.cube, self.own, self.slot_ref = cube, own, slot_ref
        self.send_sem, self.recv_sem = send_sem, recv_sem
        self.sent = []

    def push(self, step, code, part):
        slot = 2 * self.cube.other(code) + part
        target = self.slot_ref(slot)
        source = self.own.at[part] if code == 0 else target
        self.sent.append(
            self.cube.send(
                step,
                source,
                target,
                self.send_sem.at[len(self.sent)],
                self.recv_sem.at[2 * (code ^ step) + part],
            )
        )

    def take(self, code, part):
        slot = self.slot_ref(2 * self.cube.other(code) + part)
        pltpu.make_async_remote_copy(
            src_ref=slot,
            dst_ref=slot,
            send_sem=self.send_sem.at[0],
            recv_sem=self.recv_sem.at[2 * code + part],
            device_id={"seq": self.cube.other(1)},
            device_id_type=MESH,
        ).wait_recv()

    def arrived(self, code):
        for part in range(2):
            self.take(code, part)

    def open(self):
        for step, part in ((2, 0), (4, 1), (1, 0), (1, 1)):
            self.push(step, 0, part)

    def more(self):
        for step, part in ((2, 1), (4, 0)):
            self.push(step, 0, part)

    def pass_on(self):
        self.take(2, 0)
        self.push(4, 2, 0)
        self.take(4, 1)
        self.push(2, 4, 1)
        self.push(1, 2, 0)
        self.push(1, 4, 1)
        self.take(2, 1)
        self.push(1, 2, 1)
        self.take(4, 0)
        self.push(1, 4, 0)

    def finish(self):
        for part in range(2):
            self.take(6, part)
            self.push(1, 6, part)

    def close(self):
        for copy in self.sent:
            copy.wait_send()


def publish_kernel(grads, dvec, *refs):
    kept, outs, stages = refs[:3], refs[3:-8], refs[-8:-5]
    narrow, broad, load_sem, store_sem, keep_sem = refs[-5:]
    fetches = [pltpu.make_async_copy(kept[i], stages[i], keep_sem.at[i]) for i in range(3)]
    keeps = [pltpu.make_async_copy(stages[i], outs[24 + i], keep_sem.at[i]) for i in range(3)]
    order = list(range(8, 16)) + list(range(4, 8)) + list(range(4))
    loads = [pltpu.make_async_copy(grads.at[i], narrow.at[i], load_sem.at[i]) for i in order]
    ahead = 16
    for load in loads[:ahead] + fetches:
        load.start()
    for i in range(13):
        outs[10 + i][...] = dvec[i, :]
    for i in range(4):
        outs[23][i * D : (i + 1) * D] = dvec[13 + i, :]
    stores = []
    for turn, (load, i) in enumerate(zip(loads, order)):
        load.wait()
        if turn + ahead < len(loads):
            loads[turn + ahead].start()
        broad[i] = narrow[i].astype(F32)
        if i < 8:
            target = outs[i]
        elif i % 2 == 0:
            target = outs[8].at[:, pl.ds((i - 8) // 2 * D, D)]
        else:
            target = outs[9].at[pl.ds((i - 8) // 2 * D, D), :]
        store = pltpu.make_async_copy(broad.at[i], target, store_sem.at[i])
        store.start()
        stores.append(store)
    for fetch, keep in zip(fetches, keeps):
        fetch.wait()
        keep.start()
    for store in stores + keeps:
        store.wait()


def publish(grads, dvec, kept):
    vmem = pl.BlockSpec(memory_space=pltpu.VMEM)
    hbm = pl.BlockSpec(memory_space=pl.ANY)
    shapes = [(D, D)] * 8 + [(D, 4 * D), (4 * D, D)] + [(D,)] * 13 + [(4 * D,)]
    return pl.pallas_call(
        publish_kernel,
        out_shape=tuple(
            [jax.ShapeDtypeStruct(shape, F32) for shape in shapes]
            + [jax.ShapeDtypeStruct(array.shape, array.dtype) for array in kept]
        ),
        in_specs=[hbm, vmem] + [hbm] * 3,
        out_specs=tuple([hbm] * 10 + [vmem] * 14 + [hbm] * 3),
        scratch_shapes=[pltpu.VMEM(array.shape, array.dtype) for array in kept]
        + [
            pltpu.VMEM((16, D, D), BF),
            pltpu.VMEM((16, D, D), F32),
            pltpu.SemaphoreType.DMA((16,)),
            pltpu.SemaphoreType.DMA((16,)),
            pltpu.SemaphoreType.DMA((3,)),
        ],
        compiler_params=pltpu.CompilerParams(vmem_limit_bytes=64 << 20),
    )(grads, dvec, *kept)


def layer_kernel(
    sizes,
    tlen,
    slen,
    tord,
    sord,
    own_far,
    cot_far,
    own_memory,
    vectors_far,
    w_small,
    w_in,
    w_out,
    result,
    dinputs,
    dmemory,
    dvec,
    grads,
    own,
    cot,
    vectors,
    vec,
    nrm,
    memory,
    stream,
    weight,
    kv,
    queries,
    ckeys,
    cvalues,
    scores,
    powers,
    cpowers,
    inverses,
    cinverses,
    mixed,
    heard,
    unit,
    low,
    tinv,
    sinv,
    pairs,
    flats,
    edges,
    deeps,
    leaves,
    nears,
    planes,
    sem,
    send_sem,
    recv_sem,
    group_send,
    group_recv,
    group_sent,
    scatter_send,
    scatter_recv,
    small_send,
    small_recv,
    ready,
):
    rows, blocks, half, sblocks, shalf, ndoc, window = (
        sizes["rows"],
        sizes["blocks"],
        sizes["half"],
        sizes["sblocks"],
        sizes["shalf"],
        sizes["ndoc"],
        sizes["window"],
    )
    around = -(-window // half)
    pad = around * half - window
    sources = sblocks * shalf
    later = dinputs
    me = lax.axis_index("seq")
    scale = float(HDIM) ** -0.5
    thirds = half // PIECE
    cube = Cube(me, lax.axis_index("batch"), sizes["levels"])
    cube.greet()

    def raw(slot):
        return powers.at[lax.rem(slot, 4), pl.ds(lax.div(slot, 4) * thirds, thirds), :, 0:D]

    def raw_memory(slot):
        return memory.at[slot]

    gather_rows = Gather(cube, own_far, raw, send_sem.at[0], recv_sem.at[0])
    gather_sources = Gather(cube, own_memory, raw_memory, send_sem.at[1], recv_sem.at[1])
    copies = []
    for index, (source, target) in enumerate(
        [(own_far, own)]
        + list(zip(vectors_far, vectors))
        + [(w_small[i], weight.at[i]) for i in range(8)]
        + [(w_in.at[:, pl.ds(D * i, D)], weight.at[8 + 2 * i]) for i in range(4)]
        + [(w_out.at[pl.ds(D * i, D), :], weight.at[9 + 2 * i]) for i in range(4)]
        + [(cot_far, cot)]
    ):
        copy = pltpu.make_async_copy(source, target, sem.at[index])
        copy.start()
        copies.append(copy)
    cube.await_all()
    gather_rows.open()
    def deliver(turn, first, count):
        def go():
            pltpu.make_async_copy(
                weight.at[pl.ds(first, count)], grads.at[pl.ds(first, count)], sem.at[turn]
            ).start()

        return go

    groups = []
    for turn, (first, count) in enumerate(GROUPS):
        side = turn % 2
        some = pl.ds(0, count)
        groups.append(
            Reduce(
                cube, weight, first, count, pairs.at[side, some], flats.at[side, :, some],
                edges.at[side, :, some], deeps.at[side, :, :, some], leaves.at[side, :, :, some],
                group_send.at[turn], group_recv.at[turn], group_sent.at[turn],
                groups[turn - 2] if turn > 1 else None, deliver(turn, first, count),
            )
        )

    def spare_block(k):
        return powers.at[k % 4, pl.ds(k // 4 * thirds, thirds), :, 0:D]

    def end_rows():
        for part in range(2):
            own_unit, own_spread = centred(own[part].reshape(half, D).astype(F32))
            dnormed = rows_back.result(part).reshape(half, D)
            here = pl.ds(part * half, half)
            dinputs[here, :] = later[here, :] + norm_back(dnormed, own_unit, own_spread, vector(0))
            dvec[0:1, :] += column_sum(dnormed * own_unit)
            dvec[1:2, :] += column_sum(dnormed)

    def end_memory():
        for part in range(2):
            dmemory[part * shalf : (part + 1) * shalf, :] = memory_back.result(part)

    rows_back = Scatter(
        cube, lambda slot: nrm.at[slot], spare_block, scatter_send.at[0], scatter_recv.at[0],
        ready, end_rows,
    )
    memory_back = Scatter(
        cube,
        lambda slot: cvalues.at[pl.ds(pl.multiple_of(slot * shalf, shalf), shalf), :],
        lambda k: memory.at[k],
        scatter_send.at[1],
        scatter_recv.at[1],
        None,
        end_memory,
    )
    smalls = [
        Small(
            cube, dvec.at[pl.ds(start, 8 * size), :],
            nears.at[:, pl.ds(start, 8 * size), :], planes.at[:, pl.ds(start, 8 * size), :],
            small_send.at[turn], small_recv.at[turn],
        )
        for turn, (start, size) in enumerate(((0, 1), (8, 2)))
    ]
    exchanges = dict(
        A=groups[0], B=groups[1], C=groups[2], E=groups[3], R=rows_back, M=memory_back,
        S=smalls[0], V=smalls[1],
    )
    counts = dict(A=9, B=9, C=9, E=9, R=4, M=4, S=3, V=3)

    def pump(point):
        for name in SCHEDULE.get(point, ""):
            counts[name] -= 1
            exchanges[name].advance()

    dvec[...] = jnp.zeros((VECTORS, D), F32)
    for order, inverse_of, count in ((tord, tinv, blocks), (sord, sinv, sblocks)):
        for t in range(count):
            found = jnp.int32(0)
            for s in range(count):
                found = jnp.where(order[0, s] == t, s, found)
            inverse_of[t] = found
    tends, sends = [], []
    tend, send = jnp.int32(0), jnp.int32(0)
    for d in range(ndoc):
        tend, send = tend + tlen[0, d], send + slen[0, d]
        tends.append(tend)
        sends.append(send)
    base = [tord[0, 2 * me + b] for b in range(2)]

    def vector(index):
        return vec[index : index + 1, :]

    for copy in copies:
        copy.wait()
    row = 0
    for vector_ref in vectors:
        for start in range(0, vector_ref.shape[0], D):
            vec[row : row + 1, :] = vector_ref[start : start + D].astype(F32).reshape(1, D)
            row += 1

    gather_rows.more()
    states = own[...].reshape(rows, D)
    own_normed = (centred(states.astype(F32))[0] * vector(0) + vector(1)).astype(BF)
    queries[...] = ((nn(own_normed, weight[0]) + vector(2)) * scale).astype(BF)

    def project_block(s, block):
        found, _ = centred(block.astype(F32))
        normed = (found * vector(0) + vector(1)).astype(BF)
        nrm[s] = normed.reshape(thirds, PIECE, D)
        keys = nn(normed, weight[1]).astype(BF)
        values = (nn(normed, weight[2]) + vector(3)).astype(BF)
        for quad in range(2):
            kv[0, quad, s] = keys[:, quad * 256 : (quad + 1) * 256]
            kv[1, quad, s] = values[:, quad * 256 : (quad + 1) * 256]

    def project(code):
        def one(part, carry):
            s = 2 * cube.other(code) + part
            project_block(s, raw(s)[...].reshape(half, D))
            return carry

        lax.fori_loop(0, 2, one, 0)

    for part in range(2):
        project_block(2 * me + part, own[part].reshape(half, D))
    def limits(b):
        index = lax.broadcasted_iota(jnp.int32, (1, 4 * half), 1)
        row = index
        for h in range(1, 4):
            row = jnp.where(index >= h * half, index - h * half, row)
        position = base[b] * half + row
        start = jnp.zeros_like(position)
        for end in tends:
            start = jnp.where(position >= end, end, start)
        shift = (base[b] + 1) * half - window
        return start - shift, position - shift + 1

    bounds = [limits(b) for b in range(2)]
    index = lax.broadcasted_iota(jnp.int32, (1, 2 * rows), 1)
    row = jnp.where(index >= rows, index - rows, index)
    position = jnp.where(row >= half, base[1] * half + row - half, base[0] * half + row)
    cross_begin = jnp.zeros_like(position)
    cross_stop = jnp.full_like(position, sources)
    for end, send in zip(tends, sends):
        cross_begin = jnp.where(position >= end, send, cross_begin)
    for end, send in reversed(list(zip(tends, sends))):
        cross_stop = jnp.where(position < end, send, cross_stop)

    gather_rows.arrived(1)
    project(1)
    gather_rows.pass_on()
    gather_sources.open()
    gather_sources.more()
    project(2)
    project(4)
    gather_rows.arrived(3)
    project(3)
    gather_rows.arrived(5)
    project(5)
    gather_rows.finish()
    project(6)
    gather_rows.arrived(7)
    project(7)
    gather_rows.close()
    gather_sources.pass_on()

    kwin, vwin = [
        cpowers.at[kind, pl.ds(0, window // PIECE), :, pl.ds(D, 4 * HDIM)] for kind in range(2)
    ]

    def fill(b, quad):
        skip = pad // PIECE
        for j in range(around):
            slot = tinv[jnp.maximum(base[b] - (around - 1) + j, 0)]
            for kind, target in ((0, kwin), (1, vwin)):
                block = kv[kind, quad, slot].reshape(thirds, PIECE, 4 * HDIM)
                if j == 0:
                    target[0 : thirds - skip] = block[skip:]
                else:
                    target[j * thirds - skip : (j + 1) * thirds - skip] = block

    for b in range(2):
        begin, stop = bounds[b]

        def forward(quad, carry, b=b, begin=begin, stop=stop):
            fill(b, quad)
            lanes = pl.ds(pl.multiple_of(quad * 256, 256), 256)
            block = queries[b * half : (b + 1) * half, lanes].astype(F32)
            out, inverse = attend(
                spread_heads(block, 4).astype(BF),
                kwin,
                vwin,
                begin,
                stop,
                scores.at[pl.ds(0, window), :],
                powers.at[b * 2 + quad],
            )
            inverses[b * 2 + quad] = jnp.broadcast_to(inverse, (8, 4 * half))
            mixed[b * half : (b + 1) * half, lanes] = join_heads(out, 4)
            return carry

        lax.fori_loop(0, 2, forward, 0)
        if b == 0:
            gather_sources.finish()

    middle = own[...].reshape(rows, D).astype(F32) + nn(mixed[...].astype(BF), weight[3]) + vector(4)
    found, spread = centred(middle)
    later[...] = middle
    unit[0] = found
    low[0] = (found * vector(5) + vector(6)).astype(BF)
    cross_spread = spread
    low[1] = ((nn(low[0], weight[4]) + vector(7)) * scale).astype(BF)

    for code in (1, 3, 5, 7):
        gather_sources.arrived(code)
    for part in range(2):
        memory[2 * me + part] = own_memory[part]
    gather_sources.close()

    def place(t, carry):
        stream[t] = memory[sinv[t]]
        return carry

    lax.fori_loop(0, sblocks, place, 0)
    step = sources // 2
    some = sblocks // 2

    def sources_of(c, carry):
        part = pl.ds(pl.multiple_of(c * step, step), step)
        block = stream[pl.ds(c * some, some)].reshape(step, D)
        ckeys[part, :] = nn(block, weight[5]).astype(BF)
        cvalues[part, :] = (nn(block, weight[6]) + vector(8)).astype(BF)
        return carry

    lax.fori_loop(0, sources // step, sources_of, 0)
    def cross_forward(pair, carry):
        lanes = pl.ds(pl.multiple_of(pair * 128, 128), 128)
        out, inverse = attend(
            spread_heads(low[1, :, lanes].astype(F32), 2).astype(BF),
            ckeys.at[:, lanes],
            cvalues.at[:, lanes],
            cross_begin,
            cross_stop,
            scores,
            cpowers.at[pair],
        )
        cinverses[pair] = jnp.broadcast_to(inverse, (8, 2 * rows))
        heard[:, lanes] = join_heads(out, 2)
        return carry

    lax.fori_loop(0, 4, cross_forward, 0)
    after_cross = later[...] + nn(heard[...].astype(BF), weight[7]) + vector(9)
    found, spread = centred(after_cross)
    unit[1] = found
    final_spread = spread
    low[2] = (found * vector(10) + vector(11)).astype(BF)
    later[...] = after_cross + vector(12)

    cotangent = cot[...]
    unit[2] = jnp.zeros((rows, D), F32)

    def feed(c, carry):
        fed = low[2]
        first, second = weight[8 + 2 * c], weight[9 + 2 * c]
        before = nn(fed, first) + vec[pl.ds(13 + c, 1), :]
        cumulative = 0.5 * (1.0 + lax.erf(before * (2.0**-0.5)))
        after = (before * cumulative).astype(BF)
        slope = cumulative + before * jnp.exp(-0.5 * before * before) * ((2.0 * math.pi) ** -0.5)
        later[...] += nn(after, second)
        change = nt(cotangent, second) * slope
        change_low = change.astype(BF)
        dvec[pl.ds(13 + c, 1), :] = column_sum(change_low.astype(F32))
        unit[2] += nt(change_low, first)
        weight[8 + 2 * c] = tn(fed, change_low).astype(BF)
        weight[9 + 2 * c] = tn(after, cotangent).astype(BF)

        @pl.when(c == 1)
        def _():
            pump("half")

        return carry

    lax.fori_loop(0, 4, feed, 0)
    pump("feed")
    result[...] = later[...].astype(BF)
    cot_f = cotangent.astype(F32)
    dvec[12:13, :] = column_sum(cot_f)
    dfed = unit[2]
    dvec[10:11, :] = column_sum(dfed * unit[1])
    dvec[11:12, :] = column_sum(dfed)
    dlater = cot_f + norm_back(dfed, unit[1], final_spread, vector(10))
    later[...] = dlater
    branch = dlater.astype(BF)
    dvec[9:10, :] = column_sum(branch.astype(F32))
    dheard = nt(branch, weight[7]).astype(BF)
    weight[7] = tn(heard[...].astype(BF), branch).astype(BF)
    low[2] = dheard
    heard[...] = heard[...] * dheard.astype(F32)
    pump("heard")

    def cross_backward(pair, carry):
        lanes = pl.ds(pl.multiple_of(pair * 128, 128), 128)

        def store(c, dkeys, dvalues):
            part = pl.ds(pl.multiple_of(c * dkeys.shape[0], dkeys.shape[0]), dkeys.shape[0])
            scores[part, 0:128] = dkeys
            cvalues[part, lanes] = dvalues.astype(BF)

        out = attend_back(
            spread_heads(low[1, :, lanes].astype(F32), 2).astype(BF),
            spread_heads(low[2, :, lanes].astype(F32), 2).astype(BF),
            spread_heads(heard[:, lanes], 2),
            ckeys.at[:, lanes],
            cvalues.at[:, lanes],
            cinverses[pair, 0:1, :],
            cpowers.at[pair],
            store,
        )
        ckeys[:, lanes] = scores[:, 0:128].astype(BF)
        unit[1, :, lanes] = join_heads(out, 2)

        for index in range(4):

            @pl.when(pair == index)
            def _(index=index):
                pump("pair" + str(index))

        return carry

    lax.fori_loop(0, 4, cross_backward, 0)

    dvec[8:9, :] = column_sum(cvalues[...].astype(F32))
    block = stream[...].reshape(sources, D)
    fresh = [tn(block, ckeys[...]).astype(BF), tn(block, cvalues[...]).astype(BF)]

    pump("sums")

    def sources_back(c, carry):
        part = pl.ds(pl.multiple_of(c * step, step), step)
        back = nt(ckeys[part, :], weight[5]) + nt(cvalues[part, :], weight[6])
        stream[pl.ds(c * some, some)] = back.astype(BF).reshape(some, shalf, D)
        return carry

    lax.fori_loop(0, sources // step, sources_back, 0)
    weight[5] = fresh[0]
    weight[6] = fresh[1]

    def place_back(s, carry):
        there = pl.ds(pl.multiple_of(s * shalf, shalf), shalf)
        cvalues[there, :] = stream[sord[0, s]]
        return carry

    lax.fori_loop(0, sblocks, place_back, 0)
    pump("sources")
    ckeys[0:D, :] = weight[1]
    ckeys[D : 2 * D, :] = weight[2]

    dcq = unit[1].astype(BF)
    dvec[7:8, :] = column_sum(dcq.astype(F32)) * scale
    dcrossed = nt(dcq, weight[4]) * scale
    weight[4] = (tn(low[0], dcq) * scale).astype(BF)
    dvec[5:6, :] = column_sum(dcrossed * unit[0])
    dvec[6:7, :] = column_sum(dcrossed)
    dmid = later[...] + norm_back(dcrossed, unit[0], cross_spread, vector(5))
    later[...] = dmid
    branch = dmid.astype(BF)
    dvec[4:5, :] = column_sum(branch.astype(F32))
    dmixed = nt(branch, weight[3]).astype(BF)
    weight[3] = tn(mixed[...].astype(BF), branch).astype(BF)
    low[2] = dmixed
    mixed[...] = mixed[...] * dmixed.astype(F32)
    pump("middle")

    for b in range(2):
        for kind in range(2):
            if pad:
                cpowers[2 * kind + b, 0 : pad // PIECE, :, 0:D] = jnp.zeros((pad // PIECE, PIECE, D), BF)

        def backward(quad, carry, b=b):
            fill(b, quad)
            lanes = pl.ds(pl.multiple_of(quad * 256, 256), 256)

            def store(c, dkeys, dvalues):
                pieces = dkeys.shape[0] // PIECE
                part = pl.ds(c * pieces + pad // PIECE, pieces)
                cpowers[b, part, :, lanes] = dkeys.astype(BF).reshape(pieces, PIECE, 256)
                cpowers[2 + b, part, :, lanes] = dvalues.astype(BF).reshape(pieces, PIECE, 256)

            out = attend_back(
                spread_heads(queries[b * half : (b + 1) * half, lanes].astype(F32), 4).astype(BF),
                spread_heads(low[2, b * half : (b + 1) * half, lanes].astype(F32), 4).astype(BF),
                spread_heads(mixed[b * half : (b + 1) * half, lanes], 4),
                kwin,
                vwin,
                inverses[b * 2 + quad, 0:1, :],
                powers.at[b * 2 + quad],
                store,
            )
            unit[1, b * half : (b + 1) * half, lanes] = join_heads(out, 4)

            for index in range(2):

                @pl.when(quad == index)
                def _(index=index):
                    pump("self" + str(2 * b + index))

            return carry

        lax.fori_loop(0, 2, backward, 0)

        ratio = half // shalf
        for j in range(around):
            slot = tinv[jnp.maximum(base[b] - (around - 1) + j, 0)]
            stream[j * ratio : (j + 1) * ratio] = nrm[slot].reshape(ratio, shalf, D)
        normed = stream[0 : around * ratio].reshape(around * half, D)
        for kind in range(2):
            change = cpowers[2 * kind + b, 0 : around * thirds, :, 0:D].reshape(around * half, D)
            if kind == 1:
                dvec[3:4, :] += column_sum(change.astype(F32))
            total = tn(normed, change)
            there = slice(kind * D, (kind + 1) * D)
            if b == 0:
                scores[there, 0:D] = total
            else:
                weight[1 + kind] = (scores[there, 0:D] + total).astype(BF)
        if b == 0:
            pump("window")
    for index in range(3):
        pl.semaphore_signal(
            ready.at[index],
            inc=1,
            device_id={"seq": cube.other(1 << index)},
            device_id_type=MESH,
        )

    dq = unit[1].astype(BF)
    dvec[2:3, :] = column_sum(dq.astype(F32)) * scale
    heard[...] = nt(dq, weight[0]) * scale
    own_normed = nrm[pl.ds(2 * me, 2)].reshape(rows, D)
    weight[0] = (tn(own_normed, dq) * scale).astype(BF)

    pump("weights")

    for b in range(2):

        def through(c, carry, b=b):
            part = pl.ds(c * around, around)
            dkeys = cpowers[b, part, :, 0:D].reshape(around * PIECE, D)
            dvalues = cpowers[2 + b, part, :, 0:D].reshape(around * PIECE, D)
            total = nt(dkeys, ckeys[0:D, :]) + nt(dvalues, ckeys[D : 2 * D, :])
            cpowers[b, part, :, 0:D] = total.astype(BF).reshape(around, PIECE, D)
            return carry

        lax.fori_loop(0, thirds, through, 0)
        pump("through" + str(b))

    def assemble(code):
        def one(part, carry):
            s = 2 * cube.other(code) + part
            for third in range(thirds):
                total = jnp.zeros((PIECE, D), F32)
                for b in range(2):
                    back = base[b] - tord[0, s]
                    inside = (back >= 0) & (back < around)
                    first = jnp.clip(around - 1 - back, 0, around - 1) * thirds
                    found = cpowers[b, first + third][:, 0:D]
                    total = total + jnp.where(inside, found.astype(F32), 0.0)
                if code == 0:
                    start = pl.multiple_of(part * half + third * PIECE, PIECE)
                    total = total + heard[pl.ds(start, PIECE), :]
                nrm[s, third] = total.astype(BF)
            return carry

        lax.fori_loop(0, 2, one, 0)

    for code in (1, 3, 5, 7):
        assemble(code)
    pump("theirs")
    for code in (6, 2, 4, 0):
        assemble(code)
    pump("end")
    assert not any(counts.values()), counts
    for turn, (first, count) in enumerate(GROUPS):
        pltpu.make_async_copy(
            weight.at[pl.ds(first, count)], grads.at[pl.ds(first, count)], sem.at[turn]
        ).wait()


def layer_call(sizes, small_ints, own, cot, own_memory, vectors, w_small, w_in, w_out):
    rows, blocks, half, sblocks, shalf, window = (
        sizes["rows"],
        sizes["blocks"],
        sizes["half"],
        sizes["sblocks"],
        sizes["shalf"],
        sizes["window"],
    )
    sources = sblocks * shalf
    levels = sizes["levels"]
    most = max(count for _, count in GROUPS)
    vmem = pl.BlockSpec(memory_space=pltpu.VMEM)
    smem = pl.BlockSpec(memory_space=pltpu.SMEM)
    hbm = pl.BlockSpec(memory_space=pl.ANY)

    count = len(vectors)

    def body(*refs):
        head, rest = refs[:7], refs[7:]
        vector_refs, rest = rest[:count], rest[count:]
        scratch = rest[17:]
        layer_kernel(
            sizes, *head, vector_refs, rest[:8], *rest[8:15],
            *rest[15:17], scratch[:count], *scratch[count:],
        )

    return pl.pallas_call(
        body,
        out_shape=(
            jax.ShapeDtypeStruct((rows, D), BF),
            jax.ShapeDtypeStruct((rows, D), F32),
            jax.ShapeDtypeStruct((2 * shalf, D), F32),
            jax.ShapeDtypeStruct((VECTORS, D), F32),
            jax.ShapeDtypeStruct((16, D, D), BF),
        ),
        in_specs=[smem] * 4 + [hbm] * 2 + [vmem] + [hbm] * (count + 10),
        out_specs=(vmem, vmem, vmem, vmem, hbm),
        scratch_shapes=[pltpu.VMEM(own.shape, BF), pltpu.VMEM(cot.shape, BF)]
        + [pltpu.VMEM(vector.shape, BF) for vector in vectors]
        + [
            pltpu.VMEM((VECTORS, D), F32),
            pltpu.VMEM((blocks, half // PIECE, PIECE, D), BF),
            pltpu.VMEM((sblocks, shalf, D), BF),
            pltpu.VMEM((sblocks, shalf, D), BF),
            pltpu.VMEM((16, D, D), BF),
            pltpu.VMEM((2, 2, blocks, half, 256), BF),
            pltpu.VMEM((rows, D), BF),
            pltpu.VMEM((sources, D), BF),
            pltpu.VMEM((sources, D), BF),
            pltpu.VMEM((sources, 2 * rows), F32),
            pltpu.VMEM((4, window // PIECE, PIECE, 4 * half), BF),
            pltpu.VMEM((4, sources // PIECE, PIECE, 2 * rows), BF),
            pltpu.VMEM((4, 8, 4 * half), F32),
            pltpu.VMEM((4, 8, 2 * rows), F32),
            pltpu.VMEM((rows, D), F32),
            pltpu.VMEM((rows, D), F32),
            pltpu.VMEM((3, rows, D), F32),
            pltpu.VMEM((3, rows, D), BF),
            pltpu.SMEM((blocks,), jnp.int32),
            pltpu.SMEM((sblocks,), jnp.int32),
            pltpu.VMEM((2, most, D // 2, D), BF),
            pltpu.VMEM((2, 2, most, D // 8, D), BF),
            pltpu.VMEM((2, 2, most, D // 16, D), BF),
            pltpu.VMEM((2, levels - 1, 2, most, D // 16, D // levels), BF),
            pltpu.VMEM((2, levels - 1, 2, most, D // 16, D // levels), BF),
            pltpu.VMEM((8, VECTORS, D), F32),
            pltpu.VMEM((levels, VECTORS, D), F32),
            pltpu.SemaphoreType.DMA((32,)),
            pltpu.SemaphoreType.DMA((2, 16)),
            pltpu.SemaphoreType.DMA((2, 16)),
            pltpu.SemaphoreType.DMA((4, 22)),
            pltpu.SemaphoreType.DMA((4, 22)),
            pltpu.SemaphoreType.REGULAR((4, 3)),
            pltpu.SemaphoreType.DMA((2, 14)),
            pltpu.SemaphoreType.DMA((2, 14)),
            pltpu.SemaphoreType.DMA((2, 10)),
            pltpu.SemaphoreType.DMA((2, 10)),
            pltpu.SemaphoreType.REGULAR((3,)),
        ],
        compiler_params=pltpu.CompilerParams(
            vmem_limit_bytes=64 << 20, collective_id=0, has_side_effects=True
        ),
    )(*small_ints, own, cot, own_memory, *vectors, *w_small, w_in, w_out)


def fused_on_device(
    inputs, memory, target_lengths, source_lengths, target_order, source_order,
    self_gain, self_shift, self_query, query_bias, self_key, self_value, value_bias,
    self_output, output_bias, cross_gain, cross_shift, cross_query, cquery_bias, cross_key,
    cross_value, cvalue_bias, cross_output, coutput_bias, final_gain, final_shift,
    inner_weight, inner_bias, outer_weight, outer_bias, cotangent,
):
    rows = inputs.shape[1]
    blocks = target_order.shape[1]
    sblocks = source_order.shape[1]
    ranks = lax.axis_size("seq")
    half = ranks * rows // blocks
    shalf = ranks * memory.shape[1] // sblocks
    ndoc = target_lengths.shape[1]
    reach = max(LONGEST, blocks * half - LONGEST - SHORTEST * (ndoc - 1))
    window = -(-(reach - 1 + half) // CHUNK) * CHUNK
    sizes = dict(
        rows=rows, blocks=blocks, half=half, sblocks=sblocks, shalf=shalf, ndoc=ndoc, window=window,
        levels=lax.axis_size("batch"),
    )
    result, dinputs, dmemory, dvec, grads = layer_call(
        sizes, (target_lengths, source_lengths, target_order, source_order),
        inputs.reshape(2, half // PIECE, PIECE, D), cotangent[0], memory.reshape(2, shalf, D),
        (
            self_gain, self_shift, query_bias, value_bias, output_bias, cross_gain, cross_shift,
            cquery_bias, cvalue_bias, coutput_bias, final_gain, final_shift, outer_bias, inner_bias,
        ),
        (self_query, self_key, self_value, self_output, cross_query, cross_key, cross_value, cross_output),
        inner_weight, outer_weight,
    )
    made = publish(grads, dvec, (result, dinputs, dmemory))
    result, dinputs, dmemory = made[24:]
    squares, wide, tall, rows_of, units = made[:8], made[8], made[9], made[10:23], made[23]
    return (
        result[None], dinputs[None], dmemory[None],
        rows_of[0], rows_of[1], squares[0], rows_of[2], squares[1], squares[2], rows_of[3],
        squares[3], rows_of[4], rows_of[5], rows_of[6], squares[4], rows_of[7], squares[5],
        squares[6], rows_of[8], squares[7], rows_of[9], rows_of[10], rows_of[11],
        wide, units, tall, rows_of[12],
    )


def solution(mesh):
    in_specs = (
        P("batch", "seq", None),
        P("batch", "seq", None),
        P("batch", None),
        P("batch", None),
        P("batch", None),
        P("batch", None),
        P(),
        P(),
        P(),
        P(),
        P(),
        P(),
        P(),
        P(),
        P(),
        P(),
        P(),
        P(),
        P(),
        P(),
        P(),
        P(),
        P(),
        P(),
        P(),
        P(),
        P(),
        P(),
        P(),
        P(),
        P("batch", "seq", None),
    )
    out_specs = (
        P("batch", "seq", None),
        P("batch", "seq", None),
        P("batch", "seq", None),
        P(),
        P(),
        P(),
        P(),
        P(),
        P(),
        P(),
        P(),
        P(),
        P(),
        P(),
        P(),
        P(),
        P(),
        P(),
        P(),
        P(),
        P(),
        P(),
        P(),
        P(),
        P(),
        P(),
        P(),
    )
    return jax.shard_map(
        fused_on_device if (mesh.shape["seq"], mesh.shape["batch"]) == (8, 4) else on_device,
        mesh=mesh, in_specs=in_specs, out_specs=out_specs, check_vma=False,
    )
```
